32 devices in a mesh: var: 16 (over z, y, core), head: 2 (over x).
Axes of the slice: x: 2, y: 2, z: 4, core: 2. Of those that a mesh axis runs over, the one named last changes fastest.
Arguments:
- queries: bfloat16 [6144, 1024], P('var', 'head'), may hold values from -6 to 6
- keys: bfloat16 [6144, 1024], P('var', 'head'), may hold values from -6 to 6
- values: bfloat16 [6144, 1024], P('var', 'head'), may hold values from -6 to 6
- out_grad: bfloat16 [6144, 1024], P('var', 'head'), may hold values from -6 to 6
- log_sum_exp: float32 [16, 6144], P('head', 'var'), may hold values from 4.5 to 7.5
- key_blocks: int32 [48, 8], replicated, may hold values from 0 to 47, as said below
- w_qkv: bfloat16 [3, 1024, 1024], P(None, None, 'head'), may hold values from -0.1875 to 0.1875
Outputs:
- query_gradient: bfloat16 [6144, 1024], P('var', 'head')
- key_grad: bfloat16 [6144, 1024], P('var', 'head')
- value_grad: bfloat16 [6144, 1024], P('var', 'head')
- input_grad: bfloat16 [6144, 1024], P(('var', 'head'))
The draws below stay inside these ranges and needn't reach their ends.
Inputs may be any that keep to these rules, and one draw needn't show every extreme that they name: `key_blocks`: row b lists 8 different key blocks: b itself first, and the others within 8 blocks of b.
All inputs are finite; a program needn't handle non-finite values.
Results may differ from the reference program's by a relative error of at most 0.0057.
Values may be sent and summed in bfloat16 or wider, within the bound.
No kernel may reach another device: no remote copies, remote signals or barrier semaphores. Data moves between devices by JAX's collectives and lax.ppermute only.
A program may use at most 128 MiB of HBM per device.

```python
import jax
import jax.numpy as jnp
from jax import lax

HEADS = 16
HEAD_DIM = 64
D = 1024
PATCHES = 16
BLOCK = 128
SLOTS = 8
SPAN = 8
NBLOCKS = 48
TOKENS = 6144


def draw_key_blocks(key, part):
    key = jax.random.fold_in(key, 11)
    pop_key, pick_key = jax.random.split(key)
    window_width = 2 * SPAN + 1
    popular = jax.random.randint(pop_key, (NBLOCKS,), 1, 9)
    query_row = jnp.arange(NBLOCKS, dtype=jnp.int32)[:, None]
    offset = jnp.arange(window_width, dtype=jnp.int32)[None, :] - SPAN
    target = query_row + offset
    inside = (target >= 0) & (target < NBLOCKS) & (offset != 0)
    weighting = popular[jnp.clip(target, 0, NBLOCKS - 1)]
    draw_score = jax.random.randint(pick_key, (NBLOCKS, window_width), 0, 4096) * weighting
    draw_score = draw_score * 32 + jnp.arange(window_width, dtype=jnp.int32)[None, :]
    draw_score = jnp.where(inside, draw_score, -1)
    top_values, picked = lax.top_k(draw_score, SLOTS - 1)
    chosen = query_row + picked.astype(jnp.int32) - SPAN
    return jnp.concatenate([query_row, chosen], axis=1).astype(jnp.int32)


def shard_levels(rng, dims, shards, least, top_value):
    factor_of, own = 1.0, jax.random.fold_in(rng, 6)
    for dim, parts in shards:
        draws = jnp.exp(jax.random.uniform(jax.random.fold_in(own, dim), (parts,), jnp.float32, least / len(shards), top_value / len(shards)))
        factor_of = factor_of * jnp.repeat(draws, dims[dim] // parts).reshape([-1 if axis == dim else 1 for axis in range(len(dims))])
    return factor_of


def scatter_about(own_key, extent, spread, most, shards=(), kind=jnp.bfloat16):
    loudness = shard_levels(own_key, extent, shards, -0.22, 0.18) if shards else 1.0
    drawn = jax.random.normal(own_key, extent, jnp.float32) * spread * loudness
    return jnp.minimum(jnp.maximum(drawn, -most), most).astype(kind)


def setup_inputs(seed: int = 0) -> dict:
    key_of = jax.random.split(jax.random.key(seed), 8)
    return {
        "queries": scatter_about(key_of[0], (TOKENS, D), 1.0, 6.0, ((0, 16), (1, 2))),
        "keys": scatter_about(key_of[1], (TOKENS, D), 1.0, 6.0, ((0, 16), (1, 2))),
        "values": scatter_about(key_of[2], (TOKENS, D), 1.0, 6.0, ((0, 16), (1, 2))),
        "out_grad": scatter_about(key_of[3], (TOKENS, D), 1.0, 6.0, ((0, 16), (1, 2))),
        "log_sum_exp": jnp.clip(4.5 + 3.0 * jax.random.uniform(key_of[4], (HEADS, TOKENS), jnp.float32) ** shard_levels(key_of[4], (HEADS, TOKENS), ((0, 2), (1, 16)), -0.2, 0.2), 4.5, 7.5),
        "key_blocks": draw_key_blocks(jax.random.fold_in(key_of[7], 71), 0),
        "w_qkv": scatter_about(key_of[6], (3, D, D), D ** -0.5, 0.1875, ((2, 2),)),
    }


def round_keep(values_in):
    return lax.optimization_barrier(values_in.astype(jnp.bfloat16)).astype(jnp.float32)


def reference(queries, keys, values, out_grad, log_sum_exp, key_blocks, w_qkv):
    logit_scale = HEAD_DIM ** -0.5
    shape_four = (NBLOCKS, BLOCK, HEADS, HEAD_DIM)
    query_all = queries.reshape(shape_four)
    key_all = keys.reshape(shape_four)
    value_all = values.reshape(shape_four)
    grad_all = out_grad.reshape(shape_four)
    lse_all = log_sum_exp.reshape(HEADS, NBLOCKS, BLOCK)
    patch_index = jnp.arange(BLOCK, dtype=jnp.int32) % PATCHES
    usable = jnp.tile(patch_index, SLOTS)[None, :] <= patch_index[:, None]

    def block_step(totals, block_index):
        key_sums, value_sums = totals
        chosen = key_blocks[block_index]
        query_row_block = query_all[block_index].astype(jnp.float32)
        gradient_row_block = grad_all[block_index].astype(jnp.float32)
        key_row_block = key_all[chosen].reshape(SLOTS * BLOCK, HEADS, HEAD_DIM).astype(jnp.float32)
        value_row_block = value_all[chosen].reshape(SLOTS * BLOCK, HEADS, HEAD_DIM).astype(jnp.float32)
        lse_rows = lse_all[:, block_index, :]
        score_matrix = jnp.einsum("ltx,utx->tlu", query_row_block, key_row_block) * logit_scale
        soft_probs = jnp.where(usable[None], jnp.exp(score_matrix - lse_rows[:, :, None]), 0.0)
        probability_gradient = jnp.einsum("ltx,utx->tlu", gradient_row_block, value_row_block)
        row_delta = jnp.sum(soft_probs * probability_gradient, axis=-1)
        score_gradient = round_keep(soft_probs * (probability_gradient - row_delta[:, :, None]))
        rounded_probability = round_keep(soft_probs)
        query_gradient = (jnp.einsum("sov,vsp->osp", score_gradient, key_row_block) * logit_scale).astype(jnp.bfloat16)
        key_portion = jnp.einsum("yja,jye->aye", score_gradient, query_row_block) * logit_scale
        value_portion = jnp.einsum("yja,jye->aye", rounded_probability, gradient_row_block)
        key_sums = key_sums.at[chosen].add(key_portion.reshape(SLOTS, BLOCK, HEADS * HEAD_DIM))
        value_sums = value_sums.at[chosen].add(value_portion.reshape(SLOTS, BLOCK, HEADS * HEAD_DIM))
        return (key_sums, value_sums), query_gradient.reshape(BLOCK, HEADS * HEAD_DIM)

    empty = jnp.zeros((NBLOCKS, BLOCK, HEADS * HEAD_DIM), jnp.float32)
    (key_sums, value_sums), query_gradient = lax.scan(block_step, (empty, empty), jnp.arange(NBLOCKS, dtype=jnp.int32))
    query_gradient = query_gradient.reshape(TOKENS, D)
    key_grad = key_sums.reshape(TOKENS, D).astype(jnp.bfloat16)
    value_grad = value_sums.reshape(TOKENS, D).astype(jnp.bfloat16)
    input_grad = jnp.dot(query_gradient, w_qkv[0].T, preferred_element_type=jnp.float32)
    input_grad = input_grad + jnp.dot(key_grad, w_qkv[1].T, preferred_element_type=jnp.float32)
    input_grad = input_grad + jnp.dot(value_grad, w_qkv[2].T, preferred_element_type=jnp.float32)
    return query_gradient, key_grad, value_grad, input_grad.astype(jnp.bfloat16)
```

```python
import functools

import jax
import jax.numpy as jnp
from jax import lax
from jax.experimental import pallas as pl
from jax.experimental.pallas import tpu as pltpu
from jax.sharding import PartitionSpec as P

PATCHES = 16
BLOCK = 128
SPAN = 8
GROUP = 4
LANES = 128
LSE_ROWS = 16
F32 = jnp.float32
BF16 = jnp.bfloat16
VMEM_LIMIT = 40 * 1024 * 1024


def vmem():
    return pl.BlockSpec(memory_space=pltpu.VMEM)


def split_three(x):
    high = x.astype(BF16).astype(F32)
    rest = x - high
    mid = rest.astype(BF16).astype(F32)
    return high, mid, rest - mid


def pack_kernel(slots, head_dim, q_ref, k_ref, v_ref, g_ref, lse_ref, kv_ref, qo_ref):
    rows = q_ref.shape[0]
    blocks = rows // BLOCK
    scale = head_dim ** (-0.5)
    for member in range(GROUP):
        for slot in range(slots):
            head = member * slots + slot
            at = slice(head * head_dim, (head + 1) * head_dim)
            kv_ref[member, slot] = jnp.concatenate([k_ref[:, at], v_ref[:, at]], axis=1)
            scaled = (q_ref[:, at].astype(F32) * scale).astype(BF16)
            qo_ref[member, slot, :rows] = jnp.concatenate([scaled, g_ref[:, at]], axis=1)
            lse = lse_ref[head : head + 1, :]
            parts = [
                part[:, b * BLOCK : (b + 1) * BLOCK] for part in split_three(lse) for b in range(blocks)
            ]
            parts.append(jnp.zeros((LSE_ROWS - len(parts), BLOCK), F32))
            qo_ref[member, slot, rows:] = jnp.concatenate(parts, axis=0).astype(BF16)


def attend_kernel(
    slots,
    blocks_here,
    head_dim,
    kb_ref,
    own_ref,
    low_ref,
    high_ref,
    qo_ref,
    own_out,
    low_out,
    high_out,
    dq_out,
    kv_win,
    k_turn,
    acc,
    kv_pick,
    kt_pick,
    both,
    prob,
    prod,
    scores,
    sems,
):
    group_blocks = GROUP * blocks_here
    window = group_blocks + 2 * SPAN
    rows = blocks_here * BLOCK
    slot_count = kb_ref.shape[1]
    keys = slot_count * BLOCK
    chunk = 2 * BLOCK
    scale = head_dim ** (-0.5)
    first = (lax.axis_index("var") // GROUP) * group_blocks
    key_patch = lax.broadcasted_iota(jnp.int32, (PATCHES, BLOCK), 0)
    query_patch = lax.broadcasted_iota(jnp.int32, (PATCHES, BLOCK), 1) % PATCHES
    usable = key_patch <= query_patch
    lane = lax.broadcasted_iota(jnp.int32, (BLOCK, LANES), 1)

    for slot in range(slots):
        copies = [
            pltpu.make_async_copy(low_ref.at[slot], kv_win.at[pl.ds(0, SPAN)], sems.at[0]),
            pltpu.make_async_copy(
                high_ref.at[slot], kv_win.at[pl.ds(SPAN + group_blocks, SPAN)], sems.at[1]
            ),
        ]
        for member in range(GROUP):
            copies.append(
                pltpu.make_async_copy(
                    own_ref.at[member, slot],
                    kv_win.at[pl.ds(SPAN + member * blocks_here, blocks_here)],
                    sems.at[2 + member],
                )
            )
        for copy in copies:
            copy.start()
        acc[...] = jnp.zeros_like(acc)
        for copy in copies:
            copy.wait()

        @pl.loop(0, window)
        def _(block):
            k_turn[block] = kv_win[block][:, :head_dim].T

        for member in range(GROUP):
            lse_parts = qo_ref[member, slot, rows:].astype(F32)

            for local in range(blocks_here):
                query_block = member * blocks_here + local
                lse = (
                    lse_parts[local : local + 1]
                    + lse_parts[blocks_here + local : blocks_here + local + 1]
                ) + lse_parts[2 * blocks_here + local : 2 * blocks_here + local + 1]
                shift = jnp.where(usable, -lse, -1e30)
                qo = qo_ref[member, slot, local * BLOCK : (local + 1) * BLOCK]
                zero = jnp.zeros_like(qo)
                both[:BLOCK] = jnp.where(lane < head_dim, qo, zero)
                both[BLOCK:] = jnp.where(lane < head_dim, zero, qo)
                index = [
                    kb_ref[first + query_block, s] - first + SPAN for s in range(slot_count)
                ]
                for s in range(slot_count):
                    kv_pick[s * BLOCK : (s + 1) * BLOCK] = kv_win[index[s]]
                    kt_pick[:, s * BLOCK : (s + 1) * BLOCK] = k_turn[index[s]]
                delta = jnp.zeros((8, BLOCK), F32)
                for at in range(0, keys, chunk):
                    x = lax.dot_general(
                        kv_pick[at : at + chunk],
                        both[...],
                        (((1,), (1,)), ((), ())),
                        preferred_element_type=F32,
                    )
                    s_part = x[:, :BLOCK].reshape(chunk // PATCHES, PATCHES, BLOCK)
                    p = jnp.exp(s_part + shift[None]).reshape(chunk, BLOCK)
                    t = p * x[:, BLOCK:]
                    prob[at : at + chunk] = p
                    prod[at : at + chunk] = t
                    delta = delta + jnp.sum(t.reshape(chunk // 8, 8, BLOCK), axis=0)
                delta = jnp.sum(delta, axis=0, keepdims=True)
                dq = jnp.zeros((head_dim, BLOCK), F32)
                for at in range(0, keys, chunk):
                    p = prob[at : at + chunk]
                    ds = (prod[at : at + chunk] - p * delta).astype(BF16)
                    scores[at : at + chunk, :BLOCK] = ds
                    scores[at : at + chunk, BLOCK:] = p.astype(BF16)
                    dq = dq + jnp.dot(
                        kt_pick[:, at : at + chunk], ds, preferred_element_type=F32
                    )
                    r = jnp.dot(scores[at : at + chunk], both[...], preferred_element_type=F32)
                    for s in range(chunk // BLOCK):
                        where = index[at // BLOCK + s]
                        acc[where] = acc[where] + r[s * BLOCK : (s + 1) * BLOCK]
                dq_out[
                    member,
                    local * BLOCK : (local + 1) * BLOCK,
                    slot * head_dim : (slot + 1) * head_dim,
                ] = (dq * scale).T.astype(BF16)

        low_out[slot] = acc[:SPAN].astype(BF16)
        high_out[slot] = acc[SPAN + group_blocks :].astype(BF16)
        own_out[slot] = acc[SPAN : SPAN + group_blocks]


def finish_kernel(
    slots, head_dim, dkv_ref, dq_ref, w_ref, dq_out, dk_out, dv_out, send_out, keep_out, grads
):
    half = keep_out.shape[0]
    for member in range(GROUP):
        for slot in range(slots):
            head = member * slots + slot
            at = slice(head * head_dim, (head + 1) * head_dim)
            both = dkv_ref[member, slot]
            grads[1, :, at] = both[:, :head_dim]
            grads[2, :, at] = both[:, head_dim:]
            grads[0, :, at] = dq_ref[member, :, slot * head_dim : (slot + 1) * head_dim]
    dq_out[...] = grads[0]
    dk_out[...] = grads[1]
    dv_out[...] = grads[2]
    me = lax.axis_index("head")
    heads = lax.axis_size("head")
    for piece in range(heads):
        owner = (me + 1 + piece) % heads
        begin = pl.multiple_of(owner * half, half)
        total = None
        for s in range(3):
            part = lax.dot_general(
                grads[s, pl.ds(begin, half), :],
                w_ref[s],
                (((1,), (1,)), ((), ())),
                preferred_element_type=F32,
            )
            total = part if total is None else total + part
        if piece == heads - 1:
            keep_out[...] = total
        else:
            send_out[piece] = total.astype(BF16)


def body(queries, keys, values, out_grad, log_sum_exp, key_blocks, w_qkv):
    rows, features = queries.shape
    head_count = log_sum_exp.shape[0]
    head_dim = features // head_count
    slots = head_count // GROUP
    blocks_here = rows // BLOCK
    group_blocks = GROUP * blocks_here
    window = group_blocks + 2 * SPAN
    slot_count = key_blocks.shape[1]
    devices = lax.axis_size("var")
    heads = lax.axis_size("head")
    width = w_qkv.shape[1]
    groups = [[base + i for i in range(GROUP)] for base in range(0, devices, GROUP)]
    params = pltpu.CompilerParams(vmem_limit_bytes=VMEM_LIMIT)

    def swap(x):
        return lax.all_to_all(x, "var", 0, 0, axis_index_groups=groups)

    def up(x):
        return lax.ppermute(x, "var", [(n, n + GROUP) for n in range(devices - GROUP)])

    def down(x):
        return lax.ppermute(x, "var", [(n + GROUP, n) for n in range(devices - GROUP)])

    kv, qo = pl.pallas_call(
        functools.partial(pack_kernel, slots, head_dim),
        out_shape=(
            jax.ShapeDtypeStruct((GROUP, slots, rows, LANES), BF16),
            jax.ShapeDtypeStruct((GROUP, slots, rows + LSE_ROWS, LANES), BF16),
        ),
        in_specs=[vmem()] * 5,
        out_specs=(vmem(), vmem()),
        compiler_params=params,
    )(queries, keys, values, out_grad, log_sum_exp)

    own = swap(kv)
    lined = own.transpose(1, 0, 2, 3).reshape(slots, group_blocks, BLOCK, LANES)
    low = up(lined[:, group_blocks - SPAN :])
    high = down(lined[:, :SPAN])
    qo = swap(qo)
    own = own.reshape(GROUP, slots, blocks_here, BLOCK, LANES)

    anyspec = pl.BlockSpec(memory_space=pl.ANY)
    pairs = slots * group_blocks * slot_count * BLOCK * BLOCK
    own_sum, low_part, high_part, dq = pl.pallas_call(
        functools.partial(attend_kernel, slots, blocks_here, head_dim),
        out_shape=(
            jax.ShapeDtypeStruct((slots, group_blocks, BLOCK, LANES), F32),
            jax.ShapeDtypeStruct((slots, SPAN, BLOCK, LANES), BF16),
            jax.ShapeDtypeStruct((slots, SPAN, BLOCK, LANES), BF16),
            jax.ShapeDtypeStruct((GROUP, rows, slots * head_dim), BF16),
        ),
        in_specs=[pl.BlockSpec(memory_space=pltpu.SMEM), anyspec, anyspec, anyspec, vmem()],
        out_specs=(vmem(),) * 4,
        scratch_shapes=[
            pltpu.VMEM((window, BLOCK, LANES), BF16),
            pltpu.VMEM((window, head_dim, BLOCK), BF16),
            pltpu.VMEM((window, BLOCK, LANES), F32),
            pltpu.VMEM((slot_count * BLOCK, LANES), BF16),
            pltpu.VMEM((head_dim, slot_count * BLOCK), BF16),
            pltpu.VMEM((2 * BLOCK, LANES), BF16),
            pltpu.VMEM((slot_count * BLOCK, BLOCK), F32),
            pltpu.VMEM((slot_count * BLOCK, BLOCK), F32),
            pltpu.VMEM((slot_count * BLOCK, 2 * BLOCK), BF16),
            pltpu.SemaphoreType.DMA((2 + GROUP,)),
        ],
        compiler_params=params,
        cost_estimate=pl.CostEstimate(
            flops=10 * pairs * head_dim, bytes_accessed=4_000_000, transcendentals=pairs
        ),
    )(key_blocks, own, low, high, qo)

    from_above = down(low_part).astype(F32)
    from_below = up(high_part).astype(F32)
    rest = ((0, 0), (0, 0))
    left = group_blocks - SPAN
    dkv = (
        own_sum
        + jnp.pad(from_above, ((0, 0), (left, 0)) + rest)
        + jnp.pad(from_below, ((0, 0), (0, left)) + rest)
    ).astype(BF16)
    dkv = dkv.reshape(slots, GROUP, rows, LANES).transpose(1, 0, 2, 3)
    dq = swap(dq)
    dkv = swap(dkv)

    half = rows // heads
    dq_out, dk_out, dv_out, send, keep = pl.pallas_call(
        functools.partial(finish_kernel, slots, head_dim),
        out_shape=(
            jax.ShapeDtypeStruct((rows, features), BF16),
            jax.ShapeDtypeStruct((rows, features), BF16),
            jax.ShapeDtypeStruct((rows, features), BF16),
            jax.ShapeDtypeStruct((heads - 1, half, width), BF16),
            jax.ShapeDtypeStruct((half, width), F32),
        ),
        in_specs=[vmem()] * 3,
        out_specs=(vmem(),) * 5,
        scratch_shapes=[pltpu.VMEM((3, rows, features), BF16)],
        compiler_params=params,
    )(dkv, dq, w_qkv)
    total = keep
    for piece in range(heads - 1):
        turn = piece + 1
        got = lax.ppermute(send[piece], "head", [(n, (n + turn) % heads) for n in range(heads)])
        total = total + got.astype(F32)
    return dq_out, dk_out, dv_out, total.astype(BF16)


def solution(mesh):
    in_specs = (
        P("var", "head"),
        P("var", "head"),
        P("var", "head"),
        P("var", "head"),
        P("head", "var"),
        P(),
        P(None, None, "head"),
    )
    out_specs = (P("var", "head"), P("var", "head"), P("var", "head"), P(("var", "head"), None))
    return jax.shard_map(body, mesh=mesh, in_specs=in_specs, out_specs=out_specs, check_vma=False)
```

```python
import functools

import jax
import jax.numpy as jnp
from jax import lax
from jax.experimental import pallas as pl
from jax.experimental.pallas import tpu as pltpu
from jax.sharding import PartitionSpec as P

PATCHES = 16
BLOCK = 128
HALF = BLOCK // 2
SPAN = 8
GROUP = 4
LANES = 128
LSE_ROWS = 16
LOADS = 3
F32 = jnp.float32
BF16 = jnp.bfloat16
MIB = 1024 * 1024


def vmem():
    return pl.BlockSpec(memory_space=pltpu.VMEM)


def params(mib):
    return pltpu.CompilerParams(vmem_limit_bytes=mib * MIB)


def shaped(shape, dtype=BF16):
    return jax.ShapeDtypeStruct(shape, dtype)


def dot(a, b):
    return jnp.dot(a, b, preferred_element_type=F32)


def dot_nt(a, b):
    return lax.dot_general(a, b, (((1,), (1,)), ((), ())), preferred_element_type=F32)


def token_at(place):
    return (((place & (HALF - 1)) >> 3) << 4) + ((place >> 6) << 3) + (place & 7)


def one_where(mask):
    return jnp.where(mask, 1.0, 0.0).astype(BF16)


def reorder_matrix(inverse):
    row = lax.broadcasted_iota(jnp.int32, (BLOCK, BLOCK), 0)
    col = lax.broadcasted_iota(jnp.int32, (BLOCK, BLOCK), 1)
    return one_where(row == token_at(col)) if inverse else one_where(col == token_at(row))


def split_three(x):
    high = x.astype(BF16).astype(F32)
    rest = x - high
    mid = rest.astype(BF16).astype(F32)
    return high, mid, rest - mid


def widen(x):
    if x.shape[1] == LANES:
        return x
    return jnp.concatenate([x, jnp.zeros((x.shape[0], LANES - x.shape[1]), x.dtype)], axis=1)


def load_all(pairs, sems):
    copies = []
    for i, (source, target) in enumerate(pairs):
        rows = source.shape[0] // LOADS
        for part in range(LOADS):
            at = pl.ds(part * rows, rows)
            copies.append(pltpu.make_async_copy(source.at[at], target.at[at], sems.at[i, part]))
    for copy in copies:
        copy.start()
    for copy in copies:
        copy.wait()


def pack_kv_kernel(k_hbm, v_hbm, *rest):
    outs, (k_ref, v_ref, turned, sems) = rest[:GROUP], rest[GROUP:]
    load_all([(k_hbm, k_ref), (v_hbm, v_ref)], sems)
    rows, features = k_ref.shape
    width = features // GROUP
    order = reorder_matrix(False)
    for b in range(rows // BLOCK):
        at = slice(b * BLOCK, (b + 1) * BLOCK)
        for half, ref in enumerate((k_ref, v_ref)):
            moved = dot(order, ref[at]).astype(BF16)
            for member in range(GROUP):
                turned[member, at, half * LANES : (half + 1) * LANES] = widen(
                    moved[:, member * width : (member + 1) * width]
                )
    me = lax.axis_index("var") % GROUP
    for distance, out in enumerate(outs):
        out[...] = turned[me ^ distance]


def pack_qo_kernel(slots, head_dim, q_hbm, g_hbm, lse_ref, qo_ref, q_ref, g_ref, sems):
    load_all([(q_hbm, q_ref), (g_hbm, g_ref)], sems)
    rows, features = q_ref.shape
    width = features // GROUP
    blocks = rows // BLOCK
    order = reorder_matrix(False)
    scale = head_dim ** (-0.5)
    for b in range(blocks):
        at = slice(b * BLOCK, (b + 1) * BLOCK)
        for half, ref in enumerate((q_ref, g_ref)):
            moved = dot(order, ref[at])
            if half == 0:
                moved = moved * scale
            moved = moved.astype(BF16)
            for member in range(GROUP):
                qo_ref[member, at, half * LANES : (half + 1) * LANES] = widen(
                    moved[:, member * width : (member + 1) * width]
                )
    token = lax.broadcasted_iota(jnp.int32, (BLOCK, 2 * LANES), 0)
    lane = lax.broadcasted_iota(jnp.int32, (BLOCK, 2 * LANES), 1)
    place = ((lane >> 7) << 6) + (lane & (HALF - 1))
    hit = token == token_at(place)
    upper = (lane & HALF) != 0
    spread = [one_where(hit & ~upper), one_where(hit & upper)]
    for member in range(GROUP):
        total = None
        for slot in range(slots):
            lse = lse_ref[member * slots + slot : member * slots + slot + 1, :]
            parts = [
                part[:, b * BLOCK : (b + 1) * BLOCK]
                for part in split_three(lse)
                for b in range(blocks)
            ]
            parts.append(jnp.zeros((LSE_ROWS - len(parts), BLOCK), F32))
            moved = dot(jnp.concatenate(parts, axis=0).astype(BF16), spread[slot])
            total = moved if total is None else total + moved
        qo_ref[member, rows:] = total.astype(BF16)


def exchange_start(group_blocks):
    odd = (lax.axis_index("var") // GROUP) % 2
    reach = group_blocks - SPAN
    return (1 - odd) * reach, odd * reach


def line_kernel(*refs):
    pieces, (own, first_out, second_out) = refs[:GROUP], refs[GROUP:]
    blocks = pieces[0].shape[0] // BLOCK
    me = lax.axis_index("var") % GROUP
    for distance, piece in enumerate(pieces):
        own[pl.ds((me ^ distance) * blocks, blocks)] = piece[...].reshape(blocks, BLOCK, 2 * LANES)
    first, second = exchange_start(GROUP * blocks)
    first_out[...] = own[pl.ds(first, SPAN)]
    second_out[...] = own[pl.ds(second, SPAN)]


def attend_kernel(
    blocks_here,
    head_dim,
    kb_ref,
    own_ref,
    first_ref,
    second_ref,
    qo_ref,
    own_out,
    first_out,
    second_out,
    dq_out,
    kv_win,
    k_turn,
    acc,
    shifts,
    queries,
    grads,
    crossed,
    prob,
    slope,
):
    group_blocks = GROUP * blocks_here
    window = group_blocks + 2 * SPAN
    rows = blocks_here * BLOCK
    slot_count = kb_ref.shape[1]
    scale = head_dim ** (-0.5)
    base = (lax.axis_index("var") // GROUP) * group_blocks
    odd = (lax.axis_index("var") // GROUP) % 2
    top = window - SPAN
    first_at, second_at = (1 - odd) * top, odd * top
    low = slice(0, LANES)
    high = slice(LANES, 2 * LANES)

    kv_win[SPAN : SPAN + group_blocks] = own_ref[...]
    kv_win[pl.ds(first_at, SPAN)] = first_ref[...]
    kv_win[pl.ds(second_at, SPAN)] = second_ref[...]
    key_patch = lax.broadcasted_iota(jnp.int32, (8, LANES), 0)
    query_patch = lax.broadcasted_iota(jnp.int32, (8, LANES), 1) & 7
    usable = key_patch <= query_patch
    for member in range(GROUP):
        parts = qo_ref[member, rows:].astype(F32)
        for local in range(blocks_here):
            lse = (
                parts[local : local + 1] + parts[blocks_here + local : blocks_here + local + 1]
            ) + parts[2 * blocks_here + local : 2 * blocks_here + local + 1]
            at = member * blocks_here + local
            shifts[at, 0, :, low] = jnp.where(usable, -lse[:, low], -1e30)
            shifts[at, 0, :, high] = jnp.broadcast_to(-lse[:, high], (8, LANES))
            shifts[at, 1, :, low] = jnp.where(usable, -lse[:, high], -1e30)
    acc[...] = jnp.zeros_like(acc)
    crossed[...] = jnp.zeros_like(crossed)

    @pl.loop(0, window)
    def _(block):
        k_turn[block] = kv_win[block, :, low].T

    unorder = reorder_matrix(True)
    lane = lax.broadcasted_iota(jnp.int32, (HALF, LANES), 1)
    head_a = lane < HALF

    def picks(query_block):
        return [kb_ref[base + query_block, s] - base + SPAN for s in range(slot_count)]

    def lay_out(member, local, buf):
        at = pl.multiple_of(local * BLOCK, BLOCK)
        for part in range(2):
            rows_at = pl.ds(at + part * HALF, HALF)
            for cols, target in ((low, queries), (high, grads)):
                tile = qo_ref[member, rows_at, cols]
                zero = jnp.zeros_like(tile)
                both = jnp.concatenate(
                    [jnp.where(head_a, tile, zero), jnp.where(head_a, zero, tile)], axis=0
                )
                target[buf, part * BLOCK : (part + 1) * BLOCK] = both
                if part == 1:
                    side = 0 if target is queries else 1
                    crossed[
                        buf, side * BLOCK : (side + 1) * BLOCK, side * LANES : (side + 1) * LANES
                    ] = both

    def gather(index, rows_of, cols):
        return jnp.concatenate([kv_win[i, rows_of, cols] for i in index], axis=0)

    early = slice(0, HALF)
    late = slice(HALF, BLOCK)
    both_cols = slice(0, 2 * LANES)
    early_rows = slot_count * HALF

    def forward(query_block, buf):
        lay_out(query_block // blocks_here, query_block % blocks_here, buf)
        index = picks(query_block)
        s = dot_nt(gather(index, early, low), queries[buf])
        g = dot_nt(gather(index, early, high), grads[buf])
        x = dot_nt(gather(index, late, both_cols), crossed[buf])
        shift = shifts[query_block, 0][None]
        p = jnp.exp(s.reshape(early_rows // 8, 8, 2 * LANES) + shift).reshape(early_rows, 2 * LANES)
        prob[buf, :early_rows] = p
        slope[buf, :early_rows] = g
        delta = jnp.sum((p * g).reshape(early_rows // 8, 8, 2 * LANES), axis=0)
        late_shift = shifts[query_block, 1, :, low][None]
        q = jnp.exp(x[:, low].reshape(early_rows // 8, 8, LANES) + late_shift).reshape(
            early_rows, LANES
        )
        prob[buf, early_rows:, low] = q
        slope[buf, early_rows:, low] = x[:, high]
        more = jnp.sum((q * x[:, high]).reshape(early_rows // 8, 8, LANES), axis=0)
        delta_low = jnp.sum(delta[:, low], axis=0, keepdims=True)
        delta_high = jnp.sum(delta[:, high] + more, axis=0, keepdims=True)
        return jnp.concatenate([delta_low, delta_high], axis=1)

    def backward(query_block, buf, delta):
        index = picks(query_block)
        p = prob[buf, :early_rows]
        ds = (p * (slope[buf, :early_rows] - delta)).astype(BF16)
        q = prob[buf, early_rows:, low]
        ds_late = (q * (slope[buf, early_rows:, low] - delta[:, high])).astype(BF16)
        dk = dot(ds, queries[buf])
        dv = dot(p.astype(BF16), grads[buf])
        r = dot(jnp.concatenate([ds_late, q.astype(BF16)], axis=1), crossed[buf])
        nothing = jnp.zeros((HALF, LANES), BF16)
        pieces = []
        for s in range(slot_count):
            at = slice(s * HALF, (s + 1) * HALF)
            where = index[s]
            acc[where, early, low] = acc[where, early, low] + dk[at]
            acc[where, early, high] = acc[where, early, high] + dv[at]
            acc[where, late] = acc[where, late] + r[at]
            pieces.append(ds[at])
            pieces.append(jnp.concatenate([nothing, ds_late[at]], axis=1))
        keys_turned = jnp.concatenate([k_turn[i] for i in index], axis=1)
        dq = dot(keys_turned, jnp.concatenate(pieces, axis=0)) * scale
        halves = []
        for cols in (low, high):
            turned = dq[:, cols].T
            halves.append(jnp.where(head_a, turned[:HALF], turned[HALF:]))
        moved = dot(unorder, jnp.concatenate(halves, axis=0).astype(BF16)).astype(BF16)
        dq_out[pl.ds(pl.multiple_of(query_block * BLOCK, BLOCK), BLOCK)] = moved

    delta = forward(0, 0)

    def step(j, delta):
        block = 2 * j
        later = forward(block + 1, 1)
        backward(block, 0, delta)
        last = forward(block + 2, 0)
        backward(block + 1, 1, later)
        return last

    delta = lax.fori_loop(0, (group_blocks - 1) // 2, step, delta)
    if group_blocks % 2 == 0:
        later = forward(group_blocks - 1, 1)
        backward(group_blocks - 2, 0, delta)
        backward(group_blocks - 1, 1, later)
    else:
        backward(group_blocks - 1, 0, delta)

    first_out[...] = acc[pl.ds(first_at, SPAN)].astype(BF16)
    second_out[...] = acc[pl.ds(second_at, SPAN)].astype(BF16)
    own_out[...] = acc[SPAN : SPAN + group_blocks]


def owner_start(piece, half):
    heads = lax.axis_size("head")
    return pl.multiple_of(((lax.axis_index("head") + 1 + piece) % heads) * half, half)


def combine_kernel(own_ref, first_ref, second_ref, away_out, home_out, total, moved):
    group_blocks = own_ref.shape[0]
    blocks_here = group_blocks // GROUP
    half = home_out.shape[1]
    first, second = exchange_start(group_blocks)
    total[...] = own_ref[...]
    for start, ref in ((first, first_ref), (second, second_ref)):
        at = pl.ds(start, SPAN)
        total[at] = total[at] + ref[...].astype(F32)
    unorder = reorder_matrix(True)
    for block in range(group_blocks):
        at = (block % blocks_here) * BLOCK
        moved[block // blocks_here, at : at + BLOCK] = dot(
            unorder, total[block].astype(BF16)
        ).astype(BF16)
    away = away_out.shape[1] // half
    for member in range(GROUP):
        for piece in range(away):
            away_out[member, piece * half : (piece + 1) * half] = moved[
                member, pl.ds(owner_start(piece, half), half)
            ]
        home_out[member] = moved[member, pl.ds(owner_start(away, half), half)]


def gather_rows(grads, dq_ref, start, dkv_ref, dkv_at):
    half = grads.shape[1]
    width = grads.shape[2] // GROUP
    for member in range(GROUP):
        at = slice(member * width, (member + 1) * width)
        both = dkv_ref[member, dkv_at * half : (dkv_at + 1) * half]
        grads[0, :, at] = dq_ref[member, pl.ds(start, half)][:, :width]
        grads[1, :, at] = both[:, :width]
        grads[2, :, at] = both[:, LANES : LANES + width]


def product(grads, w_ref):
    total = dot_nt(grads[0], w_ref[0])
    for s in (1, 2):
        total = total + dot_nt(grads[s], w_ref[s])
    return total


def away_kernel(dq_ref, dkv_ref, w_ref, *rest):
    outs, grads = rest[:-1], rest[-1]
    half = grads.shape[1]
    for piece, out in enumerate(outs):
        gather_rows(grads, dq_ref, owner_start(piece, half), dkv_ref, piece)
        out[...] = product(grads, w_ref).astype(BF16)


def home_kernel(dq_ref, away_ref, home_ref, w_ref, dq_out, dk_out, dv_out, keep_out, grads):
    half = grads.shape[1]
    away = away_ref.shape[1] // half
    for piece in range(away + 1):
        start = owner_start(piece, half)
        if piece < away:
            gather_rows(grads, dq_ref, start, away_ref, piece)
        else:
            gather_rows(grads, dq_ref, start, home_ref, 0)
        at = pl.ds(start, half)
        dq_out[at] = grads[0]
        dk_out[at] = grads[1]
        dv_out[at] = grads[2]
    keep_out[...] = product(grads, w_ref)


def body(queries, keys, values, out_grad, log_sum_exp, key_blocks, w_qkv):
    rows, features = queries.shape
    head_count = log_sum_exp.shape[0]
    head_dim = features // head_count
    slots = head_count // GROUP
    blocks_here = rows // BLOCK
    group_blocks = GROUP * blocks_here
    window = group_blocks + 2 * SPAN
    slot_count = key_blocks.shape[1]
    devices = lax.axis_size("var")
    heads = lax.axis_size("head")
    half = rows // heads
    model = w_qkv.shape[1]
    wide = 2 * LANES
    groups = [[start + i for i in range(GROUP)] for start in range(0, devices, GROUP)]
    hbm = pl.BlockSpec(memory_space=pltpu.HBM)

    def swap(x):
        return lax.all_to_all(x, "var", 0, 0, axis_index_groups=groups)

    def trade(x, distance):
        return lax.ppermute(x, "var", [(n, n ^ distance) for n in range(devices)])

    def trade_first(x):
        pairs = [(n, n ^ GROUP) for n in range(devices) if (n ^ GROUP) < devices]
        return lax.ppermute(x, "var", pairs)

    def trade_second(x):
        pairs = []
        for n in range(devices):
            other = n + GROUP if (n // GROUP) % 2 else n - GROUP
            if 0 <= other < devices:
                pairs.append((n, other))
        return lax.ppermute(x, "var", pairs)

    loaded = [pltpu.VMEM((rows, features), BF16), pltpu.VMEM((rows, features), BF16)]
    sems = [pltpu.SemaphoreType.DMA((2, LOADS))]
    kvs = pl.pallas_call(
        pack_kv_kernel,
        out_shape=(shaped((rows, wide)),) * GROUP,
        in_specs=[hbm] * 2,
        out_specs=(vmem(),) * GROUP,
        scratch_shapes=loaded + [pltpu.VMEM((GROUP, rows, wide), BF16)] + sems,
        compiler_params=params(48),
    )(keys, values)
    qo = pl.pallas_call(
        functools.partial(pack_qo_kernel, slots, head_dim),
        out_shape=shaped((GROUP, rows + LSE_ROWS, wide)),
        in_specs=[hbm, hbm, vmem()],
        out_specs=vmem(),
        scratch_shapes=loaded + sems,
        compiler_params=params(12),
    )(queries, out_grad, log_sum_exp)

    pieces = [kvs[0]] + [None] * (GROUP - 1)
    for distance in (2, 3, 1):
        pieces[distance] = trade(kvs[distance], distance)
    own, first_send, second_send = pl.pallas_call(
        line_kernel,
        out_shape=(
            shaped((group_blocks, BLOCK, wide)),
            shaped((SPAN, BLOCK, wide)),
            shaped((SPAN, BLOCK, wide)),
        ),
        in_specs=[vmem()] * GROUP,
        out_specs=(vmem(),) * 3,
        compiler_params=params(12),
    )(*pieces)
    first = trade_first(first_send)
    second = trade_second(second_send)
    qo = swap(qo)

    pairs = group_blocks * slot_count * BLOCK * BLOCK * slots
    own_sum, first_part, second_part, dq = pl.pallas_call(
        functools.partial(attend_kernel, blocks_here, head_dim),
        out_shape=(
            shaped((group_blocks, BLOCK, wide), F32),
            shaped((SPAN, BLOCK, wide)),
            shaped((SPAN, BLOCK, wide)),
            shaped((group_blocks * BLOCK, LANES)),
        ),
        in_specs=[pl.BlockSpec(memory_space=pltpu.SMEM)] + [vmem()] * 4,
        out_specs=(vmem(),) * 4,
        scratch_shapes=[
            pltpu.VMEM((window, BLOCK, wide), BF16),
            pltpu.VMEM((window, LANES, BLOCK), BF16),
            pltpu.VMEM((window, BLOCK, wide), F32),
            pltpu.VMEM((group_blocks, 2, 8, wide), F32),
            pltpu.VMEM((2, wide, LANES), BF16),
            pltpu.VMEM((2, wide, LANES), BF16),
            pltpu.VMEM((2, wide, wide), BF16),
            pltpu.VMEM((2, slot_count * BLOCK, wide), F32),
            pltpu.VMEM((2, slot_count * BLOCK, wide), F32),
        ],
        compiler_params=params(24),
        cost_estimate=pl.CostEstimate(
            flops=40 * pairs * head_dim, bytes_accessed=2_000_000, transcendentals=pairs
        ),
    )(key_blocks, own, first, second, qo)

    first_back = trade_first(first_part)
    second_back = trade_second(second_part)
    dq = swap(dq.reshape(GROUP, rows, LANES))
    away, home = pl.pallas_call(
        combine_kernel,
        out_shape=(shaped((GROUP, rows - half, wide)), shaped((GROUP, half, wide))),
        in_specs=[vmem()] * 3,
        out_specs=(vmem(),) * 2,
        scratch_shapes=[
            pltpu.VMEM((group_blocks, BLOCK, wide), F32),
            pltpu.VMEM((GROUP, rows, wide), BF16),
        ],
        compiler_params=params(16),
    )(own_sum, first_back, second_back)
    away = swap(away)
    home = swap(home)

    grads = [pltpu.VMEM((3, half, features), BF16)]
    sends = pl.pallas_call(
        away_kernel,
        out_shape=(shaped((half, model)),) * (heads - 1),
        in_specs=[vmem()] * 3,
        out_specs=(vmem(),) * (heads - 1),
        scratch_shapes=grads,
        compiler_params=params(16),
        cost_estimate=pl.CostEstimate(
            flops=6 * (rows - half) * features * model, bytes_accessed=4_000_000, transcendentals=0
        ),
    )(dq, away, w_qkv)
    dq_out, dk_out, dv_out, total = pl.pallas_call(
        home_kernel,
        out_shape=(shaped((rows, features)),) * 3 + (shaped((half, model), F32),),
        in_specs=[vmem()] * 4,
        out_specs=(vmem(),) * 4,
        scratch_shapes=grads,
        compiler_params=params(16),
        cost_estimate=pl.CostEstimate(
            flops=6 * half * features * model, bytes_accessed=6_000_000, transcendentals=0
        ),
    )(dq, away, home, w_qkv)
    for piece, send in enumerate(sends):
        got = lax.ppermute(send, "head", [(n, (n + piece + 1) % heads) for n in range(heads)])
        total = total + got.astype(F32)
    return dq_out, dk_out, dv_out, total.astype(BF16)


def solution(mesh):
    in_specs = (
        P("var", "head"),
        P("var", "head"),
        P("var", "head"),
        P("var", "head"),
        P("head", "var"),
        P(),
        P(None, None, "head"),
    )
    out_specs = (P("var", "head"), P("var", "head"), P("var", "head"), P(("var", "head"), None))
    return jax.shard_map(body, mesh=mesh, in_specs=in_specs, out_specs=out_specs, check_vma=False)
```

```python
import functools

import jax
import jax.numpy as jnp
from jax import lax
from jax.experimental import pallas as pl
from jax.experimental.pallas import tpu as pltpu
from jax.sharding import PartitionSpec as P

PATCHES = 16
BLOCK = 128
HALF = BLOCK // 2
SPAN = 8
GROUP = 4
LANES = 128
LSE_ROWS = 16
LOADS = 3
F32 = jnp.float32
BF16 = jnp.bfloat16
MIB = 1024 * 1024


def vmem():
    return pl.BlockSpec(memory_space=pltpu.VMEM)


def params(mib):
    return pltpu.CompilerParams(vmem_limit_bytes=mib * MIB)


def shaped(shape, dtype=BF16):
    return jax.ShapeDtypeStruct(shape, dtype)


def dot(a, b):
    return jnp.dot(a, b, preferred_element_type=F32)


def dot_nt(a, b):
    return lax.dot_general(a, b, (((1,), (1,)), ((), ())), preferred_element_type=F32)


def token_at(place):
    return (((place & (HALF - 1)) >> 3) << 4) + ((place >> 6) << 3) + (place & 7)


def one_where(mask):
    return jnp.where(mask, 1.0, 0.0).astype(BF16)


def reorder_matrix(inverse):
    row = lax.broadcasted_iota(jnp.int32, (BLOCK, BLOCK), 0)
    col = lax.broadcasted_iota(jnp.int32, (BLOCK, BLOCK), 1)
    return one_where(row == token_at(col)) if inverse else one_where(col == token_at(row))


def split_three(x):
    high = x.astype(BF16).astype(F32)
    rest = x - high
    mid = rest.astype(BF16).astype(F32)
    return high, mid, rest - mid


def widen(x):
    if x.shape[1] == LANES:
        return x
    return jnp.concatenate([x, jnp.zeros((x.shape[0], LANES - x.shape[1]), x.dtype)], axis=1)


def load_all(pairs, sems):
    copies = []
    for i, (source, target) in enumerate(pairs):
        rows = source.shape[0] // LOADS
        for part in range(LOADS):
            at = pl.ds(part * rows, rows)
            copies.append(pltpu.make_async_copy(source.at[at], target.at[at], sems.at[i, part]))
    for copy in copies:
        copy.start()
    for copy in copies:
        copy.wait()


def send_pieces(outs, stage):
    me = lax.axis_index("var") % GROUP
    for distance, out in enumerate(outs):
        out[...] = stage[me ^ distance]


def stage_pieces(stage, pieces):
    me = lax.axis_index("var") % GROUP
    for distance, piece in enumerate(pieces):
        stage[me ^ distance] = piece[...]


def pack_kernel(x_hbm, *rest):
    outs, (x_ref, turned, sems) = rest[:GROUP], rest[GROUP:]
    load_all([(x_hbm, x_ref)], sems)
    rows, features = x_ref.shape
    width = features // GROUP
    order = reorder_matrix(False)
    for b in range(rows // BLOCK):
        at = slice(b * BLOCK, (b + 1) * BLOCK)
        moved = dot(order, x_ref[at]).astype(BF16)
        for member in range(GROUP):
            turned[member, at] = widen(moved[:, member * width : (member + 1) * width])
    send_pieces(outs, turned)


def pack_qo_kernel(slots, head_dim, q_hbm, g_hbm, lse_ref, *rest):
    outs, (q_ref, g_ref, qo_ref, sems) = rest[:GROUP], rest[GROUP:]
    load_all([(q_hbm, q_ref), (g_hbm, g_ref)], sems)
    rows, features = q_ref.shape
    width = features // GROUP
    blocks = rows // BLOCK
    order = reorder_matrix(False)
    scale = head_dim ** (-0.5)
    for b in range(blocks):
        at = slice(b * BLOCK, (b + 1) * BLOCK)
        for half, ref in enumerate((q_ref, g_ref)):
            moved = dot(order, ref[at])
            if half == 0:
                moved = moved * scale
            moved = moved.astype(BF16)
            for member in range(GROUP):
                qo_ref[member, at, half * LANES : (half + 1) * LANES] = widen(
                    moved[:, member * width : (member + 1) * width]
                )
    token = lax.broadcasted_iota(jnp.int32, (BLOCK, 2 * LANES), 0)
    lane = lax.broadcasted_iota(jnp.int32, (BLOCK, 2 * LANES), 1)
    place = ((lane >> 7) << 6) + (lane & (HALF - 1))
    hit = token == token_at(place)
    upper = (lane & HALF) != 0
    spread = [one_where(hit & ~upper), one_where(hit & upper)]
    for member in range(GROUP):
        total = None
        for slot in range(slots):
            lse = lse_ref[member * slots + slot : member * slots + slot + 1, :]
            parts = [
                part[:, b * BLOCK : (b + 1) * BLOCK]
                for part in split_three(lse)
                for b in range(blocks)
            ]
            parts.append(jnp.zeros((LSE_ROWS - len(parts), BLOCK), F32))
            moved = dot(jnp.concatenate(parts, axis=0).astype(BF16), spread[slot])
            total = moved if total is None else total + moved
        qo_ref[member, rows:] = total.astype(BF16)
    send_pieces(outs, qo_ref)


def exchange_start(group_blocks):
    odd = (lax.axis_index("var") // GROUP) % 2
    reach = group_blocks - SPAN
    return (1 - odd) * reach, odd * reach


def line_kernel(*refs):
    pieces, (own, first_out, second_out) = refs[:GROUP], refs[GROUP:]
    blocks = pieces[0].shape[0] // BLOCK
    me = lax.axis_index("var") % GROUP
    for distance, piece in enumerate(pieces):
        own[pl.ds((me ^ distance) * blocks, blocks)] = piece[...].reshape(blocks, BLOCK, LANES)
    first, second = exchange_start(GROUP * blocks)
    first_out[...] = own[pl.ds(first, SPAN)]
    second_out[...] = own[pl.ds(second, SPAN)]


def attend_kernel(
    blocks_here,
    head_dim,
    kb_ref,
    *refs,
):
    key_refs, value_refs, refs = refs[:3], refs[3:6], refs[6:]
    qo_pieces, refs = refs[:GROUP], refs[GROUP:]
    key_outs, value_outs, refs = refs[:3], refs[3:6], refs[6:]
    dq_outs, refs = refs[:GROUP], refs[GROUP:]
    kv_win, k_turn, acc, shifts, queries, grads, crossed, prob, slope, qo_ref, dq_all = refs
    group_blocks = GROUP * blocks_here
    window = group_blocks + 2 * SPAN
    rows = blocks_here * BLOCK
    slot_count = kb_ref.shape[1]
    scale = head_dim ** (-0.5)
    base = (lax.axis_index("var") // GROUP) * group_blocks
    odd = (lax.axis_index("var") // GROUP) % 2
    top = window - SPAN
    first_at, second_at = (1 - odd) * top, odd * top
    low = slice(0, LANES)
    high = slice(LANES, 2 * LANES)

    for cols, (own_ref, first_ref, second_ref) in ((low, key_refs), (high, value_refs)):
        kv_win[SPAN : SPAN + group_blocks, :, cols] = own_ref[...]
        kv_win[pl.ds(first_at, SPAN), :, cols] = first_ref[...]
        kv_win[pl.ds(second_at, SPAN), :, cols] = second_ref[...]
    stage_pieces(qo_ref, qo_pieces)
    key_patch = lax.broadcasted_iota(jnp.int32, (8, LANES), 0)
    query_patch = lax.broadcasted_iota(jnp.int32, (8, LANES), 1) & 7
    usable = key_patch <= query_patch
    for member in range(GROUP):
        parts = qo_ref[member, rows:].astype(F32)
        for local in range(blocks_here):
            lse = (
                parts[local : local + 1] + parts[blocks_here + local : blocks_here + local + 1]
            ) + parts[2 * blocks_here + local : 2 * blocks_here + local + 1]
            at = member * blocks_here + local
            shifts[at, 0, :, low] = jnp.where(usable, -lse[:, low], -1e30)
            shifts[at, 0, :, high] = jnp.broadcast_to(-lse[:, high], (8, LANES))
            shifts[at, 1, :, low] = jnp.where(usable, -lse[:, high], -1e30)
    acc[...] = jnp.zeros_like(acc)
    crossed[...] = jnp.zeros_like(crossed)

    @pl.loop(0, window)
    def _(block):
        k_turn[block] = kv_win[block, :, low].T

    unorder = reorder_matrix(True)
    lane = lax.broadcasted_iota(jnp.int32, (HALF, LANES), 1)
    head_a = lane < HALF

    def picks(query_block):
        return [kb_ref[base + query_block, s] - base + SPAN for s in range(slot_count)]

    def lay_out(member, local, buf):
        at = pl.multiple_of(local * BLOCK, BLOCK)
        for part in range(2):
            rows_at = pl.ds(at + part * HALF, HALF)
            for cols, target in ((low, queries), (high, grads)):
                tile = qo_ref[member, rows_at, cols]
                zero = jnp.zeros_like(tile)
                both = jnp.concatenate(
                    [jnp.where(head_a, tile, zero), jnp.where(head_a, zero, tile)], axis=0
                )
                target[buf, part * BLOCK : (part + 1) * BLOCK] = both
                if part == 1:
                    side = 0 if target is queries else 1
                    crossed[
                        buf, side * BLOCK : (side + 1) * BLOCK, side * LANES : (side + 1) * LANES
                    ] = both

    def gather(index, rows_of, cols):
        return jnp.concatenate([kv_win[i, rows_of, cols] for i in index], axis=0)

    early = slice(0, HALF)
    late = slice(HALF, BLOCK)
    both_cols = slice(0, 2 * LANES)
    early_rows = slot_count * HALF

    def forward(query_block, buf):
        lay_out(query_block // blocks_here, query_block % blocks_here, buf)
        index = picks(query_block)
        s = dot_nt(gather(index, early, low), queries[buf])
        g = dot_nt(gather(index, early, high), grads[buf])
        x = dot_nt(gather(index, late, both_cols), crossed[buf])
        shift = shifts[query_block, 0][None]
        p = jnp.exp(s.reshape(early_rows // 8, 8, 2 * LANES) + shift).reshape(early_rows, 2 * LANES)
        prob[buf, :early_rows] = p
        slope[buf, :early_rows] = g
        delta = jnp.sum((p * g).reshape(early_rows // 8, 8, 2 * LANES), axis=0)
        late_shift = shifts[query_block, 1, :, low][None]
        q = jnp.exp(x[:, low].reshape(early_rows // 8, 8, LANES) + late_shift).reshape(
            early_rows, LANES
        )
        prob[buf, early_rows:, low] = q
        slope[buf, early_rows:, low] = x[:, high]
        more = jnp.sum((q * x[:, high]).reshape(early_rows // 8, 8, LANES), axis=0)
        delta_low = jnp.sum(delta[:, low], axis=0, keepdims=True)
        delta_high = jnp.sum(delta[:, high] + more, axis=0, keepdims=True)
        return jnp.concatenate([delta_low, delta_high], axis=1)

    def backward(query_block, buf, delta):
        index = picks(query_block)
        p = prob[buf, :early_rows]
        ds = (p * (slope[buf, :early_rows] - delta)).astype(BF16)
        q = prob[buf, early_rows:, low]
        ds_late = (q * (slope[buf, early_rows:, low] - delta[:, high])).astype(BF16)
        dk = dot(ds, queries[buf])
        dv = dot(p.astype(BF16), grads[buf])
        r = dot(jnp.concatenate([ds_late, q.astype(BF16)], axis=1), crossed[buf])
        nothing = jnp.zeros((HALF, LANES), BF16)
        pieces = []
        for s in range(slot_count):
            at = slice(s * HALF, (s + 1) * HALF)
            where = index[s]
            acc[where, early, low] = acc[where, early, low] + dk[at]
            acc[where, early, high] = acc[where, early, high] + dv[at]
            acc[where, late] = acc[where, late] + r[at]
            pieces.append(ds[at])
            pieces.append(jnp.concatenate([nothing, ds_late[at]], axis=1))
        keys_turned = jnp.concatenate([k_turn[i] for i in index], axis=1)
        dq = dot(keys_turned, jnp.concatenate(pieces, axis=0)) * scale
        halves = []
        for cols in (low, high):
            turned = dq[:, cols].T
            halves.append(jnp.where(head_a, turned[:HALF], turned[HALF:]))
        moved = dot(unorder, jnp.concatenate(halves, axis=0).astype(BF16)).astype(BF16)
        local = pl.multiple_of((query_block % blocks_here) * BLOCK, BLOCK)
        dq_all[query_block // blocks_here, pl.ds(local, BLOCK)] = moved

    delta = forward(0, 0)

    def step(j, delta):
        block = 2 * j
        later = forward(block + 1, 1)
        backward(block, 0, delta)
        last = forward(block + 2, 0)
        backward(block + 1, 1, later)
        return last

    delta = lax.fori_loop(0, (group_blocks - 1) // 2, step, delta)
    if group_blocks % 2 == 0:
        later = forward(group_blocks - 1, 1)
        backward(group_blocks - 2, 0, delta)
        backward(group_blocks - 1, 1, later)
    else:
        backward(group_blocks - 1, 0, delta)

    groups = BLOCK // 16
    for cols, (own_out, first_out, second_out) in ((low, key_outs), (high, value_outs)):
        for out, start, count in (
            (first_out, first_at, SPAN),
            (second_out, second_at, SPAN),
            (own_out, SPAN, group_blocks),
        ):
            part = acc[pl.ds(start, count), :, cols].reshape(count, 2, groups, 8, LANES)
            out[...] = jnp.swapaxes(part, 1, 2).reshape(count, BLOCK, LANES).astype(out.dtype)
    send_pieces(dq_outs, dq_all)


def owner_start(piece, half):
    heads = lax.axis_size("head")
    return pl.multiple_of(((lax.axis_index("head") + 1 + piece) % heads) * half, half)


def add_parts(own_ref, first_ref, second_ref, total, moved):
    group_blocks = own_ref.shape[0]
    first, second = exchange_start(group_blocks)
    total[...] = own_ref[...]
    for start, ref in ((first, first_ref), (second, second_ref)):
        at = pl.ds(start, SPAN)
        total[at] = total[at] + ref[...].astype(F32)
    moved[...] = total[...].astype(BF16).reshape(moved.shape)


def combine_kernel(own_ref, first_ref, second_ref, *rest):
    outs, (total, moved) = rest[:GROUP], rest[GROUP:]
    add_parts(own_ref, first_ref, second_ref, total, moved)
    send_pieces(outs, moved)


def combine_split_kernel(own_ref, first_ref, second_ref, *rest):
    aways, homes, (total, moved) = rest[:GROUP], rest[GROUP : 2 * GROUP], rest[2 * GROUP :]
    add_parts(own_ref, first_ref, second_ref, total, moved)
    half = homes[0].shape[0]
    away = aways[0].shape[0] // half
    me = lax.axis_index("var") % GROUP
    for distance in range(GROUP):
        member = me ^ distance
        for piece in range(away):
            aways[distance][piece * half : (piece + 1) * half] = moved[
                member, pl.ds(owner_start(piece, half), half)
            ]
        homes[distance][...] = moved[member, pl.ds(owner_start(away, half), half)]


def gather_rows(grads, stages, start, dv_stage, dv_at):
    half = grads.shape[1]
    width = grads.shape[2] // GROUP
    for member in range(GROUP):
        at = slice(member * width, (member + 1) * width)
        for s, stage in enumerate(stages):
            grads[s, :, at] = stage[member, pl.ds(start, half)][:, :width]
        grads[2, :, at] = dv_stage[member, dv_at * half : (dv_at + 1) * half][:, :width]


def product(grads, w_ref):
    total = dot_nt(grads[0], w_ref[0])
    for s in (1, 2):
        total = total + dot_nt(grads[s], w_ref[s])
    return total


def away_kernel(*refs):
    dqs, dks, dvs, (w_ref, *rest) = refs[:4], refs[4:8], refs[8:12], refs[12:]
    outs, (grads, dq, dk, dv) = rest[:-4], rest[-4:]
    half = grads.shape[1]
    stage_pieces(dq, dqs)
    stage_pieces(dk, dks)
    stage_pieces(dv, dvs)
    for piece, out in enumerate(outs):
        gather_rows(grads, (dq, dk), owner_start(piece, half), dv, piece)
        out[...] = product(grads, w_ref).astype(BF16)


def home_kernel(*refs):
    dqs, dks, aways, homes, rest = refs[:4], refs[4:8], refs[8:12], refs[12:16], refs[16:]
    w_ref, dq_out, dk_out, dv_out, keep_out, grads, dq, dk, away_dv, home_dv = rest
    half = grads.shape[1]
    away = away_dv.shape[1] // half
    stage_pieces(dq, dqs)
    stage_pieces(dk, dks)
    stage_pieces(away_dv, aways)
    stage_pieces(home_dv, homes)
    for piece in range(away + 1):
        start = owner_start(piece, half)
        if piece < away:
            gather_rows(grads, (dq, dk), start, away_dv, piece)
        else:
            gather_rows(grads, (dq, dk), start, home_dv, 0)
        at = pl.ds(start, half)
        dq_out[at] = grads[0]
        dk_out[at] = grads[1]
        dv_out[at] = grads[2]
    keep_out[...] = product(grads, w_ref)


def body(queries, keys, values, out_grad, log_sum_exp, key_blocks, w_qkv):
    rows, features = queries.shape
    head_count = log_sum_exp.shape[0]
    head_dim = features // head_count
    slots = head_count // GROUP
    blocks_here = rows // BLOCK
    group_blocks = GROUP * blocks_here
    window = group_blocks + 2 * SPAN
    slot_count = key_blocks.shape[1]
    devices = lax.axis_size("var")
    heads = lax.axis_size("head")
    half = rows // heads
    model = w_qkv.shape[1]
    wide = 2 * LANES
    hbm = pl.BlockSpec(memory_space=pltpu.HBM)

    def trade(x, distance):
        return lax.ppermute(x, "var", [(n, n ^ distance) for n in range(devices)])

    def trade_first(x):
        pairs = [(n, n ^ GROUP) for n in range(devices) if (n ^ GROUP) < devices]
        return lax.ppermute(x, "var", pairs)

    def trade_second(x):
        pairs = []
        for n in range(devices):
            other = n + GROUP if (n // GROUP) % 2 else n - GROUP
            if 0 <= other < devices:
                pairs.append((n, other))
        return lax.ppermute(x, "var", pairs)

    def swap(pieces):
        got = [pieces[0]] + [None] * (GROUP - 1)
        for distance in (2, 3, 1):
            got[distance] = trade(pieces[distance], distance)
        return got

    def staged(count, width=LANES):
        return pltpu.VMEM((GROUP, count, width), BF16)

    loaded = pltpu.VMEM((rows, features), BF16)
    block = (BLOCK, LANES)

    def pack(x):
        return pl.pallas_call(
            pack_kernel,
            out_shape=(shaped((rows, LANES)),) * GROUP,
            in_specs=[hbm],
            out_specs=(vmem(),) * GROUP,
            scratch_shapes=[loaded, staged(rows), pltpu.SemaphoreType.DMA((1, LOADS))],
            compiler_params=params(8),
        )(x)

    def line_up(pieces):
        return pl.pallas_call(
            line_kernel,
            out_shape=(shaped((group_blocks,) + block),) + (shaped((SPAN,) + block),) * 2,
            in_specs=[vmem()] * GROUP,
            out_specs=(vmem(),) * 3,
            compiler_params=params(8),
        )(*pieces)

    key_pieces = swap(pack(keys))
    value_pieces = swap(pack(values))
    own_keys, first_keys, second_keys = line_up(key_pieces)
    first_keys = trade_first(first_keys)
    second_keys = trade_second(second_keys)
    own_values, first_values, second_values = line_up(value_pieces)
    first_values = trade_first(first_values)
    second_values = trade_second(second_values)
    qos = swap(
        pl.pallas_call(
            functools.partial(pack_qo_kernel, slots, head_dim),
            out_shape=(shaped((rows + LSE_ROWS, wide)),) * GROUP,
            in_specs=[hbm, hbm, vmem()],
            out_specs=(vmem(),) * GROUP,
            scratch_shapes=[
                loaded,
                loaded,
                staged(rows + LSE_ROWS, wide),
                pltpu.SemaphoreType.DMA((2, LOADS)),
            ],
            compiler_params=params(8),
        )(queries, out_grad, log_sum_exp)
    )

    pairs = group_blocks * slot_count * BLOCK * BLOCK * slots
    sums = (shaped((group_blocks,) + block, F32),) + (shaped((SPAN,) + block),) * 2
    results = pl.pallas_call(
        functools.partial(attend_kernel, blocks_here, head_dim),
        out_shape=sums + sums + (shaped((rows, LANES)),) * GROUP,
        in_specs=[pl.BlockSpec(memory_space=pltpu.SMEM)] + [vmem()] * (6 + GROUP),
        out_specs=(vmem(),) * (6 + GROUP),
        scratch_shapes=[
            pltpu.VMEM((window, BLOCK, wide), BF16),
            pltpu.VMEM((window, LANES, BLOCK), BF16),
            pltpu.VMEM((window, BLOCK, wide), F32),
            pltpu.VMEM((group_blocks, 2, 8, wide), F32),
            pltpu.VMEM((2, wide, LANES), BF16),
            pltpu.VMEM((2, wide, LANES), BF16),
            pltpu.VMEM((2, wide, wide), BF16),
            pltpu.VMEM((2, slot_count * BLOCK, wide), F32),
            pltpu.VMEM((2, slot_count * BLOCK, wide), F32),
            staged(rows + LSE_ROWS, wide),
            staged(rows),
        ],
        compiler_params=params(24),
        cost_estimate=pl.CostEstimate(
            flops=40 * pairs * head_dim, bytes_accessed=2_000_000, transcendentals=pairs
        ),
    )(
        key_blocks,
        own_keys,
        first_keys,
        second_keys,
        own_values,
        first_values,
        second_values,
        *qos,
    )
    key_sum, first_part, second_part = results[:3]
    first_back = trade_first(first_part)
    second_back = trade_second(second_part)
    value_sum, first_part, second_part = results[3:6]
    first_value_back = trade_first(first_part)
    second_value_back = trade_second(second_part)
    dqs = swap(results[6:])
    summing = [pltpu.VMEM((group_blocks,) + block, F32), staged(rows)]
    dks = swap(
        pl.pallas_call(
            combine_kernel,
            out_shape=(shaped((rows, LANES)),) * GROUP,
            in_specs=[vmem()] * 3,
            out_specs=(vmem(),) * GROUP,
            scratch_shapes=summing,
            compiler_params=params(8),
        )(key_sum, first_back, second_back)
    )
    split = pl.pallas_call(
        combine_split_kernel,
        out_shape=(shaped((rows - half, LANES)),) * GROUP + (shaped((half, LANES)),) * GROUP,
        in_specs=[vmem()] * 3,
        out_specs=(vmem(),) * (2 * GROUP),
        scratch_shapes=summing,
        compiler_params=params(8),
    )(value_sum, first_value_back, second_value_back)
    aways = swap(split[:GROUP])
    homes = swap(split[GROUP:])

    grads = pltpu.VMEM((3, half, features), BF16)
    sends = pl.pallas_call(
        away_kernel,
        out_shape=(shaped((half, model)),) * (heads - 1),
        in_specs=[vmem()] * (3 * GROUP + 1),
        out_specs=(vmem(),) * (heads - 1),
        scratch_shapes=[grads, staged(rows), staged(rows), staged(rows - half)],
        compiler_params=params(12),
        cost_estimate=pl.CostEstimate(
            flops=6 * (rows - half) * features * model, bytes_accessed=4_000_000, transcendentals=0
        ),
    )(*dqs, *dks, *aways, w_qkv)
    dq_out, dk_out, dv_out, total = pl.pallas_call(
        home_kernel,
        out_shape=(shaped((rows, features)),) * 3 + (shaped((half, model), F32),),
        in_specs=[vmem()] * (4 * GROUP + 1),
        out_specs=(vmem(),) * 4,
        scratch_shapes=[grads, staged(rows), staged(rows), staged(rows - half), staged(half)],
        compiler_params=params(12),
        cost_estimate=pl.CostEstimate(
            flops=6 * half * features * model, bytes_accessed=6_000_000, transcendentals=0
        ),
    )(*dqs, *dks, *aways, *homes, w_qkv)
    for piece, send in enumerate(sends):
        got = lax.ppermute(send, "head", [(n, (n + piece + 1) % heads) for n in range(heads)])
        total = total + got.astype(F32)
    return dq_out, dk_out, dv_out, total.astype(BF16)


def solution(mesh):
    in_specs = (
        P("var", "head"),
        P("var", "head"),
        P("var", "head"),
        P("var", "head"),
        P("head", "var"),
        P(),
        P(None, None, "head"),
    )
    out_specs = (P("var", "head"), P("var", "head"), P("var", "head"), P(("var", "head"), None))
    return jax.shard_map(body, mesh=mesh, in_specs=in_specs, out_specs=out_specs, check_vma=False)
```

```python
import functools

import jax
import jax.numpy as jnp
from jax import lax
from jax.experimental import pallas as pl
from jax.experimental.pallas import tpu as pltpu
from jax.sharding import PartitionSpec as P

PATCHES = 16
BLOCK = 128
HALF = BLOCK // 2
SPAN = 8
GROUP = 4
LANES = 128
LSE_ROWS = 16
LOADS = 3
F32 = jnp.float32
BF16 = jnp.bfloat16
MIB = 1024 * 1024
PACK_MIB = 62


def vmem():
    return pl.BlockSpec(memory_space=pltpu.VMEM)


def params(mib):
    return pltpu.CompilerParams(vmem_limit_bytes=mib * MIB)


def shaped(shape, dtype=BF16):
    return jax.ShapeDtypeStruct(shape, dtype)


def dot(a, b):
    return jnp.dot(a, b, preferred_element_type=F32)


def dot_nt(a, b):
    return lax.dot_general(a, b, (((1,), (1,)), ((), ())), preferred_element_type=F32)


def token_at(place):
    return (((place & (HALF - 1)) >> 3) << 4) + ((place >> 6) << 3) + (place & 7)


def one_where(mask):
    return jnp.where(mask, 1.0, 0.0).astype(BF16)


def reorder_matrix(inverse):
    row = lax.broadcasted_iota(jnp.int32, (BLOCK, BLOCK), 0)
    col = lax.broadcasted_iota(jnp.int32, (BLOCK, BLOCK), 1)
    return one_where(row == token_at(col)) if inverse else one_where(col == token_at(row))


def split_three(x):
    high = x.astype(BF16).astype(F32)
    rest = x - high
    mid = rest.astype(BF16).astype(F32)
    return high, mid, rest - mid


def widen(x):
    if x.shape[1] == LANES:
        return x
    return jnp.concatenate([x, jnp.zeros((x.shape[0], LANES - x.shape[1]), x.dtype)], axis=1)


def send_pieces(outs, stage):
    me = lax.axis_index("var") % GROUP
    for distance, out in enumerate(outs):
        out[...] = stage[me ^ distance]


def stage_pieces(stage, pieces):
    me = lax.axis_index("var") % GROUP
    for distance, piece in enumerate(pieces):
        stage[me ^ distance] = piece[...]


def load_all(pairs, sems):
    copies = []
    for i, (source, target) in enumerate(pairs):
        rows = source.shape[0] // LOADS
        for part in range(LOADS):
            at = pl.ds(part * rows, rows)
            copies.append(pltpu.make_async_copy(source.at[at], target.at[at], sems.at[i, part]))
    for copy in copies:
        copy.start()
    return [copies[i * LOADS : (i + 1) * LOADS] for i in range(len(pairs))]


def reorder_into(staged, half, ref, scale=None):
    rows, features = ref.shape
    width = features // GROUP
    order = reorder_matrix(False)
    for b in range(rows // BLOCK):
        at = slice(b * BLOCK, (b + 1) * BLOCK)
        moved = dot(order, ref[at])
        if scale is not None:
            moved = moved * scale
        moved = moved.astype(BF16)
        for member in range(GROUP):
            staged[member, at, half * LANES : (half + 1) * LANES] = widen(
                moved[:, member * width : (member + 1) * width]
            )


def pack_kv_kernel(k_hbm, v_hbm, *rest):
    outs, (k_ref, v_ref, turned, sems) = rest[:GROUP], rest[GROUP:]
    arrivals = load_all([(k_hbm, k_ref), (v_hbm, v_ref)], sems)
    for half, ref in enumerate((k_ref, v_ref)):
        for copy in arrivals[half]:
            copy.wait()
        reorder_into(turned, half, ref)
    send_pieces(outs, turned)


def pack_qo_kernel(slots, head_dim, q_ref, g_ref, lse_ref, after_ref, *rest):
    outs, qo_ref = rest[:GROUP], rest[GROUP]
    rows = q_ref.shape[0]
    blocks = rows // BLOCK
    reorder_into(qo_ref, 0, q_ref, head_dim ** (-0.5))
    reorder_into(qo_ref, 1, g_ref)
    token = lax.broadcasted_iota(jnp.int32, (BLOCK, 2 * LANES), 0)
    lane = lax.broadcasted_iota(jnp.int32, (BLOCK, 2 * LANES), 1)
    place = ((lane >> 7) << 6) + (lane & (HALF - 1))
    hit = token == token_at(place)
    upper = (lane & HALF) != 0
    spread = [one_where(hit & ~upper), one_where(hit & upper)]
    for member in range(GROUP):
        total = None
        for slot in range(slots):
            lse = lse_ref[member * slots + slot : member * slots + slot + 1, :]
            parts = [
                part[:, b * BLOCK : (b + 1) * BLOCK]
                for part in split_three(lse)
                for b in range(blocks)
            ]
            parts.append(jnp.zeros((LSE_ROWS - len(parts), BLOCK), F32))
            moved = dot(jnp.concatenate(parts, axis=0).astype(BF16), spread[slot])
            total = moved if total is None else total + moved
        qo_ref[member, rows:] = total.astype(BF16)
    send_pieces(outs, qo_ref)


def below_first():
    me = lax.axis_index("var")
    return (me // GROUP + me) % 2


def exchange_start(group_blocks):
    odd = below_first()
    reach = group_blocks - SPAN
    return (1 - odd) * reach, odd * reach


def line_kernel(carried, *refs):
    pieces, refs = refs[:GROUP], refs[GROUP + carried :]
    own, first_out, second_out = refs[:3]
    rows = pieces[0].shape[0]
    blocks = rows // BLOCK
    me = lax.axis_index("var") % GROUP
    for distance in range(GROUP):
        at = pl.ds(pl.multiple_of((me ^ distance) * rows, rows), rows)
        own[at] = pieces[distance][...]
    first, second = exchange_start(GROUP * blocks)
    for start, out in ((first, first_out), (second, second_out)):
        out[...] = own[pl.ds(pl.multiple_of(start * BLOCK, BLOCK), SPAN * BLOCK)]


def attend_kernel(
    blocks_here,
    head_dim,
    kb_ref,
    *refs,
):
    kv_refs, refs = refs[:3], refs[3:]
    qo_pieces, refs = refs[:GROUP], refs[GROUP:]
    key_outs, value_outs, refs = refs[:3], refs[3:6], refs[6:]
    dq_outs, refs = refs[:GROUP], refs[GROUP:]
    kv_win, k_turn, acc, shifts, queries, grads, crossed, prob, slope, qo_ref, dq_all = refs
    group_blocks = GROUP * blocks_here
    window = group_blocks + 2 * SPAN
    rows = blocks_here * BLOCK
    slot_count = kb_ref.shape[1]
    scale = head_dim ** (-0.5)
    base = (lax.axis_index("var") // GROUP) * group_blocks
    odd = below_first()
    top = window - SPAN
    first_at, second_at = (1 - odd) * top, odd * top
    low = slice(0, LANES)
    high = slice(LANES, 2 * LANES)

    for ref, start, count in zip(
        kv_refs, (SPAN, first_at, second_at), (group_blocks, SPAN, SPAN)
    ):
        kv_win[pl.ds(start, count)] = ref[...].reshape(count, BLOCK, 2 * LANES)
    stage_pieces(qo_ref, qo_pieces)
    key_patch = lax.broadcasted_iota(jnp.int32, (8, LANES), 0)
    query_patch = lax.broadcasted_iota(jnp.int32, (8, LANES), 1) & 7
    usable = key_patch <= query_patch
    for member in range(GROUP):
        parts = qo_ref[member, rows:].astype(F32)
        for local in range(blocks_here):
            lse = (
                parts[local : local + 1] + parts[blocks_here + local : blocks_here + local + 1]
            ) + parts[2 * blocks_here + local : 2 * blocks_here + local + 1]
            at = member * blocks_here + local
            shifts[at, 0, :, low] = jnp.where(usable, -lse[:, low], -1e30)
            shifts[at, 0, :, high] = jnp.broadcast_to(-lse[:, high], (8, LANES))
            shifts[at, 1, :, low] = jnp.where(usable, -lse[:, high], -1e30)
    acc[...] = jnp.zeros_like(acc)
    crossed[...] = jnp.zeros_like(crossed)

    @pl.loop(0, window)
    def _(block):
        k_turn[block] = kv_win[block, :, low].T

    unorder = reorder_matrix(True)
    lane = lax.broadcasted_iota(jnp.int32, (HALF, LANES), 1)
    head_a = lane < HALF

    def picks(query_block):
        return [kb_ref[base + query_block, s] - base + SPAN for s in range(slot_count)]

    def lay_out(member, local, buf):
        at = pl.multiple_of(local * BLOCK, BLOCK)
        for part in range(2):
            rows_at = pl.ds(at + part * HALF, HALF)
            for cols, target in ((low, queries), (high, grads)):
                tile = qo_ref[member, rows_at, cols]
                zero = jnp.zeros_like(tile)
                both = jnp.concatenate(
                    [jnp.where(head_a, tile, zero), jnp.where(head_a, zero, tile)], axis=0
                )
                target[buf, part * BLOCK : (part + 1) * BLOCK] = both
                if part == 1:
                    side = 0 if target is queries else 1
                    crossed[
                        buf, side * BLOCK : (side + 1) * BLOCK, side * LANES : (side + 1) * LANES
                    ] = both

    def gather(index, rows_of, cols):
        return jnp.concatenate([kv_win[i, rows_of, cols] for i in index], axis=0)

    early = slice(0, HALF)
    late = slice(HALF, BLOCK)
    both_cols = slice(0, 2 * LANES)
    early_rows = slot_count * HALF

    def forward(query_block, buf):
        lay_out(query_block // blocks_here, query_block % blocks_here, buf)
        index = picks(query_block)
        s = dot_nt(gather(index, early, low), queries[buf])
        g = dot_nt(gather(index, early, high), grads[buf])
        x = dot_nt(gather(index, late, both_cols), crossed[buf])
        shift = shifts[query_block, 0][None]
        p = jnp.exp(s.reshape(early_rows // 8, 8, 2 * LANES) + shift).reshape(early_rows, 2 * LANES)
        prob[buf, :early_rows] = p
        slope[buf, :early_rows] = g
        delta = jnp.sum((p * g).reshape(early_rows // 8, 8, 2 * LANES), axis=0)
        late_shift = shifts[query_block, 1, :, low][None]
        q = jnp.exp(x[:, low].reshape(early_rows // 8, 8, LANES) + late_shift).reshape(
            early_rows, LANES
        )
        prob[buf, early_rows:, low] = q
        slope[buf, early_rows:, low] = x[:, high]
        more = jnp.sum((q * x[:, high]).reshape(early_rows // 8, 8, LANES), axis=0)
        delta_low = jnp.sum(delta[:, low], axis=0, keepdims=True)
        delta_high = jnp.sum(delta[:, high] + more, axis=0, keepdims=True)
        return jnp.concatenate([delta_low, delta_high], axis=1)

    def backward(query_block, buf, delta):
        index = picks(query_block)
        p = prob[buf, :early_rows]
        ds = (p * (slope[buf, :early_rows] - delta)).astype(BF16)
        q = prob[buf, early_rows:, low]
        ds_late = (q * (slope[buf, early_rows:, low] - delta[:, high])).astype(BF16)
        dk = dot(ds, queries[buf])
        dv = dot(p.astype(BF16), grads[buf])
        r = dot(jnp.concatenate([ds_late, q.astype(BF16)], axis=1), crossed[buf])
        nothing = jnp.zeros((HALF, LANES), BF16)
        pieces = []
        for s in range(slot_count):
            at = slice(s * HALF, (s + 1) * HALF)
            where = index[s]
            acc[where, early, low] = acc[where, early, low] + dk[at]
            acc[where, early, high] = acc[where, early, high] + dv[at]
            acc[where, late] = acc[where, late] + r[at]
            pieces.append(ds[at])
            pieces.append(jnp.concatenate([nothing, ds_late[at]], axis=1))
        keys_turned = jnp.concatenate([k_turn[i] for i in index], axis=1)
        dq = dot(keys_turned, jnp.concatenate(pieces, axis=0)) * scale
        halves = []
        for cols in (low, high):
            turned = dq[:, cols].T
            halves.append(jnp.where(head_a, turned[:HALF], turned[HALF:]))
        moved = dot(unorder, jnp.concatenate(halves, axis=0).astype(BF16)).astype(BF16)
        local = pl.multiple_of((query_block % blocks_here) * BLOCK, BLOCK)
        dq_all[query_block // blocks_here, pl.ds(local, BLOCK)] = moved

    delta = forward(0, 0)

    def step(j, delta):
        block = 2 * j
        later = forward(block + 1, 1)
        backward(block, 0, delta)
        last = forward(block + 2, 0)
        backward(block + 1, 1, later)
        return last

    delta = lax.fori_loop(0, (group_blocks - 1) // 2, step, delta)
    if group_blocks % 2 == 0:
        later = forward(group_blocks - 1, 1)
        backward(group_blocks - 2, 0, delta)
        backward(group_blocks - 1, 1, later)
    else:
        backward(group_blocks - 1, 0, delta)

    groups = BLOCK // 16
    for cols, (own_out, first_out, second_out) in ((low, key_outs), (high, value_outs)):
        for out, start, count in (
            (first_out, first_at, SPAN),
            (second_out, second_at, SPAN),
            (own_out, SPAN, group_blocks),
        ):
            part = acc[pl.ds(start, count), :, cols].reshape(count, 2, groups, 8, LANES)
            out[...] = jnp.swapaxes(part, 1, 2).reshape(count, BLOCK, LANES).astype(out.dtype)
    send_pieces(dq_outs, dq_all)


def owner_start(piece, half):
    heads = lax.axis_size("head")
    return pl.multiple_of(((lax.axis_index("head") + 1 + piece) % heads) * half, half)


def add_parts(own_ref, first_ref, second_ref, total, moved):
    group_blocks = own_ref.shape[0]
    first, second = exchange_start(group_blocks)
    total[...] = own_ref[...]
    for start, ref in ((first, first_ref), (second, second_ref)):
        at = pl.ds(start, SPAN)
        total[at] = total[at] + ref[...].astype(F32)
    moved[...] = total[...].astype(BF16).reshape(moved.shape)


def combine_kernel(own_ref, first_ref, second_ref, *rest):
    outs, (total, moved) = rest[:GROUP], rest[GROUP:]
    add_parts(own_ref, first_ref, second_ref, total, moved)
    send_pieces(outs, moved)


def combine_split_kernel(own_ref, first_ref, second_ref, *rest):
    aways, homes, (total, moved) = rest[:GROUP], rest[GROUP : 2 * GROUP], rest[2 * GROUP :]
    add_parts(own_ref, first_ref, second_ref, total, moved)
    half = homes[0].shape[0]
    away = aways[0].shape[0] // half
    me = lax.axis_index("var") % GROUP
    for distance in range(GROUP):
        member = me ^ distance
        for piece in range(away):
            aways[distance][piece * half : (piece + 1) * half] = moved[
                member, pl.ds(owner_start(piece, half), half)
            ]
        homes[distance][...] = moved[member, pl.ds(owner_start(away, half), half)]


def gather_rows(grads, stages, start, dv_stage, dv_at):
    half = grads.shape[1]
    width = grads.shape[2] // GROUP
    for member in range(GROUP):
        at = slice(member * width, (member + 1) * width)
        for s, stage in enumerate(stages):
            grads[s, :, at] = stage[member, pl.ds(start, half)][:, :width]
        grads[2, :, at] = dv_stage[member, dv_at * half : (dv_at + 1) * half][:, :width]


def product(grads, w_ref):
    total = dot_nt(grads[0], w_ref[0])
    for s in (1, 2):
        total = total + dot_nt(grads[s], w_ref[s])
    return total


def away_kernel(*refs):
    dqs, dks, dvs, (w_ref, *rest) = refs[:4], refs[4:8], refs[8:12], refs[12:]
    outs, (grads, dq, dk, dv) = rest[:-4], rest[-4:]
    half = grads.shape[1]
    stage_pieces(dq, dqs)
    stage_pieces(dk, dks)
    stage_pieces(dv, dvs)
    for piece, out in enumerate(outs):
        gather_rows(grads, (dq, dk), owner_start(piece, half), dv, piece)
        out[...] = product(grads, w_ref).astype(BF16)


def home_kernel(*refs):
    dqs, dks, aways, homes, rest = refs[:4], refs[4:8], refs[8:12], refs[12:16], refs[16:]
    w_ref, dq_out, dk_out, dv_out, keep_out, grads, dq, dk, away_dv, home_dv = rest
    half = grads.shape[1]
    away = away_dv.shape[1] // half
    stage_pieces(dq, dqs)
    stage_pieces(dk, dks)
    stage_pieces(away_dv, aways)
    stage_pieces(home_dv, homes)
    for piece in range(away + 1):
        start = owner_start(piece, half)
        if piece < away:
            gather_rows(grads, (dq, dk), start, away_dv, piece)
        else:
            gather_rows(grads, (dq, dk), start, home_dv, 0)
        at = pl.ds(start, half)
        dq_out[at] = grads[0]
        dk_out[at] = grads[1]
        dv_out[at] = grads[2]
    keep_out[...] = product(grads, w_ref)


def body(queries, keys, values, out_grad, log_sum_exp, key_blocks, w_qkv):
    rows, features = queries.shape
    head_count = log_sum_exp.shape[0]
    head_dim = features // head_count
    slots = head_count // GROUP
    blocks_here = rows // BLOCK
    group_blocks = GROUP * blocks_here
    window = group_blocks + 2 * SPAN
    slot_count = key_blocks.shape[1]
    devices = lax.axis_size("var")
    heads = lax.axis_size("head")
    half = rows // heads
    model = w_qkv.shape[1]
    wide = 2 * LANES
    hbm = pl.BlockSpec(memory_space=pltpu.HBM)

    def trade(x, distance):
        return lax.ppermute(x, "var", [(n, n ^ distance) for n in range(devices)])

    def trade_level(x, turn):
        pairs = []
        for n in range(devices):
            other = n - GROUP if (n // GROUP + n + turn) % 2 else n + GROUP
            if 0 <= other < devices:
                pairs.append((n, other))
        return lax.ppermute(x, "var", pairs)

    def trade_first(x):
        return trade_level(x, 0)

    def trade_second(x):
        return trade_level(x, 1)

    def swap(pieces):
        got = [pieces[0]] + [None] * (GROUP - 1)
        for distance in (2, 3, 1):
            got[distance] = trade(pieces[distance], distance)
        return got

    def staged(count, width=LANES):
        return pltpu.VMEM((GROUP, count, width), BF16)

    block = (BLOCK, LANES)
    anywhere = pl.BlockSpec(memory_space=pl.ANY)

    def cost(flops, moved):
        return pl.CostEstimate(flops=flops, bytes_accessed=moved, transcendentals=0)

    size = rows * features * 2

    kvs = pl.pallas_call(
        pack_kv_kernel,
        out_shape=(shaped((rows, wide)),) * GROUP,
        in_specs=[hbm] * 2,
        out_specs=(vmem(),) * GROUP,
        scratch_shapes=[pltpu.VMEM((rows, features), BF16)] * 2
        + [staged(rows, wide), pltpu.SemaphoreType.DMA((2, LOADS))],
        compiler_params=params(PACK_MIB),
        cost_estimate=cost(4 * rows * features * BLOCK, 5 * size),
    )(keys, values)
    kvs = swap(kvs)
    qos = pl.pallas_call(
        functools.partial(pack_qo_kernel, slots, head_dim),
        out_shape=(shaped((rows + LSE_ROWS, wide)),) * GROUP,
        in_specs=[vmem()] * 3 + [anywhere],
        out_specs=(vmem(),) * GROUP,
        scratch_shapes=[staged(rows + LSE_ROWS, wide)],
        compiler_params=params(8),
        cost_estimate=cost(4 * rows * features * BLOCK, 10 * size),
    )(queries, out_grad, log_sum_exp, kvs[1])
    carried = tuple(qos[1:])
    own, first, second, *carried = pl.pallas_call(
        functools.partial(line_kernel, len(carried)),
        out_shape=(shaped((GROUP * rows, wide)),)
        + (shaped((SPAN * BLOCK, wide)),) * 2
        + tuple(shaped(x.shape) for x in carried),
        in_specs=[vmem()] * GROUP + [anywhere] * len(carried),
        out_specs=(vmem(),) * 3 + (anywhere,) * len(carried),
        input_output_aliases={GROUP + i: 3 + i for i in range(len(carried))},
        compiler_params=params(8),
        cost_estimate=cost(0, 5 * size),
    )(*kvs, *carried)
    first = trade_first(first)
    second = trade_second(second)
    qos = swap([qos[0], *carried])

    pairs = group_blocks * slot_count * BLOCK * BLOCK * slots
    sums = (shaped((group_blocks,) + block, F32),) + (shaped((SPAN,) + block),) * 2
    results = pl.pallas_call(
        functools.partial(attend_kernel, blocks_here, head_dim),
        out_shape=sums + sums + (shaped((rows, LANES)),) * GROUP,
        in_specs=[pl.BlockSpec(memory_space=pltpu.SMEM)] + [vmem()] * (3 + GROUP),
        out_specs=(vmem(),) * (6 + GROUP),
        scratch_shapes=[
            pltpu.VMEM((window, BLOCK, wide), BF16),
            pltpu.VMEM((window, LANES, BLOCK), BF16),
            pltpu.VMEM((window, BLOCK, wide), F32),
            pltpu.VMEM((group_blocks, 2, 8, wide), F32),
            pltpu.VMEM((2, wide, LANES), BF16),
            pltpu.VMEM((2, wide, LANES), BF16),
            pltpu.VMEM((2, wide, wide), BF16),
            pltpu.VMEM((2, slot_count * BLOCK, wide), F32),
            pltpu.VMEM((2, slot_count * BLOCK, wide), F32),
            staged(rows + LSE_ROWS, wide),
            staged(rows),
        ],
        compiler_params=params(24),
        cost_estimate=pl.CostEstimate(
            flops=40 * pairs * head_dim, bytes_accessed=2_000_000, transcendentals=pairs
        ),
    )(
        key_blocks,
        own,
        first,
        second,
        *qos,
    )
    key_sum, first_part, second_part = results[:3]
    first_back = trade_first(first_part)
    second_back = trade_second(second_part)
    value_sum, first_part, second_part = results[3:6]
    first_value_back = trade_first(first_part)
    second_value_back = trade_second(second_part)
    dqs = swap(results[6:])
    summing = [pltpu.VMEM((group_blocks,) + block, F32), staged(rows)]
    dks = swap(
        pl.pallas_call(
            combine_kernel,
            out_shape=(shaped((rows, LANES)),) * GROUP,
            in_specs=[vmem()] * 3,
            out_specs=(vmem(),) * GROUP,
            scratch_shapes=summing,
            compiler_params=params(8),
            cost_estimate=cost(0, 4 * size),
        )(key_sum, first_back, second_back)
    )
    split = pl.pallas_call(
        combine_split_kernel,
        out_shape=(shaped((rows - half, LANES)),) * GROUP + (shaped((half, LANES)),) * GROUP,
        in_specs=[vmem()] * 3,
        out_specs=(vmem(),) * (2 * GROUP),
        scratch_shapes=summing,
        compiler_params=params(8),
        cost_estimate=cost(0, 4 * size),
    )(value_sum, first_value_back, second_value_back)
    aways = swap(split[:GROUP])
    homes = swap(split[GROUP:])

    grads = pltpu.VMEM((3, half, features), BF16)
    sends = pl.pallas_call(
        away_kernel,
        out_shape=(shaped((half, model)),) * (heads - 1),
        in_specs=[vmem()] * (3 * GROUP + 1),
        out_specs=(vmem(),) * (heads - 1),
        scratch_shapes=[grads, staged(rows), staged(rows), staged(rows - half)],
        compiler_params=params(12),
        cost_estimate=pl.CostEstimate(
            flops=6 * (rows - half) * features * model, bytes_accessed=4_000_000, transcendentals=0
        ),
    )(*dqs, *dks, *aways, w_qkv)
    dq_out, dk_out, dv_out, total = pl.pallas_call(
        home_kernel,
        out_shape=(shaped((rows, features)),) * 3 + (shaped((half, model), F32),),
        in_specs=[vmem()] * (4 * GROUP + 1),
        out_specs=(vmem(),) * 4,
        scratch_shapes=[grads, staged(rows), staged(rows), staged(rows - half), staged(half)],
        compiler_params=params(12),
        cost_estimate=pl.CostEstimate(
            flops=6 * half * features * model, bytes_accessed=6_000_000, transcendentals=0
        ),
    )(*dqs, *dks, *aways, *homes, w_qkv)
    for piece, send in enumerate(sends):
        got = lax.ppermute(send, "head", [(n, (n + piece + 1) % heads) for n in range(heads)])
        total = total + got.astype(F32)
    return dq_out, dk_out, dv_out, total.astype(BF16)


def solution(mesh):
    in_specs = (
        P("var", "head"),
        P("var", "head"),
        P("var", "head"),
        P("var", "head"),
        P("head", "var"),
        P(),
        P(None, None, "head"),
    )
    out_specs = (P("var", "head"), P("var", "head"), P("var", "head"), P(("var", "head"), None))
    return jax.shard_map(body, mesh=mesh, in_specs=in_specs, out_specs=out_specs, check_vma=False)
```

```python
import functools

import jax
import jax.numpy as jnp
from jax import lax
from jax.experimental import pallas as pl
from jax.experimental.pallas import tpu as pltpu
from jax.sharding import PartitionSpec as P

PATCHES = 16
BLOCK = 128
HALF = BLOCK // 2
SPAN = 8
GROUP = 4
LANES = 128
LSE_ROWS = 16
LOADS = 3
F32 = jnp.float32
BF16 = jnp.bfloat16
MIB = 1024 * 1024
PACK_MIB = 62


def vmem():
    return pl.BlockSpec(memory_space=pltpu.VMEM)


def params(mib):
    return pltpu.CompilerParams(vmem_limit_bytes=mib * MIB)


def shaped(shape, dtype=BF16):
    return jax.ShapeDtypeStruct(shape, dtype)


def dot(a, b):
    return jnp.dot(a, b, preferred_element_type=F32)


def dot_nt(a, b):
    return lax.dot_general(a, b, (((1,), (1,)), ((), ())), preferred_element_type=F32)


def token_at(place):
    return (((place & (HALF - 1)) >> 3) << 4) + ((place >> 6) << 3) + (place & 7)


def one_where(mask):
    return jnp.where(mask, 1.0, 0.0).astype(BF16)


def reorder_matrix(inverse):
    row = lax.broadcasted_iota(jnp.int32, (BLOCK, BLOCK), 0)
    col = lax.broadcasted_iota(jnp.int32, (BLOCK, BLOCK), 1)
    return one_where(row == token_at(col)) if inverse else one_where(col == token_at(row))


def split_three(x):
    high = x.astype(BF16).astype(F32)
    rest = x - high
    mid = rest.astype(BF16).astype(F32)
    return high, mid, rest - mid


def widen(x):
    if x.shape[1] == LANES:
        return x
    return jnp.concatenate([x, jnp.zeros((x.shape[0], LANES - x.shape[1]), x.dtype)], axis=1)


def send_pieces(outs, stage):
    me = lax.axis_index("var") % GROUP
    for distance, out in enumerate(outs):
        out[...] = stage[me ^ distance]


def stage_pieces(stage, pieces):
    me = lax.axis_index("var") % GROUP
    for distance, piece in enumerate(pieces):
        stage[me ^ distance] = piece[...]


def load_all(pairs, sems):
    copies = []
    for i, (source, target) in enumerate(pairs):
        rows = source.shape[0] // LOADS
        for part in range(LOADS):
            at = pl.ds(part * rows, rows)
            copies.append(pltpu.make_async_copy(source.at[at], target.at[at], sems.at[i, part]))
    for copy in copies:
        copy.start()
    return [copies[i * LOADS : (i + 1) * LOADS] for i in range(len(pairs))]


def reorder_into(staged, half, ref, scale=None):
    rows, features = ref.shape
    width = features // GROUP
    order = reorder_matrix(False)
    for b in range(rows // BLOCK):
        at = slice(b * BLOCK, (b + 1) * BLOCK)
        moved = dot(order, ref[at])
        if scale is not None:
            moved = moved * scale
        moved = moved.astype(BF16)
        for member in range(GROUP):
            staged[member, at, half * LANES : (half + 1) * LANES] = widen(
                moved[:, member * width : (member + 1) * width]
            )


def pack_kv_kernel(k_hbm, v_hbm, *rest):
    outs, (k_ref, v_ref, turned, sems) = rest[:GROUP], rest[GROUP:]
    arrivals = load_all([(k_hbm, k_ref), (v_hbm, v_ref)], sems)
    for half, ref in enumerate((k_ref, v_ref)):
        for copy in arrivals[half]:
            copy.wait()
        reorder_into(turned, half, ref)
    send_pieces(outs, turned)


def pack_qo_kernel(slots, head_dim, q_ref, g_ref, lse_ref, mine_ref, after_ref, *rest):
    outs, (hold, qo_ref) = rest[:GROUP], rest[GROUP:]
    hold[...] = mine_ref[...]
    rows = q_ref.shape[0]
    blocks = rows // BLOCK
    reorder_into(qo_ref, 0, q_ref, head_dim ** (-0.5))
    reorder_into(qo_ref, 1, g_ref)
    token = lax.broadcasted_iota(jnp.int32, (BLOCK, 2 * LANES), 0)
    lane = lax.broadcasted_iota(jnp.int32, (BLOCK, 2 * LANES), 1)
    place = ((lane >> 7) << 6) + (lane & (HALF - 1))
    hit = token == token_at(place)
    upper = (lane & HALF) != 0
    spread = [one_where(hit & ~upper), one_where(hit & upper)]
    for member in range(GROUP):
        total = None
        for slot in range(slots):
            lse = lse_ref[member * slots + slot : member * slots + slot + 1, :]
            parts = [
                part[:, b * BLOCK : (b + 1) * BLOCK]
                for part in split_three(lse)
                for b in range(blocks)
            ]
            parts.append(jnp.zeros((LSE_ROWS - len(parts), BLOCK), F32))
            moved = dot(jnp.concatenate(parts, axis=0).astype(BF16), spread[slot])
            total = moved if total is None else total + moved
        qo_ref[member, rows:] = total.astype(BF16)
    send_pieces(outs, qo_ref)


def below_first():
    me = lax.axis_index("var")
    return (me // GROUP + me) % 2


def exchange_start(group_blocks):
    odd = below_first()
    reach = group_blocks - SPAN
    return (1 - odd) * reach, odd * reach


def line_kernel(carried, *refs):
    pieces, query_piece, refs = refs[:GROUP], refs[GROUP], refs[GROUP + 1 + carried :]
    own, first_out, second_out = refs[:3]
    rows = pieces[0].shape[0]
    own[GROUP * rows :] = query_piece[...]
    blocks = rows // BLOCK
    me = lax.axis_index("var") % GROUP
    for distance in range(GROUP):
        at = pl.ds(pl.multiple_of((me ^ distance) * rows, rows), rows)
        own[at] = pieces[distance][...]
    first, second = exchange_start(GROUP * blocks)
    for start, out in ((first, first_out), (second, second_out)):
        out[...] = own[pl.ds(pl.multiple_of(start * BLOCK, BLOCK), SPAN * BLOCK)]


def attend_kernel(
    blocks_here,
    head_dim,
    kb_ref,
    *refs,
):
    kv_refs, refs = refs[:3], refs[3:]
    qo_pieces, refs = refs[: GROUP - 1], refs[GROUP - 1 :]
    key_outs, value_outs, refs = refs[:3], refs[3:6], refs[6:]
    dq_outs, refs = refs[:GROUP], refs[GROUP:]
    kv_win, k_turn, acc, shifts, queries, grads, crossed, prob, slope, qo_ref, dq_all = refs
    group_blocks = GROUP * blocks_here
    window = group_blocks + 2 * SPAN
    rows = blocks_here * BLOCK
    slot_count = kb_ref.shape[1]
    scale = head_dim ** (-0.5)
    base = (lax.axis_index("var") // GROUP) * group_blocks
    odd = below_first()
    top = window - SPAN
    first_at, second_at = (1 - odd) * top, odd * top
    low = slice(0, LANES)
    high = slice(LANES, 2 * LANES)

    for ref, start, count in zip(
        kv_refs, (SPAN, first_at, second_at), (group_blocks, SPAN, SPAN)
    ):
        kv_win[pl.ds(start, count)] = ref[: count * BLOCK].reshape(count, BLOCK, 2 * LANES)
    own_queries = kv_refs[0].at[pl.ds(group_blocks * BLOCK, rows + LSE_ROWS)]
    stage_pieces(qo_ref, (own_queries, *qo_pieces))
    key_patch = lax.broadcasted_iota(jnp.int32, (8, LANES), 0)
    query_patch = lax.broadcasted_iota(jnp.int32, (8, LANES), 1) & 7
    usable = key_patch <= query_patch
    for member in range(GROUP):
        parts = qo_ref[member, rows:].astype(F32)
        for local in range(blocks_here):
            lse = (
                parts[local : local + 1] + parts[blocks_here + local : blocks_here + local + 1]
            ) + parts[2 * blocks_here + local : 2 * blocks_here + local + 1]
            at = member * blocks_here + local
            shifts[at, 0, :, low] = jnp.where(usable, -lse[:, low], -1e30)
            shifts[at, 0, :, high] = jnp.broadcast_to(-lse[:, high], (8, LANES))
            shifts[at, 1, :, low] = jnp.where(usable, -lse[:, high], -1e30)
    acc[...] = jnp.zeros_like(acc)
    crossed[...] = jnp.zeros_like(crossed)

    @pl.loop(0, window)
    def _(block):
        k_turn[block] = kv_win[block, :, low].T

    unorder = reorder_matrix(True)
    lane = lax.broadcasted_iota(jnp.int32, (HALF, LANES), 1)
    head_a = lane < HALF

    def picks(query_block):
        return [kb_ref[base + query_block, s] - base + SPAN for s in range(slot_count)]

    def lay_out(member, local, buf):
        at = pl.multiple_of(local * BLOCK, BLOCK)
        for part in range(2):
            rows_at = pl.ds(at + part * HALF, HALF)
            for cols, target in ((low, queries), (high, grads)):
                tile = qo_ref[member, rows_at, cols]
                zero = jnp.zeros_like(tile)
                both = jnp.concatenate(
                    [jnp.where(head_a, tile, zero), jnp.where(head_a, zero, tile)], axis=0
                )
                target[buf, part * BLOCK : (part + 1) * BLOCK] = both
                if part == 1:
                    side = 0 if target is queries else 1
                    crossed[
                        buf, side * BLOCK : (side + 1) * BLOCK, side * LANES : (side + 1) * LANES
                    ] = both

    def gather(index, rows_of, cols):
        return jnp.concatenate([kv_win[i, rows_of, cols] for i in index], axis=0)

    early = slice(0, HALF)
    late = slice(HALF, BLOCK)
    both_cols = slice(0, 2 * LANES)
    early_rows = slot_count * HALF

    def forward(query_block, buf):
        lay_out(query_block // blocks_here, query_block % blocks_here, buf)
        index = picks(query_block)
        s = dot_nt(gather(index, early, low), queries[buf])
        g = dot_nt(gather(index, early, high), grads[buf])
        x = dot_nt(gather(index, late, both_cols), crossed[buf])
        shift = shifts[query_block, 0][None]
        p = jnp.exp(s.reshape(early_rows // 8, 8, 2 * LANES) + shift).reshape(early_rows, 2 * LANES)
        prob[buf, :early_rows] = p
        slope[buf, :early_rows] = g
        delta = jnp.sum((p * g).reshape(early_rows // 8, 8, 2 * LANES), axis=0)
        late_shift = shifts[query_block, 1, :, low][None]
        q = jnp.exp(x[:, low].reshape(early_rows // 8, 8, LANES) + late_shift).reshape(
            early_rows, LANES
        )
        prob[buf, early_rows:, low] = q
        slope[buf, early_rows:, low] = x[:, high]
        more = jnp.sum((q * x[:, high]).reshape(early_rows // 8, 8, LANES), axis=0)
        delta_low = jnp.sum(delta[:, low], axis=0, keepdims=True)
        delta_high = jnp.sum(delta[:, high] + more, axis=0, keepdims=True)
        return jnp.concatenate([delta_low, delta_high], axis=1)

    def backward(query_block, buf, delta):
        index = picks(query_block)
        p = prob[buf, :early_rows]
        ds = (p * (slope[buf, :early_rows] - delta)).astype(BF16)
        q = prob[buf, early_rows:, low]
        ds_late = (q * (slope[buf, early_rows:, low] - delta[:, high])).astype(BF16)
        dk = dot(ds, queries[buf])
        dv = dot(p.astype(BF16), grads[buf])
        r = dot(jnp.concatenate([ds_late, q.astype(BF16)], axis=1), crossed[buf])
        nothing = jnp.zeros((HALF, LANES), BF16)
        pieces = []
        for s in range(slot_count):
            at = slice(s * HALF, (s + 1) * HALF)
            where = index[s]
            acc[where, early, low] = acc[where, early, low] + dk[at]
            acc[where, early, high] = acc[where, early, high] + dv[at]
            acc[where, late] = acc[where, late] + r[at]
            pieces.append(ds[at])
            pieces.append(jnp.concatenate([nothing, ds_late[at]], axis=1))
        keys_turned = jnp.concatenate([k_turn[i] for i in index], axis=1)
        dq = dot(keys_turned, jnp.concatenate(pieces, axis=0)) * scale
        halves = []
        for cols in (low, high):
            turned = dq[:, cols].T
            halves.append(jnp.where(head_a, turned[:HALF], turned[HALF:]))
        moved = dot(unorder, jnp.concatenate(halves, axis=0).astype(BF16)).astype(BF16)
        local = pl.multiple_of((query_block % blocks_here) * BLOCK, BLOCK)
        dq_all[query_block // blocks_here, pl.ds(local, BLOCK)] = moved

    delta = forward(0, 0)

    def step(j, delta):
        block = 2 * j
        later = forward(block + 1, 1)
        backward(block, 0, delta)
        last = forward(block + 2, 0)
        backward(block + 1, 1, later)
        return last

    delta = lax.fori_loop(0, (group_blocks - 1) // 2, step, delta)
    if group_blocks % 2 == 0:
        later = forward(group_blocks - 1, 1)
        backward(group_blocks - 2, 0, delta)
        backward(group_blocks - 1, 1, later)
    else:
        backward(group_blocks - 1, 0, delta)

    groups = BLOCK // 16
    for cols, (own_out, first_out, second_out) in ((low, key_outs), (high, value_outs)):
        for out, start, count in (
            (first_out, first_at, SPAN),
            (second_out, second_at, SPAN),
            (own_out, SPAN, group_blocks),
        ):
            part = acc[pl.ds(start, count), :, cols].reshape(count, 2, groups, 8, LANES)
            out[...] = jnp.swapaxes(part, 1, 2).reshape(count, BLOCK, LANES).astype(out.dtype)
    send_pieces(dq_outs, dq_all)


def owner_start(piece, half):
    heads = lax.axis_size("head")
    return pl.multiple_of(((lax.axis_index("head") + 1 + piece) % heads) * half, half)


def add_parts(own_ref, first_ref, second_ref, total, moved):
    group_blocks = own_ref.shape[0]
    first, second = exchange_start(group_blocks)
    total[...] = own_ref[...]
    level = lax.axis_index("var") // GROUP
    levels = lax.axis_size("var") // GROUP
    odd = below_first()
    for other, start, ref in (
        (level + 1 - 2 * odd, first, first_ref),
        (level - 1 + 2 * odd, second, second_ref),
    ):

        @pl.when((other >= 0) & (other < levels))
        def _(start=start, ref=ref):
            at = pl.ds(start, SPAN)
            total[at] = total[at] + ref[...].astype(F32)

    moved[...] = total[...].astype(BF16).reshape(moved.shape)


def combine_kernel(own_ref, first_ref, second_ref, *rest):
    outs, (total, moved) = rest[:GROUP], rest[GROUP:]
    add_parts(own_ref, first_ref, second_ref, total, moved)
    send_pieces(outs, moved)


def combine_split_kernel(own_ref, first_ref, second_ref, *rest):
    aways, homes, (total, moved) = rest[:GROUP], rest[GROUP : 2 * GROUP], rest[2 * GROUP :]
    add_parts(own_ref, first_ref, second_ref, total, moved)
    half = homes[0].shape[0]
    away = aways[0].shape[0] // half
    me = lax.axis_index("var") % GROUP
    for distance in range(GROUP):
        member = me ^ distance
        for piece in range(away):
            aways[distance][piece * half : (piece + 1) * half] = moved[
                member, pl.ds(owner_start(piece, half), half)
            ]
        homes[distance][...] = moved[member, pl.ds(owner_start(away, half), half)]


def gather_rows(grads, stages, start, dv_stage, dv_at):
    half = grads.shape[1]
    width = grads.shape[2] // GROUP
    for member in range(GROUP):
        at = slice(member * width, (member + 1) * width)
        for s, stage in enumerate(stages):
            grads[s, :, at] = stage[member, pl.ds(start, half)][:, :width]
        grads[2, :, at] = dv_stage[member, dv_at * half : (dv_at + 1) * half][:, :width]


def product(grads, w_ref):
    total = dot_nt(grads[0], w_ref[0])
    for s in (1, 2):
        total = total + dot_nt(grads[s], w_ref[s])
    return total


def away_kernel(*refs):
    dqs, dks, dvs, (w_ref, *rest) = refs[:4], refs[4:8], refs[8:12], refs[12:]
    outs, (grads, dq, dk, dv) = rest[:-4], rest[-4:]
    half = grads.shape[1]
    stage_pieces(dq, dqs)
    stage_pieces(dk, dks)
    stage_pieces(dv, dvs)
    for piece, out in enumerate(outs):
        gather_rows(grads, (dq, dk), owner_start(piece, half), dv, piece)
        out[...] = product(grads, w_ref).astype(BF16)


def home_kernel(*refs):
    dqs, dks, aways, homes, rest = refs[:4], refs[4:8], refs[8:12], refs[12:16], refs[16:]
    w_ref, dq_out, dk_out, dv_out, keep_out, grads, dq, dk, away_dv, home_dv = rest
    half = grads.shape[1]
    away = away_dv.shape[1] // half
    stage_pieces(dq, dqs)
    stage_pieces(dk, dks)
    stage_pieces(away_dv, aways)
    stage_pieces(home_dv, homes)
    for piece in range(away + 1):
        start = owner_start(piece, half)
        if piece < away:
            gather_rows(grads, (dq, dk), start, away_dv, piece)
        else:
            gather_rows(grads, (dq, dk), start, home_dv, 0)
        at = pl.ds(start, half)
        dq_out[at] = grads[0]
        dk_out[at] = grads[1]
        dv_out[at] = grads[2]
    keep_out[...] = product(grads, w_ref)


def body(queries, keys, values, out_grad, log_sum_exp, key_blocks, w_qkv):
    rows, features = queries.shape
    head_count = log_sum_exp.shape[0]
    head_dim = features // head_count
    slots = head_count // GROUP
    blocks_here = rows // BLOCK
    group_blocks = GROUP * blocks_here
    window = group_blocks + 2 * SPAN
    slot_count = key_blocks.shape[1]
    devices = lax.axis_size("var")
    heads = lax.axis_size("head")
    half = rows // heads
    model = w_qkv.shape[1]
    wide = 2 * LANES
    hbm = pl.BlockSpec(memory_space=pltpu.HBM)

    def trade(x, distance):
        return lax.ppermute(x, "var", [(n, n ^ distance) for n in range(devices)])

    def trade_level(x, turn):
        pairs = []
        for n in range(devices):
            other = n - GROUP if (n // GROUP + n + turn) % 2 else n + GROUP
            pairs.append((n, other if 0 <= other < devices else n))
        return lax.ppermute(x, "var", pairs)

    def trade_first(x):
        return trade_level(x, 0)

    def trade_second(x):
        return trade_level(x, 1)

    def swap(pieces):
        got = [pieces[0]] + [None] * (GROUP - 1)
        for distance in (2, 3, 1):
            got[distance] = trade(pieces[distance], distance)
        return got

    def staged(count, width=LANES):
        return pltpu.VMEM((GROUP, count, width), BF16)

    block = (BLOCK, LANES)
    anywhere = pl.BlockSpec(memory_space=pl.ANY)

    def cost(flops, moved):
        return pl.CostEstimate(flops=flops, bytes_accessed=moved, transcendentals=0)

    size = rows * features * 2

    kvs = pl.pallas_call(
        pack_kv_kernel,
        out_shape=(shaped((rows, wide)),) * GROUP,
        in_specs=[hbm] * 2,
        out_specs=(vmem(),) * GROUP,
        scratch_shapes=[pltpu.VMEM((rows, features), BF16)] * 2
        + [staged(rows, wide), pltpu.SemaphoreType.DMA((2, LOADS))],
        compiler_params=params(PACK_MIB),
        cost_estimate=cost(4 * rows * features * BLOCK, 5 * size),
    )(keys, values)
    kvs = swap(kvs)
    *qos, kvs[0] = pl.pallas_call(
        functools.partial(pack_qo_kernel, slots, head_dim),
        out_shape=(shaped((rows + LSE_ROWS, wide)),) * GROUP + (shaped((rows, wide)),),
        in_specs=[vmem()] * 4 + [anywhere],
        out_specs=(vmem(),) * (GROUP + 1),
        scratch_shapes=[staged(rows + LSE_ROWS, wide)],
        compiler_params=params(8),
        cost_estimate=cost(4 * rows * features * BLOCK, 10 * size),
    )(queries, out_grad, log_sum_exp, kvs[0], kvs[1])
    carried = tuple(qos[1:])
    own, first, second, *carried = pl.pallas_call(
        functools.partial(line_kernel, len(carried)),
        out_shape=(shaped((GROUP * rows + rows + LSE_ROWS, wide)),)
        + (shaped((SPAN * BLOCK, wide)),) * 2
        + tuple(shaped(x.shape) for x in carried),
        in_specs=[vmem()] * (GROUP + 1) + [anywhere] * len(carried),
        out_specs=(vmem(),) * 3 + (anywhere,) * len(carried),
        input_output_aliases={GROUP + 1 + i: 3 + i for i in range(len(carried))},
        compiler_params=params(8),
        cost_estimate=cost(0, 5 * size),
    )(*kvs, qos[0], *carried)
    first = trade_first(first)
    second = trade_second(second)
    qos = swap([None, *carried])[1:]

    pairs = group_blocks * slot_count * BLOCK * BLOCK * slots
    sums = (shaped((group_blocks,) + block, F32),) + (shaped((SPAN,) + block),) * 2
    results = pl.pallas_call(
        functools.partial(attend_kernel, blocks_here, head_dim),
        out_shape=sums + sums + (shaped((rows, LANES)),) * GROUP,
        in_specs=[pl.BlockSpec(memory_space=pltpu.SMEM)] + [vmem()] * (2 + GROUP),
        out_specs=(vmem(),) * (6 + GROUP),
        scratch_shapes=[
            pltpu.VMEM((window, BLOCK, wide), BF16),
            pltpu.VMEM((window, LANES, BLOCK), BF16),
            pltpu.VMEM((window, BLOCK, wide), F32),
            pltpu.VMEM((group_blocks, 2, 8, wide), F32),
            pltpu.VMEM((2, wide, LANES), BF16),
            pltpu.VMEM((2, wide, LANES), BF16),
            pltpu.VMEM((2, wide, wide), BF16),
            pltpu.VMEM((2, slot_count * BLOCK, wide), F32),
            pltpu.VMEM((2, slot_count * BLOCK, wide), F32),
            staged(rows + LSE_ROWS, wide),
            staged(rows),
        ],
        compiler_params=params(24),
        cost_estimate=pl.CostEstimate(
            flops=40 * pairs * head_dim, bytes_accessed=2_000_000, transcendentals=pairs
        ),
    )(
        key_blocks,
        own,
        first,
        second,
        *qos,
    )
    key_sum, first_part, second_part = results[:3]
    first_back = trade_first(first_part)
    second_back = trade_second(second_part)
    value_sum, first_part, second_part = results[3:6]
    first_value_back = trade_first(first_part)
    second_value_back = trade_second(second_part)
    dqs = swap(results[6:])
    summing = [pltpu.VMEM((group_blocks,) + block, F32), staged(rows)]
    dks = swap(
        pl.pallas_call(
            combine_kernel,
            out_shape=(shaped((rows, LANES)),) * GROUP,
            in_specs=[vmem()] * 3,
            out_specs=(vmem(),) * GROUP,
            scratch_shapes=summing,
            compiler_params=params(8),
            cost_estimate=cost(0, 4 * size),
        )(key_sum, first_back, second_back)
    )
    split = pl.pallas_call(
        combine_split_kernel,
        out_shape=(shaped((rows - half, LANES)),) * GROUP + (shaped((half, LANES)),) * GROUP,
        in_specs=[vmem()] * 3,
        out_specs=(vmem(),) * (2 * GROUP),
        scratch_shapes=summing,
        compiler_params=params(8),
        cost_estimate=cost(0, 4 * size),
    )(value_sum, first_value_back, second_value_back)
    aways = swap(split[:GROUP])
    homes = swap(split[GROUP:])

    grads = pltpu.VMEM((3, half, features), BF16)
    sends = pl.pallas_call(
        away_kernel,
        out_shape=(shaped((half, model)),) * (heads - 1),
        in_specs=[vmem()] * (3 * GROUP + 1),
        out_specs=(vmem(),) * (heads - 1),
        scratch_shapes=[grads, staged(rows), staged(rows), staged(rows - half)],
        compiler_params=params(12),
        cost_estimate=pl.CostEstimate(
            flops=6 * (rows - half) * features * model, bytes_accessed=4_000_000, transcendentals=0
        ),
    )(*dqs, *dks, *aways, w_qkv)
    dq_out, dk_out, dv_out, total = pl.pallas_call(
        home_kernel,
        out_shape=(shaped((rows, features)),) * 3 + (shaped((half, model), F32),),
        in_specs=[vmem()] * (4 * GROUP + 1),
        out_specs=(vmem(),) * 4,
        scratch_shapes=[grads, staged(rows), staged(rows), staged(rows - half), staged(half)],
        compiler_params=params(12),
        cost_estimate=pl.CostEstimate(
            flops=6 * half * features * model, bytes_accessed=6_000_000, transcendentals=0
        ),
    )(*dqs, *dks, *aways, *homes, w_qkv)
    for piece, send in enumerate(sends):
        got = lax.ppermute(send, "head", [(n, (n + piece + 1) % heads) for n in range(heads)])
        total = total + got.astype(F32)
    return dq_out, dk_out, dv_out, total.astype(BF16)


def solution(mesh):
    in_specs = (
        P("var", "head"),
        P("var", "head"),
        P("var", "head"),
        P("var", "head"),
        P("head", "var"),
        P(),
        P(None, None, "head"),
    )
    out_specs = (P("var", "head"), P("var", "head"), P("var", "head"), P(("var", "head"), None))
    return jax.shard_map(body, mesh=mesh, in_specs=in_specs, out_specs=out_specs, check_vma=False)
```

```python
import functools

import jax
import jax.numpy as jnp
from jax import lax
from jax.experimental import pallas as pl
from jax.experimental.pallas import tpu as pltpu
from jax.sharding import PartitionSpec as P

PATCHES = 16
BLOCK = 128
HALF = BLOCK // 2
SPAN = 8
GROUP = 4
LANES = 128
LSE_ROWS = 16
LOADS = 3
F32 = jnp.float32
BF16 = jnp.bfloat16
MIB = 1024 * 1024
PACK_MIB = 62


def vmem():
    return pl.BlockSpec(memory_space=pltpu.VMEM)


def params(mib):
    return pltpu.CompilerParams(vmem_limit_bytes=mib * MIB)


def shaped(shape, dtype=BF16):
    return jax.ShapeDtypeStruct(shape, dtype)


def dot(a, b):
    return jnp.dot(a, b, preferred_element_type=F32)


def dot_nt(a, b):
    return lax.dot_general(a, b, (((1,), (1,)), ((), ())), preferred_element_type=F32)


def token_at(place):
    return (((place & (HALF - 1)) >> 3) << 4) + ((place >> 6) << 3) + (place & 7)


def one_where(mask):
    return jnp.where(mask, 1.0, 0.0).astype(BF16)


def reorder_matrix(inverse):
    row = lax.broadcasted_iota(jnp.int32, (BLOCK, BLOCK), 0)
    col = lax.broadcasted_iota(jnp.int32, (BLOCK, BLOCK), 1)
    return one_where(row == token_at(col)) if inverse else one_where(col == token_at(row))


def split_three(x):
    high = x.astype(BF16).astype(F32)
    rest = x - high
    mid = rest.astype(BF16).astype(F32)
    return high, mid, rest - mid


def widen(x):
    if x.shape[1] == LANES:
        return x
    return jnp.concatenate([x, jnp.zeros((x.shape[0], LANES - x.shape[1]), x.dtype)], axis=1)


def send_pieces(outs, stage):
    me = lax.axis_index("var") % GROUP
    for distance, out in enumerate(outs):
        out[...] = stage[me ^ distance]


def stage_pieces(stage, pieces):
    me = lax.axis_index("var") % GROUP
    for distance, piece in enumerate(pieces):
        stage[me ^ distance] = piece[...]


def load_all(pairs, sems):
    copies = []
    for i, (source, target) in enumerate(pairs):
        rows = source.shape[0] // LOADS
        for part in range(LOADS):
            at = pl.ds(part * rows, rows)
            copies.append(pltpu.make_async_copy(source.at[at], target.at[at], sems.at[i, part]))
    for copy in copies:
        copy.start()
    return [copies[i * LOADS : (i + 1) * LOADS] for i in range(len(pairs))]


def reorder_into(staged, half, ref, scale=None):
    rows, features = ref.shape
    width = features // GROUP
    order = reorder_matrix(False)
    for b in range(rows // BLOCK):
        at = slice(b * BLOCK, (b + 1) * BLOCK)
        moved = dot(order, ref[at])
        if scale is not None:
            moved = moved * scale
        moved = moved.astype(BF16)
        for member in range(GROUP):
            staged[member, at, half * LANES : (half + 1) * LANES] = widen(
                moved[:, member * width : (member + 1) * width]
            )


def pack_kv_kernel(k_hbm, v_hbm, *rest):
    outs, (k_ref, v_ref, turned, sems) = rest[:GROUP], rest[GROUP:]
    arrivals = load_all([(k_hbm, k_ref), (v_hbm, v_ref)], sems)
    for half, ref in enumerate((k_ref, v_ref)):
        for copy in arrivals[half]:
            copy.wait()
        reorder_into(turned, half, ref)
    send_pieces(outs, turned)


def pack_qo_kernel(slots, head_dim, q_ref, g_ref, lse_ref, mine_ref, after_ref, *rest):
    outs, (hold, qo_ref) = rest[:GROUP], rest[GROUP:]
    hold[...] = mine_ref[...]
    rows = q_ref.shape[0]
    blocks = rows // BLOCK
    reorder_into(qo_ref, 0, q_ref, head_dim ** (-0.5))
    reorder_into(qo_ref, 1, g_ref)
    token = lax.broadcasted_iota(jnp.int32, (BLOCK, 2 * LANES), 0)
    lane = lax.broadcasted_iota(jnp.int32, (BLOCK, 2 * LANES), 1)
    place = ((lane >> 7) << 6) + (lane & (HALF - 1))
    hit = token == token_at(place)
    upper = (lane & HALF) != 0
    spread = [one_where(hit & ~upper), one_where(hit & upper)]
    for member in range(GROUP):
        total = None
        for slot in range(slots):
            lse = lse_ref[member * slots + slot : member * slots + slot + 1, :]
            parts = [
                part[:, b * BLOCK : (b + 1) * BLOCK]
                for part in split_three(lse)
                for b in range(blocks)
            ]
            parts.append(jnp.zeros((LSE_ROWS - len(parts), BLOCK), F32))
            moved = dot(jnp.concatenate(parts, axis=0).astype(BF16), spread[slot])
            total = moved if total is None else total + moved
        qo_ref[member, rows:] = total.astype(BF16)
    send_pieces(outs, qo_ref)


def below_first():
    me = lax.axis_index("var")
    return (me // GROUP + me) % 2


def exchange_start(group_blocks):
    odd = below_first()
    reach = group_blocks - SPAN
    return (1 - odd) * reach, odd * reach


def line_kernel(carried, *refs):
    pieces, query_piece, refs = refs[:GROUP], refs[GROUP], refs[GROUP + 1 + carried :]
    own, first_out, second_out = refs[:3]
    rows = pieces[0].shape[0]
    own[GROUP * rows :] = query_piece[...]
    blocks = rows // BLOCK
    me = lax.axis_index("var") % GROUP
    for distance in range(GROUP):
        at = pl.ds(pl.multiple_of((me ^ distance) * rows, rows), rows)
        own[at] = pieces[distance][...]
    first, second = exchange_start(GROUP * blocks)
    for start, out in ((first, first_out), (second, second_out)):
        out[...] = own[pl.ds(pl.multiple_of(start * BLOCK, BLOCK), SPAN * BLOCK)]


def attend_kernel(
    blocks_here,
    head_dim,
    kb_ref,
    *refs,
):
    kv_refs, refs = refs[:3], refs[3:]
    qo_pieces, refs = refs[: GROUP - 1], refs[GROUP - 1 :]
    key_outs, value_outs, refs = refs[:3], refs[3:6], refs[6:]
    dq_outs, refs = refs[:GROUP], refs[GROUP:]
    kv_win, k_turn, acc, shifts, queries, grads, crossed, prob, slope, qo_ref, dq_all = refs
    group_blocks = GROUP * blocks_here
    window = group_blocks + 2 * SPAN
    rows = blocks_here * BLOCK
    slot_count = kb_ref.shape[1]
    scale = head_dim ** (-0.5)
    base = (lax.axis_index("var") // GROUP) * group_blocks
    odd = below_first()
    top = window - SPAN
    first_at, second_at = (1 - odd) * top, odd * top
    low = slice(0, LANES)
    high = slice(LANES, 2 * LANES)

    for ref, start, count in zip(
        kv_refs, (SPAN, first_at, second_at), (group_blocks, SPAN, SPAN)
    ):
        kv_win[pl.ds(start, count)] = ref[: count * BLOCK].reshape(count, BLOCK, 2 * LANES)
    own_queries = kv_refs[0].at[pl.ds(group_blocks * BLOCK, rows + LSE_ROWS)]
    stage_pieces(qo_ref, (own_queries, *qo_pieces))
    key_patch = lax.broadcasted_iota(jnp.int32, (8, LANES), 0)
    query_patch = lax.broadcasted_iota(jnp.int32, (8, LANES), 1) & 7
    usable = key_patch <= query_patch
    for member in range(GROUP):
        parts = qo_ref[member, rows:].astype(F32)
        for local in range(blocks_here):
            lse = (
                parts[local : local + 1] + parts[blocks_here + local : blocks_here + local + 1]
            ) + parts[2 * blocks_here + local : 2 * blocks_here + local + 1]
            at = member * blocks_here + local
            shifts[at, 0, :, low] = jnp.where(usable, -lse[:, low], -1e30)
            shifts[at, 0, :, high] = jnp.broadcast_to(-lse[:, high], (8, LANES))
            shifts[at, 1, :, low] = jnp.where(usable, -lse[:, high], -1e30)
    acc[...] = jnp.zeros_like(acc)
    crossed[...] = jnp.zeros_like(crossed)

    @pl.loop(0, window)
    def _(block):
        k_turn[block] = kv_win[block, :, low].T

    unorder = reorder_matrix(True)
    lane = lax.broadcasted_iota(jnp.int32, (HALF, LANES), 1)
    head_a = lane < HALF

    def picks(query_block):
        return [kb_ref[base + query_block, s] - base + SPAN for s in range(slot_count)]

    def lay_out(member, local, buf):
        at = pl.multiple_of(local * BLOCK, BLOCK)
        for part in range(2):
            rows_at = pl.ds(at + part * HALF, HALF)
            for cols, target in ((low, queries), (high, grads)):
                tile = qo_ref[member, rows_at, cols]
                zero = jnp.zeros_like(tile)
                both = jnp.concatenate(
                    [jnp.where(head_a, tile, zero), jnp.where(head_a, zero, tile)], axis=0
                )
                target[buf, part * BLOCK : (part + 1) * BLOCK] = both
                if part == 1:
                    side = 0 if target is queries else 1
                    crossed[
                        buf, side * BLOCK : (side + 1) * BLOCK, side * LANES : (side + 1) * LANES
                    ] = both

    def gather(index, rows_of, cols):
        return jnp.concatenate([kv_win[i, rows_of, cols] for i in index], axis=0)

    early = slice(0, HALF)
    late = slice(HALF, BLOCK)
    both_cols = slice(0, 2 * LANES)
    early_rows = slot_count * HALF

    def forward(query_block, buf):
        lay_out(query_block // blocks_here, query_block % blocks_here, buf)
        index = picks(query_block)
        s = dot_nt(gather(index, early, low), queries[buf])
        g = dot_nt(gather(index, early, high), grads[buf])
        x = dot_nt(gather(index, late, both_cols), crossed[buf])
        shift = shifts[query_block, 0][None]
        p = jnp.exp(s.reshape(early_rows // 8, 8, 2 * LANES) + shift).reshape(early_rows, 2 * LANES)
        prob[buf, :early_rows] = p
        slope[buf, :early_rows] = g
        delta = jnp.sum((p * g).reshape(early_rows // 8, 8, 2 * LANES), axis=0)
        late_shift = shifts[query_block, 1, :, low][None]
        q = jnp.exp(x[:, low].reshape(early_rows // 8, 8, LANES) + late_shift).reshape(
            early_rows, LANES
        )
        prob[buf, early_rows:, low] = q
        slope[buf, early_rows:, low] = x[:, high]
        more = jnp.sum((q * x[:, high]).reshape(early_rows // 8, 8, LANES), axis=0)
        delta_low = jnp.sum(delta[:, low], axis=0, keepdims=True)
        delta_high = jnp.sum(delta[:, high] + more, axis=0, keepdims=True)
        return jnp.concatenate([delta_low, delta_high], axis=1)

    def backward(query_block, buf, delta):
        index = picks(query_block)
        p = prob[buf, :early_rows]
        ds = (p * (slope[buf, :early_rows] - delta)).astype(BF16)
        q = prob[buf, early_rows:, low]
        ds_late = (q * (slope[buf, early_rows:, low] - delta[:, high])).astype(BF16)
        dk = dot(ds, queries[buf])
        dv = dot(p.astype(BF16), grads[buf])
        r = dot(jnp.concatenate([ds_late, q.astype(BF16)], axis=1), crossed[buf])
        nothing = jnp.zeros((HALF, LANES), BF16)
        pieces = []
        for s in range(slot_count):
            at = slice(s * HALF, (s + 1) * HALF)
            where = index[s]
            acc[where, early, low] = acc[where, early, low] + dk[at]
            acc[where, early, high] = acc[where, early, high] + dv[at]
            acc[where, late] = acc[where, late] + r[at]
            pieces.append(ds[at])
            pieces.append(jnp.concatenate([nothing, ds_late[at]], axis=1))
        keys_turned = jnp.concatenate([k_turn[i] for i in index], axis=1)
        dq = dot(keys_turned, jnp.concatenate(pieces, axis=0)) * scale
        halves = []
        for cols in (low, high):
            turned = dq[:, cols].T
            halves.append(jnp.where(head_a, turned[:HALF], turned[HALF:]))
        moved = dot(unorder, jnp.concatenate(halves, axis=0).astype(BF16)).astype(BF16)
        local = pl.multiple_of((query_block % blocks_here) * BLOCK, BLOCK)
        dq_all[query_block // blocks_here, pl.ds(local, BLOCK)] = moved

    delta = forward(0, 0)

    def step(j, delta):
        block = 2 * j
        later = forward(block + 1, 1)
        backward(block, 0, delta)
        last = forward(block + 2, 0)
        backward(block + 1, 1, later)
        return last

    delta = lax.fori_loop(0, (group_blocks - 1) // 2, step, delta)
    if group_blocks % 2 == 0:
        later = forward(group_blocks - 1, 1)
        backward(group_blocks - 2, 0, delta)
        backward(group_blocks - 1, 1, later)
    else:
        backward(group_blocks - 1, 0, delta)

    groups = BLOCK // 16
    for cols, (own_out, first_out, second_out) in ((low, key_outs), (high, value_outs)):
        for out, start, count in (
            (first_out, first_at, SPAN),
            (second_out, second_at, SPAN),
            (own_out, SPAN, group_blocks),
        ):
            part = acc[pl.ds(start, count), :, cols].reshape(count, 2, groups, 8, LANES)
            out[...] = jnp.swapaxes(part, 1, 2).reshape(count, BLOCK, LANES).astype(out.dtype)
    send_pieces(dq_outs, dq_all)


def owner_start(piece, half):
    heads = lax.axis_size("head")
    return pl.multiple_of(((lax.axis_index("head") + 1 + piece) % heads) * half, half)


def add_parts(own_ref, first_ref, second_ref, total, moved):
    group_blocks = own_ref.shape[0]
    first, second = exchange_start(group_blocks)
    total[...] = own_ref[...]
    level = lax.axis_index("var") // GROUP
    levels = lax.axis_size("var") // GROUP
    odd = below_first()
    for other, start, ref in (
        (level + 1 - 2 * odd, first, first_ref),
        (level - 1 + 2 * odd, second, second_ref),
    ):

        @pl.when((other >= 0) & (other < levels))
        def _(start=start, ref=ref):
            at = pl.ds(start, SPAN)
            total[at] = total[at] + ref[...].astype(F32)

    moved[...] = total[...].astype(BF16).reshape(moved.shape)


def combine_kernel(own_ref, first_ref, second_ref, *rest):
    outs, (total, moved) = rest[:GROUP], rest[GROUP:]
    add_parts(own_ref, first_ref, second_ref, total, moved)
    send_pieces(outs, moved)


def combine_split_kernel(own_ref, first_ref, second_ref, *rest):
    aways, homes, (total, moved) = rest[:GROUP], rest[GROUP : 2 * GROUP], rest[2 * GROUP :]
    add_parts(own_ref, first_ref, second_ref, total, moved)
    half = homes[0].shape[0]
    away = aways[0].shape[0] // half
    me = lax.axis_index("var") % GROUP
    for distance in range(GROUP):
        member = me ^ distance
        for piece in range(away):
            aways[distance][piece * half : (piece + 1) * half] = moved[
                member, pl.ds(owner_start(piece, half), half)
            ]
        homes[distance][...] = moved[member, pl.ds(owner_start(away, half), half)]


def gather_rows(grads, stages, start, dv_stage, dv_at):
    half = grads.shape[1]
    width = grads.shape[2] // GROUP
    for member in range(GROUP):
        at = slice(member * width, (member + 1) * width)
        for s, stage in enumerate(stages):
            grads[s, :, at] = stage[member, pl.ds(start, half)][:, :width]
        grads[2, :, at] = dv_stage[member, dv_at * half : (dv_at + 1) * half][:, :width]


def product(grads, w_ref):
    total = dot_nt(grads[0], w_ref[0])
    for s in (1, 2):
        total = total + dot_nt(grads[s], w_ref[s])
    return total


def away_kernel(*refs):
    dqs, dks, dvs, (w_ref, *rest) = refs[:4], refs[4:8], refs[8:12], refs[12:]
    outs, (grads, dq, dk, dv) = rest[:-4], rest[-4:]
    half = grads.shape[1]
    stage_pieces(dq, dqs)
    stage_pieces(dk, dks)
    stage_pieces(dv, dvs)
    for piece, out in enumerate(outs):
        gather_rows(grads, (dq, dk), owner_start(piece, half), dv, piece)
        out[...] = product(grads, w_ref).astype(BF16)


def home_kernel(*refs):
    dqs, dks, aways, homes, rest = refs[:4], refs[4:8], refs[8:12], refs[12:16], refs[16:]
    w_ref, dq_out, dk_out, dv_out, keep_out, grads, dq, dk, away_dv, home_dv = rest
    half = grads.shape[1]
    away = away_dv.shape[1] // half
    stage_pieces(dq, dqs)
    stage_pieces(dk, dks)
    stage_pieces(away_dv, aways)
    stage_pieces(home_dv, homes)
    for piece in range(away + 1):
        start = owner_start(piece, half)
        if piece < away:
            gather_rows(grads, (dq, dk), start, away_dv, piece)
        else:
            gather_rows(grads, (dq, dk), start, home_dv, 0)
        at = pl.ds(start, half)
        dq_out[at] = grads[0]
        dk_out[at] = grads[1]
        dv_out[at] = grads[2]
    keep_out[...] = product(grads, w_ref)


def body(queries, keys, values, out_grad, log_sum_exp, key_blocks, w_qkv):
    rows, features = queries.shape
    head_count = log_sum_exp.shape[0]
    head_dim = features // head_count
    slots = head_count // GROUP
    blocks_here = rows // BLOCK
    group_blocks = GROUP * blocks_here
    window = group_blocks + 2 * SPAN
    slot_count = key_blocks.shape[1]
    devices = lax.axis_size("var")
    heads = lax.axis_size("head")
    half = rows // heads
    model = w_qkv.shape[1]
    wide = 2 * LANES
    hbm = pl.BlockSpec(memory_space=pltpu.HBM)

    def trade(x, distance):
        return lax.ppermute(x, "var", [(n, n ^ distance) for n in range(devices)])

    def trade_level(x, turn):
        pairs = []
        for n in range(devices):
            other = n - GROUP if (n // GROUP + n + turn) % 2 else n + GROUP
            for h in range(heads):
                if 0 <= other < devices:
                    target = other * heads + h
                else:
                    target = n * heads + (h ^ 1) % heads
                pairs.append((n * heads + h, target))
        return lax.ppermute(x, ("var", "head"), pairs)

    def trade_first(x):
        return trade_level(x, 0)

    def trade_second(x):
        return trade_level(x, 1)

    def swap(pieces):
        got = [pieces[0]] + [None] * (GROUP - 1)
        for distance in (2, 3, 1):
            got[distance] = trade(pieces[distance], distance)
        return got

    def staged(count, width=LANES):
        return pltpu.VMEM((GROUP, count, width), BF16)

    block = (BLOCK, LANES)
    anywhere = pl.BlockSpec(memory_space=pl.ANY)

    def cost(flops, moved):
        return pl.CostEstimate(flops=flops, bytes_accessed=moved, transcendentals=0)

    size = rows * features * 2

    kvs = pl.pallas_call(
        pack_kv_kernel,
        out_shape=(shaped((rows, wide)),) * GROUP,
        in_specs=[hbm] * 2,
        out_specs=(vmem(),) * GROUP,
        scratch_shapes=[pltpu.VMEM((rows, features), BF16)] * 2
        + [staged(rows, wide), pltpu.SemaphoreType.DMA((2, LOADS))],
        compiler_params=params(PACK_MIB),
        cost_estimate=cost(4 * rows * features * BLOCK, 5 * size),
    )(keys, values)
    kvs = swap(kvs)
    *qos, kvs[0] = pl.pallas_call(
        functools.partial(pack_qo_kernel, slots, head_dim),
        out_shape=(shaped((rows + LSE_ROWS, wide)),) * GROUP + (shaped((rows, wide)),),
        in_specs=[vmem()] * 4 + [anywhere],
        out_specs=(vmem(),) * (GROUP + 1),
        scratch_shapes=[staged(rows + LSE_ROWS, wide)],
        compiler_params=params(8),
        cost_estimate=cost(4 * rows * features * BLOCK, 10 * size),
    )(queries, out_grad, log_sum_exp, kvs[0], kvs[1])
    carried = tuple(qos[1:])
    own, first, second, *carried = pl.pallas_call(
        functools.partial(line_kernel, len(carried)),
        out_shape=(shaped((GROUP * rows + rows + LSE_ROWS, wide)),)
        + (shaped((SPAN * BLOCK, wide)),) * 2
        + tuple(shaped(x.shape) for x in carried),
        in_specs=[vmem()] * (GROUP + 1) + [anywhere] * len(carried),
        out_specs=(vmem(),) * 3 + (anywhere,) * len(carried),
        input_output_aliases={GROUP + 1 + i: 3 + i for i in range(len(carried))},
        compiler_params=params(8),
        cost_estimate=cost(0, 5 * size),
    )(*kvs, qos[0], *carried)
    first = trade_first(first)
    second = trade_second(second)
    qos = swap([None, *carried])[1:]

    pairs = group_blocks * slot_count * BLOCK * BLOCK * slots
    sums = (shaped((group_blocks,) + block, F32),) + (shaped((SPAN,) + block),) * 2
    results = pl.pallas_call(
        functools.partial(attend_kernel, blocks_here, head_dim),
        out_shape=sums + sums + (shaped((rows, LANES)),) * GROUP,
        in_specs=[pl.BlockSpec(memory_space=pltpu.SMEM)] + [vmem()] * (2 + GROUP),
        out_specs=(vmem(),) * (6 + GROUP),
        scratch_shapes=[
            pltpu.VMEM((window, BLOCK, wide), BF16),
            pltpu.VMEM((window, LANES, BLOCK), BF16),
            pltpu.VMEM((window, BLOCK, wide), F32),
            pltpu.VMEM((group_blocks, 2, 8, wide), F32),
            pltpu.VMEM((2, wide, LANES), BF16),
            pltpu.VMEM((2, wide, LANES), BF16),
            pltpu.VMEM((2, wide, wide), BF16),
            pltpu.VMEM((2, slot_count * BLOCK, wide), F32),
            pltpu.VMEM((2, slot_count * BLOCK, wide), F32),
            staged(rows + LSE_ROWS, wide),
            staged(rows),
        ],
        compiler_params=params(24),
        cost_estimate=pl.CostEstimate(
            flops=40 * pairs * head_dim, bytes_accessed=2_000_000, transcendentals=pairs
        ),
    )(
        key_blocks,
        own,
        first,
        second,
        *qos,
    )
    key_sum, first_part, second_part = results[:3]
    first_back = trade_first(first_part)
    second_back = trade_second(second_part)
    value_sum, first_part, second_part = results[3:6]
    first_value_back = trade_first(first_part)
    second_value_back = trade_second(second_part)
    dqs = swap(results[6:])
    summing = [pltpu.VMEM((group_blocks,) + block, F32), staged(rows)]
    dks = swap(
        pl.pallas_call(
            combine_kernel,
            out_shape=(shaped((rows, LANES)),) * GROUP,
            in_specs=[vmem()] * 3,
            out_specs=(vmem(),) * GROUP,
            scratch_shapes=summing,
            compiler_params=params(8),
            cost_estimate=cost(0, 4 * size),
        )(key_sum, first_back, second_back)
    )
    split = pl.pallas_call(
        combine_split_kernel,
        out_shape=(shaped((rows - half, LANES)),) * GROUP + (shaped((half, LANES)),) * GROUP,
        in_specs=[vmem()] * 3,
        out_specs=(vmem(),) * (2 * GROUP),
        scratch_shapes=summing,
        compiler_params=params(8),
        cost_estimate=cost(0, 4 * size),
    )(value_sum, first_value_back, second_value_back)
    aways = swap(split[:GROUP])
    homes = swap(split[GROUP:])

    grads = pltpu.VMEM((3, half, features), BF16)
    sends = pl.pallas_call(
        away_kernel,
        out_shape=(shaped((half, model)),) * (heads - 1),
        in_specs=[vmem()] * (3 * GROUP + 1),
        out_specs=(vmem(),) * (heads - 1),
        scratch_shapes=[grads, staged(rows), staged(rows), staged(rows - half)],
        compiler_params=params(12),
        cost_estimate=pl.CostEstimate(
            flops=6 * (rows - half) * features * model, bytes_accessed=4_000_000, transcendentals=0
        ),
    )(*dqs, *dks, *aways, w_qkv)
    dq_out, dk_out, dv_out, total = pl.pallas_call(
        home_kernel,
        out_shape=(shaped((rows, features)),) * 3 + (shaped((half, model), F32),),
        in_specs=[vmem()] * (4 * GROUP + 1),
        out_specs=(vmem(),) * 4,
        scratch_shapes=[grads, staged(rows), staged(rows), staged(rows - half), staged(half)],
        compiler_params=params(12),
        cost_estimate=pl.CostEstimate(
            flops=6 * half * features * model, bytes_accessed=6_000_000, transcendentals=0
        ),
    )(*dqs, *dks, *aways, *homes, w_qkv)
    for piece, send in enumerate(sends):
        got = lax.ppermute(send, "head", [(n, (n + piece + 1) % heads) for n in range(heads)])
        total = total + got.astype(F32)
    return dq_out, dk_out, dv_out, total.astype(BF16)


def solution(mesh):
    in_specs = (
        P("var", "head"),
        P("var", "head"),
        P("var", "head"),
        P("var", "head"),
        P("head", "var"),
        P(),
        P(None, None, "head"),
    )
    out_specs = (P("var", "head"), P("var", "head"), P("var", "head"), P(("var", "head"), None))
    return jax.shard_map(body, mesh=mesh, in_specs=in_specs, out_specs=out_specs, check_vma=False)
```

```python
import functools

import jax
import jax.numpy as jnp
from jax import lax
from jax.experimental import pallas as pl
from jax.experimental.pallas import tpu as pltpu
from jax.sharding import PartitionSpec as P

PATCHES = 16
BLOCK = 128
HALF = BLOCK // 2
SPAN = 8
OUTER = SPAN // 2
GROUP = 4
LANES = 128
LSE_ROWS = 16
LOADS = 3
F32 = jnp.float32
BF16 = jnp.bfloat16
MIB = 1024 * 1024
PACK_MIB = 62


def vmem():
    return pl.BlockSpec(memory_space=pltpu.VMEM)


def params(mib):
    return pltpu.CompilerParams(vmem_limit_bytes=mib * MIB)


def shaped(shape, dtype=BF16):
    return jax.ShapeDtypeStruct(shape, dtype)


def dot(a, b):
    return jnp.dot(a, b, preferred_element_type=F32)


def dot_nt(a, b):
    return lax.dot_general(a, b, (((1,), (1,)), ((), ())), preferred_element_type=F32)


def token_at(place):
    return (((place & (HALF - 1)) >> 3) << 4) + ((place >> 6) << 3) + (place & 7)


def one_where(mask):
    return jnp.where(mask, 1.0, 0.0).astype(BF16)


def reorder_matrix(inverse):
    row = lax.broadcasted_iota(jnp.int32, (BLOCK, BLOCK), 0)
    col = lax.broadcasted_iota(jnp.int32, (BLOCK, BLOCK), 1)
    return one_where(row == token_at(col)) if inverse else one_where(col == token_at(row))


def split_three(x):
    high = x.astype(BF16).astype(F32)
    rest = x - high
    mid = rest.astype(BF16).astype(F32)
    return high, mid, rest - mid


def widen(x):
    if x.shape[1] == LANES:
        return x
    return jnp.concatenate([x, jnp.zeros((x.shape[0], LANES - x.shape[1]), x.dtype)], axis=1)


def send_pieces(outs, stage):
    me = lax.axis_index("var") % GROUP
    for distance, out in enumerate(outs):
        out[...] = stage[me ^ distance]


def stage_pieces(stage, pieces):
    me = lax.axis_index("var") % GROUP
    for distance, piece in enumerate(pieces):
        stage[me ^ distance] = piece[...]


def load_all(pairs, sems):
    copies = []
    for i, (source, target) in enumerate(pairs):
        rows = source.shape[0] // LOADS
        for part in range(LOADS):
            at = pl.ds(part * rows, rows)
            copies.append(pltpu.make_async_copy(source.at[at], target.at[at], sems.at[i, part]))
    for copy in copies:
        copy.start()
    return [copies[i * LOADS : (i + 1) * LOADS] for i in range(len(pairs))]


def reorder_into(staged, half, ref, scale=None):
    rows, features = ref.shape
    width = features // GROUP
    order = reorder_matrix(False)
    for b in range(rows // BLOCK):
        at = slice(b * BLOCK, (b + 1) * BLOCK)
        moved = dot(order, ref[at])
        if scale is not None:
            moved = moved * scale
        moved = moved.astype(BF16)
        for member in range(GROUP):
            staged[member, at, half * LANES : (half + 1) * LANES] = widen(
                moved[:, member * width : (member + 1) * width]
            )


def pack_kv_kernel(k_hbm, v_hbm, *rest):
    outs, (k_ref, v_ref, turned, sems) = rest[:GROUP], rest[GROUP:]
    arrivals = load_all([(k_hbm, k_ref), (v_hbm, v_ref)], sems)
    for half, ref in enumerate((k_ref, v_ref)):
        for copy in arrivals[half]:
            copy.wait()
        reorder_into(turned, half, ref)
    send_pieces(outs, turned)


def pack_qo_kernel(slots, head_dim, q_ref, g_ref, lse_ref, mine_ref, after_ref, *rest):
    outs, (hold, qo_ref) = rest[:GROUP], rest[GROUP:]
    hold[...] = mine_ref[...]
    rows = q_ref.shape[0]
    blocks = rows // BLOCK
    reorder_into(qo_ref, 0, q_ref, head_dim ** (-0.5))
    reorder_into(qo_ref, 1, g_ref)
    token = lax.broadcasted_iota(jnp.int32, (BLOCK, 2 * LANES), 0)
    lane = lax.broadcasted_iota(jnp.int32, (BLOCK, 2 * LANES), 1)
    place = ((lane >> 7) << 6) + (lane & (HALF - 1))
    hit = token == token_at(place)
    upper = (lane & HALF) != 0
    spread = [one_where(hit & ~upper), one_where(hit & upper)]
    for member in range(GROUP):
        total = None
        for slot in range(slots):
            lse = lse_ref[member * slots + slot : member * slots + slot + 1, :]
            parts = [
                part[:, b * BLOCK : (b + 1) * BLOCK]
                for part in split_three(lse)
                for b in range(blocks)
            ]
            parts.append(jnp.zeros((LSE_ROWS - len(parts), BLOCK), F32))
            moved = dot(jnp.concatenate(parts, axis=0).astype(BF16), spread[slot])
            total = moved if total is None else total + moved
        qo_ref[member, rows:] = total.astype(BF16)
    send_pieces(outs, qo_ref)


def below_first():
    me = lax.axis_index("var")
    return (me // GROUP + me) % 2


def exchange_start(group_blocks):
    odd = below_first()
    reach = group_blocks - SPAN
    return (1 - odd) * reach, odd * reach


def line_kernel(carried, *refs):
    pieces, query_piece, refs = refs[:GROUP], refs[GROUP], refs[GROUP + 1 + carried :]
    own, first_out, second_out = refs[:3]
    rows = pieces[0].shape[0]
    own[GROUP * rows :] = query_piece[...]
    blocks = rows // BLOCK
    me = lax.axis_index("var") % GROUP
    for distance in range(GROUP):
        at = pl.ds(pl.multiple_of((me ^ distance) * rows, rows), rows)
        own[at] = pieces[distance][...]
    first, second = exchange_start(GROUP * blocks)
    for start, out in ((first, first_out), (second, second_out)):
        out[...] = own[pl.ds(pl.multiple_of(start * BLOCK, BLOCK), SPAN * BLOCK)]


def attend_kernel(last, blocks_here, head_dim, kb_ref, *refs):
    if last:
        kv_win, k_turn, shifts, qo_ref, before, dq_before, *refs = refs
        own_out, first_out, second_out, *refs = refs
        dq_outs, refs = refs[:GROUP], refs[GROUP:]
        acc, queries, grads, crossed, prob, slope, dq_all = refs
    else:
        kv_refs, refs = refs[:3], refs[3:]
        qo_pieces, refs = refs[: GROUP - 1], refs[GROUP - 1 :]
        first_out, second_out, kv_win, k_turn, shifts, qo_ref, kept_out, dq_all, *refs = refs
        acc, queries, grads, crossed, prob, slope = refs
    group_blocks = GROUP * blocks_here
    window = group_blocks + 2 * SPAN
    rows = blocks_here * BLOCK
    slot_count = kb_ref.shape[1]
    scale = head_dim ** (-0.5)
    base = (lax.axis_index("var") // GROUP) * group_blocks
    odd = below_first()
    low = slice(0, LANES)
    high = slice(LANES, 2 * LANES)

    acc[...] = jnp.zeros_like(acc)
    crossed[...] = jnp.zeros_like(crossed)
    if last:
        dq_all[...] = dq_before[...]
    else:
        top = window - SPAN
        for ref, start, count in zip(
            kv_refs, (SPAN, (1 - odd) * top, odd * top), (group_blocks, SPAN, SPAN)
        ):
            kv_win[pl.ds(start, count)] = ref[: count * BLOCK].reshape(count, BLOCK, 2 * LANES)
        own_queries = kv_refs[0].at[pl.ds(group_blocks * BLOCK, rows + LSE_ROWS)]
        stage_pieces(qo_ref, (own_queries, *qo_pieces))
        key_patch = lax.broadcasted_iota(jnp.int32, (8, LANES), 0)
        query_patch = lax.broadcasted_iota(jnp.int32, (8, LANES), 1) & 7
        usable = key_patch <= query_patch
        for member in range(GROUP):
            parts = qo_ref[member, rows:].astype(F32)
            for local in range(blocks_here):
                lse = (
                    parts[local : local + 1] + parts[blocks_here + local : blocks_here + local + 1]
                ) + parts[2 * blocks_here + local : 2 * blocks_here + local + 1]
                at = member * blocks_here + local
                shifts[at, 0, :, low] = jnp.where(usable, -lse[:, low], -1e30)
                shifts[at, 0, :, high] = jnp.broadcast_to(-lse[:, high], (8, LANES))
                shifts[at, 1, :, low] = jnp.where(usable, -lse[:, high], -1e30)

        @pl.loop(0, window)
        def _(block):
            k_turn[block] = kv_win[block, :, low].T

    unorder = reorder_matrix(True)
    lane = lax.broadcasted_iota(jnp.int32, (HALF, LANES), 1)
    head_a = lane < HALF

    def picks(query_block):
        return [kb_ref[base + query_block, s] - base + SPAN for s in range(slot_count)]

    def lay_out(member, local, buf):
        at = pl.multiple_of(local * BLOCK, BLOCK)
        for part in range(2):
            rows_at = pl.ds(at + part * HALF, HALF)
            for cols, target in ((low, queries), (high, grads)):
                tile = qo_ref[member, rows_at, cols]
                zero = jnp.zeros_like(tile)
                both = jnp.concatenate(
                    [jnp.where(head_a, tile, zero), jnp.where(head_a, zero, tile)], axis=0
                )
                target[buf, part * BLOCK : (part + 1) * BLOCK] = both
                if part == 1:
                    side = 0 if target is queries else 1
                    crossed[
                        buf, side * BLOCK : (side + 1) * BLOCK, side * LANES : (side + 1) * LANES
                    ] = both

    def gather(index, rows_of, cols):
        return jnp.concatenate([kv_win[i, rows_of, cols] for i in index], axis=0)

    early = slice(0, HALF)
    late = slice(HALF, BLOCK)
    both_cols = slice(0, 2 * LANES)
    early_rows = slot_count * HALF

    def forward(query_block, buf):
        lay_out(query_block // blocks_here, query_block % blocks_here, buf)
        index = picks(query_block)
        s = dot_nt(gather(index, early, low), queries[buf])
        g = dot_nt(gather(index, early, high), grads[buf])
        x = dot_nt(gather(index, late, both_cols), crossed[buf])
        shift = shifts[query_block, 0][None]
        p = jnp.exp(s.reshape(early_rows // 8, 8, 2 * LANES) + shift).reshape(early_rows, 2 * LANES)
        prob[buf, :early_rows] = p
        slope[buf, :early_rows] = g
        delta = jnp.sum((p * g).reshape(early_rows // 8, 8, 2 * LANES), axis=0)
        late_shift = shifts[query_block, 1, :, low][None]
        q = jnp.exp(x[:, low].reshape(early_rows // 8, 8, LANES) + late_shift).reshape(
            early_rows, LANES
        )
        prob[buf, early_rows:, low] = q
        slope[buf, early_rows:, low] = x[:, high]
        more = jnp.sum((q * x[:, high]).reshape(early_rows // 8, 8, LANES), axis=0)
        delta_low = jnp.sum(delta[:, low], axis=0, keepdims=True)
        delta_high = jnp.sum(delta[:, high] + more, axis=0, keepdims=True)
        return jnp.concatenate([delta_low, delta_high], axis=1)

    def backward(query_block, buf, delta):
        index = picks(query_block)
        p = prob[buf, :early_rows]
        ds = (p * (slope[buf, :early_rows] - delta)).astype(BF16)
        q = prob[buf, early_rows:, low]
        ds_late = (q * (slope[buf, early_rows:, low] - delta[:, high])).astype(BF16)
        dk = dot(ds, queries[buf])
        dv = dot(p.astype(BF16), grads[buf])
        r = dot(jnp.concatenate([ds_late, q.astype(BF16)], axis=1), crossed[buf])
        nothing = jnp.zeros((HALF, LANES), BF16)
        pieces = []
        for s in range(slot_count):
            at = slice(s * HALF, (s + 1) * HALF)
            where = index[s]
            acc[where, early, low] = acc[where, early, low] + dk[at]
            acc[where, early, high] = acc[where, early, high] + dv[at]
            acc[where, late] = acc[where, late] + r[at]
            pieces.append(ds[at])
            pieces.append(jnp.concatenate([nothing, ds_late[at]], axis=1))
        keys_turned = jnp.concatenate([k_turn[i] for i in index], axis=1)
        dq = dot(keys_turned, jnp.concatenate(pieces, axis=0)) * scale
        halves = []
        for cols in (low, high):
            turned = dq[:, cols].T
            halves.append(jnp.where(head_a, turned[:HALF], turned[HALF:]))
        moved = dot(unorder, jnp.concatenate(halves, axis=0).astype(BF16)).astype(BF16)
        local = pl.multiple_of((query_block % blocks_here) * BLOCK, BLOCK)
        dq_all[query_block // blocks_here, pl.ds(local, BLOCK)] = moved

    def block_of(j):
        if last:
            return j + OUTER
        return j + jnp.where(j < OUTER, 0, group_blocks - 2 * OUTER)

    count = group_blocks - 2 * OUTER if last else 2 * OUTER
    delta = forward(block_of(0), 0)

    def step(j, delta):
        later = forward(block_of(2 * j + 1), 1)
        backward(block_of(2 * j), 0, delta)
        following = forward(block_of(2 * j + 2), 0)
        backward(block_of(2 * j + 1), 1, later)
        return following

    delta = lax.fori_loop(0, (count - 1) // 2, step, delta)
    if count % 2 == 0:
        later = forward(block_of(count - 1), 1)
        backward(block_of(count - 2), 0, delta)
        backward(block_of(count - 1), 1, later)
    else:
        backward(block_of(count - 1), 0, delta)

    groups = BLOCK // 16

    def in_token_order(part):
        blocks = part.shape[0]
        part = part.reshape(blocks, 2, groups, 8, 2 * LANES)
        return jnp.swapaxes(part, 1, 2).reshape(blocks, BLOCK, 2 * LANES)

    if last:
        acc[OUTER : window - OUTER] = acc[OUTER : window - OUTER] + before[...]
        top = window - SPAN
        for out, side in ((first_out, 1 - odd), (second_out, odd)):
            start = OUTER + side * (top - OUTER)
            out[...] = in_token_order(acc[pl.ds(start, OUTER)]).astype(BF16)
        own_out[...] = in_token_order(acc[SPAN : SPAN + group_blocks])
        send_pieces(dq_outs, dq_all)
    else:
        for out, side in ((first_out, 1 - odd), (second_out, odd)):
            start = side * (window - OUTER)
            out[...] = in_token_order(acc[pl.ds(start, OUTER)]).astype(BF16)
        kept_out[...] = acc[OUTER : window - OUTER]


def owner_start(piece, half):
    heads = lax.axis_size("head")
    return pl.multiple_of(((lax.axis_index("head") + 1 + piece) % heads) * half, half)


def add_arrived(total, starts, refs):
    level = lax.axis_index("var") // GROUP
    levels = lax.axis_size("var") // GROUP
    odd = below_first()
    for side, ref in zip((1 - odd, odd), refs):
        other = level - 1 + 2 * side
        start = jnp.where(side == 1, starts[1], starts[0])

        @pl.when((other >= 0) & (other < levels))
        def _(start=start, ref=ref):
            at = pl.ds(start, OUTER)
            total[at] = total[at] + ref[...].astype(F32)


def combine_outer_kernel(carried, own_ref, first_ref, second_ref, *refs):
    total = refs[carried]
    total[...] = own_ref[...]
    add_arrived(total, (SPAN - OUTER, own_ref.shape[0] - SPAN), (first_ref, second_ref))


def combine_kernel(own_ref, first_ref, second_ref, *rest):
    aways, homes, (total, moved) = rest[:GROUP], rest[GROUP : 2 * GROUP], rest[2 * GROUP :]
    total[...] = own_ref[...]
    add_arrived(total, (0, own_ref.shape[0] - OUTER), (first_ref, second_ref))
    moved[...] = total[...].astype(BF16).reshape(moved.shape)
    half = homes[0].shape[0]
    away = aways[0].shape[0] // half
    me = lax.axis_index("var") % GROUP
    for distance in range(GROUP):
        member = me ^ distance
        for piece in range(away):
            aways[distance][piece * half : (piece + 1) * half] = moved[
                member, pl.ds(owner_start(piece, half), half)
            ]
        homes[distance][...] = moved[member, pl.ds(owner_start(away, half), half)]


def gather_rows(grads, dq, start, dkv, dkv_at):
    half = grads.shape[1]
    width = grads.shape[2] // GROUP
    for member in range(GROUP):
        at = slice(member * width, (member + 1) * width)
        both = dkv[member, dkv_at * half : (dkv_at + 1) * half]
        grads[0, :, at] = dq[member, pl.ds(start, half)][:, :width]
        grads[1, :, at] = both[:, :width]
        grads[2, :, at] = both[:, LANES : LANES + width]


def product(grads, w_ref):
    total = dot_nt(grads[0], w_ref[0])
    for s in (1, 2):
        total = total + dot_nt(grads[s], w_ref[s])
    return total


def away_kernel(*refs):
    dqs, dkvs, (w_ref, *rest) = refs[:4], refs[4:8], refs[8:]
    outs, (grads, dq, dkv) = rest[:-3], rest[-3:]
    half = grads.shape[1]
    stage_pieces(dq, dqs)
    stage_pieces(dkv, dkvs)
    for piece, out in enumerate(outs):
        gather_rows(grads, dq, owner_start(piece, half), dkv, piece)
        out[...] = product(grads, w_ref).astype(BF16)


def home_kernel(*refs):
    dqs, aways, homes, rest = refs[:4], refs[4:8], refs[8:12], refs[12:]
    w_ref, dq_out, dk_out, dv_out, keep_out, grads, dq, away_dkv, home_dkv = rest
    half = grads.shape[1]
    away = away_dkv.shape[1] // half
    stage_pieces(dq, dqs)
    stage_pieces(away_dkv, aways)
    stage_pieces(home_dkv, homes)
    for piece in range(away + 1):
        start = owner_start(piece, half)
        if piece < away:
            gather_rows(grads, dq, start, away_dkv, piece)
        else:
            gather_rows(grads, dq, start, home_dkv, 0)
        at = pl.ds(start, half)
        dq_out[at] = grads[0]
        dk_out[at] = grads[1]
        dv_out[at] = grads[2]
    keep_out[...] = product(grads, w_ref)


def body(queries, keys, values, out_grad, log_sum_exp, key_blocks, w_qkv):
    rows, features = queries.shape
    head_count = log_sum_exp.shape[0]
    head_dim = features // head_count
    slots = head_count // GROUP
    blocks_here = rows // BLOCK
    group_blocks = GROUP * blocks_here
    window = group_blocks + 2 * SPAN
    slot_count = key_blocks.shape[1]
    devices = lax.axis_size("var")
    heads = lax.axis_size("head")
    half = rows // heads
    model = w_qkv.shape[1]
    wide = 2 * LANES
    hbm = pl.BlockSpec(memory_space=pltpu.HBM)

    def trade(x, distance):
        return lax.ppermute(x, "var", [(n, n ^ distance) for n in range(devices)])

    def trade_level(x, turn):
        pairs = []
        for n in range(devices):
            other = n - GROUP if (n // GROUP + n + turn) % 2 else n + GROUP
            for h in range(heads):
                if 0 <= other < devices:
                    target = other * heads + h
                else:
                    target = n * heads + (h ^ 1) % heads
                pairs.append((n * heads + h, target))
        return lax.ppermute(x, ("var", "head"), pairs)

    def trade_first(x):
        return trade_level(x, 0)

    def trade_second(x):
        return trade_level(x, 1)

    def swap(pieces):
        got = [pieces[0]] + [None] * (GROUP - 1)
        for distance in (2, 3, 1):
            got[distance] = trade(pieces[distance], distance)
        return got

    def staged(count, width=LANES):
        return pltpu.VMEM((GROUP, count, width), BF16)

    block = (BLOCK, LANES)
    anywhere = pl.BlockSpec(memory_space=pl.ANY)

    def cost(flops, moved):
        return pl.CostEstimate(flops=flops, bytes_accessed=moved, transcendentals=0)

    size = rows * features * 2

    kvs = pl.pallas_call(
        pack_kv_kernel,
        out_shape=(shaped((rows, wide)),) * GROUP,
        in_specs=[hbm] * 2,
        out_specs=(vmem(),) * GROUP,
        scratch_shapes=[pltpu.VMEM((rows, features), BF16)] * 2
        + [staged(rows, wide), pltpu.SemaphoreType.DMA((2, LOADS))],
        compiler_params=params(PACK_MIB),
        cost_estimate=cost(4 * rows * features * BLOCK, 5 * size),
    )(keys, values)
    kvs = swap(kvs)
    *qos, kvs[0] = pl.pallas_call(
        functools.partial(pack_qo_kernel, slots, head_dim),
        out_shape=(shaped((rows + LSE_ROWS, wide)),) * GROUP + (shaped((rows, wide)),),
        in_specs=[vmem()] * 4 + [anywhere],
        out_specs=(vmem(),) * (GROUP + 1),
        scratch_shapes=[staged(rows + LSE_ROWS, wide)],
        compiler_params=params(8),
        cost_estimate=cost(4 * rows * features * BLOCK, 10 * size),
    )(queries, out_grad, log_sum_exp, kvs[0], kvs[1])
    carried = tuple(qos[1:])
    own, first, second, *carried = pl.pallas_call(
        functools.partial(line_kernel, len(carried)),
        out_shape=(shaped((GROUP * rows + rows + LSE_ROWS, wide)),)
        + (shaped((SPAN * BLOCK, wide)),) * 2
        + tuple(shaped(x.shape) for x in carried),
        in_specs=[vmem()] * (GROUP + 1) + [anywhere] * len(carried),
        out_specs=(vmem(),) * 3 + (anywhere,) * len(carried),
        input_output_aliases={GROUP + 1 + i: 3 + i for i in range(len(carried))},
        compiler_params=params(8),
        cost_estimate=cost(0, 5 * size),
    )(*kvs, qos[0], *carried)
    first = trade_first(first)
    second = trade_second(second)
    qos = swap([None, *carried])[1:]

    pairs = group_blocks * slot_count * BLOCK * BLOCK * slots
    tall = (BLOCK, wide)
    acc_scratch = pltpu.VMEM((window,) + tall, F32)
    work = [
        pltpu.VMEM((2, wide, LANES), BF16),
        pltpu.VMEM((2, wide, LANES), BF16),
        pltpu.VMEM((2, wide, wide), BF16),
        pltpu.VMEM((2, slot_count * BLOCK, wide), F32),
        pltpu.VMEM((2, slot_count * BLOCK, wide), F32),
    ]
    smem = pl.BlockSpec(memory_space=pltpu.SMEM)
    outer = (shaped((OUTER,) + tall),) * 2

    def attend_cost(part):
        return pl.CostEstimate(
            flops=int(40 * pairs * head_dim * part),
            bytes_accessed=2_000_000,
            transcendentals=int(pairs * part),
        )

    state = (
        shaped((window,) + tall),
        shaped((window, LANES, BLOCK)),
        shaped((group_blocks, 2, 8, wide), F32),
        shaped((GROUP, rows + LSE_ROWS, wide)),
        shaped((window - 2 * OUTER,) + tall, F32),
        shaped((GROUP, rows, LANES)),
    )
    first, second, *state = pl.pallas_call(
        functools.partial(attend_kernel, False, blocks_here, head_dim),
        out_shape=outer + state,
        in_specs=[smem] + [vmem()] * (2 + GROUP),
        out_specs=(vmem(),) * 8,
        scratch_shapes=[acc_scratch] + work,
        compiler_params=params(24),
        cost_estimate=attend_cost(0.67),
    )(key_blocks, own, first, second, *qos)
    outer_back = (trade_first(first), trade_second(second))
    own_sum, first, second, *dqs = pl.pallas_call(
        functools.partial(attend_kernel, True, blocks_here, head_dim),
        out_shape=(shaped((group_blocks,) + tall, F32),)
        + outer
        + (shaped((rows, LANES)),) * GROUP,
        in_specs=[smem] + [vmem()] * 6,
        out_specs=(vmem(),) * (3 + GROUP),
        scratch_shapes=[acc_scratch] + work + [staged(rows)],
        compiler_params=params(24),
        cost_estimate=attend_cost(0.33),
    )(key_blocks, *state)
    inner_back = (trade_first(first), trade_second(second))
    carried = tuple(dqs[1:])
    *carried, own_sum = pl.pallas_call(
        functools.partial(combine_outer_kernel, 2 * len(carried)),
        out_shape=tuple(shaped(x.shape) for x in carried) + (shaped((group_blocks,) + tall, F32),),
        in_specs=[vmem()] * 3 + [anywhere] * len(carried),
        out_specs=(anywhere,) * len(carried) + (vmem(),),
        input_output_aliases={3 + i: i for i in range(len(carried))},
        compiler_params=params(8),
        cost_estimate=cost(0, 4 * size),
    )(own_sum, *outer_back, *carried)
    dqs = swap([dqs[0], *carried])
    split = pl.pallas_call(
        combine_kernel,
        out_shape=(shaped((rows - half, wide)),) * GROUP + (shaped((half, wide)),) * GROUP,
        in_specs=[vmem()] * 3,
        out_specs=(vmem(),) * (2 * GROUP),
        scratch_shapes=[pltpu.VMEM((group_blocks,) + tall, F32), staged(rows, wide)],
        compiler_params=params(8),
        cost_estimate=cost(0, 8 * size),
    )(own_sum, *inner_back)
    aways = swap(split[:GROUP])
    homes = swap(split[GROUP:])

    grads = pltpu.VMEM((3, half, features), BF16)
    sends = pl.pallas_call(
        away_kernel,
        out_shape=(shaped((half, model)),) * (heads - 1),
        in_specs=[vmem()] * (2 * GROUP + 1),
        out_specs=(vmem(),) * (heads - 1),
        scratch_shapes=[grads, staged(rows), staged(rows - half, wide)],
        compiler_params=params(12),
        cost_estimate=cost(6 * (rows - half) * features * model, 4_000_000),
    )(*dqs, *aways, w_qkv)
    dq_out, dk_out, dv_out, total = pl.pallas_call(
        home_kernel,
        out_shape=(shaped((rows, features)),) * 3 + (shaped((half, model), F32),),
        in_specs=[vmem()] * (3 * GROUP + 1),
        out_specs=(vmem(),) * 4,
        scratch_shapes=[grads, staged(rows), staged(rows - half, wide), staged(half, wide)],
        compiler_params=params(12),
        cost_estimate=cost(6 * half * features * model, 6_000_000),
    )(*dqs, *aways, *homes, w_qkv)
    for piece, send in enumerate(sends):
        got = lax.ppermute(send, "head", [(n, (n + piece + 1) % heads) for n in range(heads)])
        total = total + got.astype(F32)
    return dq_out, dk_out, dv_out, total.astype(BF16)


def solution(mesh):
    in_specs = (
        P("var", "head"),
        P("var", "head"),
        P("var", "head"),
        P("var", "head"),
        P("head", "var"),
        P(),
        P(None, None, "head"),
    )
    out_specs = (P("var", "head"), P("var", "head"), P("var", "head"), P(("var", "head"), None))
    return jax.shard_map(body, mesh=mesh, in_specs=in_specs, out_specs=out_specs, check_vma=False)
```

```python
import functools

import jax
import jax.numpy as jnp
from jax import lax
from jax.experimental import pallas as pl
from jax.experimental.pallas import tpu as pltpu
from jax.sharding import PartitionSpec as P

PATCHES = 16
BLOCK = 128
HALF = BLOCK // 2
SPAN = 8
OUTER = SPAN // 2
GROUP = 4
LANES = 128
LSE_ROWS = 16
PARTS = 2
LOADS = 3
F32 = jnp.float32
BF16 = jnp.bfloat16
MIB = 1024 * 1024
PACK_MIB = 62


def vmem():
    return pl.BlockSpec(memory_space=pltpu.VMEM)


def params(mib):
    return pltpu.CompilerParams(vmem_limit_bytes=mib * MIB)


def shaped(shape, dtype=BF16):
    return jax.ShapeDtypeStruct(shape, dtype)


def dot(a, b):
    return jnp.dot(a, b, preferred_element_type=F32)


def dot_nt(a, b):
    return lax.dot_general(a, b, (((1,), (1,)), ((), ())), preferred_element_type=F32)


def token_at(place):
    return (((place & (HALF - 1)) >> 3) << 4) + ((place >> 6) << 3) + (place & 7)


def one_where(mask):
    return jnp.where(mask, 1.0, 0.0).astype(BF16)


def reorder_matrix(inverse):
    row = lax.broadcasted_iota(jnp.int32, (BLOCK, BLOCK), 0)
    col = lax.broadcasted_iota(jnp.int32, (BLOCK, BLOCK), 1)
    return one_where(row == token_at(col)) if inverse else one_where(col == token_at(row))


def split_three(x):
    high = x.astype(BF16).astype(F32)
    rest = x - high
    mid = rest.astype(BF16).astype(F32)
    return high, mid, rest - mid


def widen(x):
    if x.shape[1] == LANES:
        return x
    return jnp.concatenate([x, jnp.zeros((x.shape[0], LANES - x.shape[1]), x.dtype)], axis=1)


def send_pieces(outs, stage):
    me = lax.axis_index("var") % GROUP
    for distance, out in enumerate(outs):
        out[...] = stage[me ^ distance]


def stage_pieces(stage, pieces):
    me = lax.axis_index("var") % GROUP
    for distance, piece in enumerate(pieces):
        stage[me ^ distance] = piece[...]


def load_all(pairs, sems):
    copies = []
    for i, (source, target) in enumerate(pairs):
        rows = source.shape[0] // LOADS
        for part in range(LOADS):
            at = pl.ds(part * rows, rows)
            copies.append(pltpu.make_async_copy(source.at[at], target.at[at], sems.at[i, part]))
    for copy in copies:
        copy.start()
    return [copies[i * LOADS : (i + 1) * LOADS] for i in range(len(pairs))]


def reorder_into(staged, half, ref, scale=None):
    rows, features = ref.shape
    width = features // GROUP
    order = reorder_matrix(False)
    for b in range(rows // BLOCK):
        at = slice(b * BLOCK, (b + 1) * BLOCK)
        moved = dot(order, ref[at])
        if scale is not None:
            moved = moved * scale
        moved = moved.astype(BF16)
        for member in range(GROUP):
            staged[member, at, half * LANES : (half + 1) * LANES] = widen(
                moved[:, member * width : (member + 1) * width]
            )


def pack_kv_kernel(k_hbm, v_hbm, *rest):
    outs, (k_ref, v_ref, turned, sems) = rest[:GROUP], rest[GROUP:]
    arrivals = load_all([(k_hbm, k_ref), (v_hbm, v_ref)], sems)
    for half, ref in enumerate((k_ref, v_ref)):
        for copy in arrivals[half]:
            copy.wait()
        reorder_into(turned, half, ref)
    send_pieces(outs, turned)


def pack_qo_kernel(slots, head_dim, q_ref, g_ref, lse_ref, mine_ref, after_ref, *rest):
    outs, (hold, qo_ref) = rest[:GROUP], rest[GROUP:]
    hold[...] = mine_ref[...]
    rows = q_ref.shape[0]
    blocks = rows // BLOCK
    reorder_into(qo_ref, 0, q_ref, head_dim ** (-0.5))
    reorder_into(qo_ref, 1, g_ref)
    token = lax.broadcasted_iota(jnp.int32, (BLOCK, 2 * LANES), 0)
    lane = lax.broadcasted_iota(jnp.int32, (BLOCK, 2 * LANES), 1)
    place = ((lane >> 7) << 6) + (lane & (HALF - 1))
    hit = token == token_at(place)
    upper = (lane & HALF) != 0
    spread = [one_where(hit & ~upper), one_where(hit & upper)]
    for member in range(GROUP):
        total = None
        for slot in range(slots):
            lse = lse_ref[member * slots + slot : member * slots + slot + 1, :]
            parts = [
                part[:, b * BLOCK : (b + 1) * BLOCK]
                for part in split_three(lse)
                for b in range(blocks)
            ]
            parts.append(jnp.zeros((LSE_ROWS - len(parts), BLOCK), F32))
            moved = dot(jnp.concatenate(parts, axis=0).astype(BF16), spread[slot])
            total = moved if total is None else total + moved
        qo_ref[member, rows:] = total.astype(BF16)
    send_pieces(outs, qo_ref)


def below_first():
    me = lax.axis_index("var")
    return (me // GROUP + me) % 2


def exchange_start(group_blocks):
    odd = below_first()
    reach = group_blocks - SPAN
    return (1 - odd) * reach, odd * reach


def line_kernel(carried, *refs):
    pieces, query_piece, refs = refs[:GROUP], refs[GROUP], refs[GROUP + 1 + carried :]
    own, first_out, second_out = refs[:3]
    rows = pieces[0].shape[0]
    own[GROUP * rows :] = query_piece[...]
    blocks = rows // BLOCK
    me = lax.axis_index("var") % GROUP
    for distance in range(GROUP):
        at = pl.ds(pl.multiple_of((me ^ distance) * rows, rows), rows)
        own[at] = pieces[distance][...]
    first, second = exchange_start(GROUP * blocks)
    for start, out in ((first, first_out), (second, second_out)):
        out[...] = own[pl.ds(pl.multiple_of(start * BLOCK, BLOCK), SPAN * BLOCK)]


def attend_kernel(last, blocks_here, head_dim, kb_ref, *refs):
    if last:
        kv_win, k_turn, shifts, qo_ref, before, dq_before, *refs = refs
        own_out, first_out, second_out, *refs = refs
        dq_outs, refs = refs[:GROUP], refs[GROUP:]
        acc, queries, grads, crossed, prob, slope, dq_all = refs
    else:
        kv_refs, refs = refs[:3], refs[3:]
        qo_pieces, refs = refs[: GROUP - 1], refs[GROUP - 1 :]
        first_out, second_out, kv_win, k_turn, shifts, qo_ref, kept_out, dq_all, *refs = refs
        acc, queries, grads, crossed, prob, slope = refs
    group_blocks = GROUP * blocks_here
    window = group_blocks + 2 * SPAN
    rows = blocks_here * BLOCK
    slot_count = kb_ref.shape[1]
    scale = head_dim ** (-0.5)
    base = (lax.axis_index("var") // GROUP) * group_blocks
    odd = below_first()
    low = slice(0, LANES)
    high = slice(LANES, 2 * LANES)

    acc[...] = jnp.zeros_like(acc)
    crossed[...] = jnp.zeros_like(crossed)
    if last:
        dq_all[...] = dq_before[...]
    else:
        top = window - SPAN
        for ref, start, count in zip(
            kv_refs, (SPAN, (1 - odd) * top, odd * top), (group_blocks, SPAN, SPAN)
        ):
            kv_win[pl.ds(start, count)] = ref[: count * BLOCK].reshape(count, BLOCK, 2 * LANES)
        own_queries = kv_refs[0].at[pl.ds(group_blocks * BLOCK, rows + LSE_ROWS)]
        stage_pieces(qo_ref, (own_queries, *qo_pieces))
        key_patch = lax.broadcasted_iota(jnp.int32, (8, LANES), 0)
        query_patch = lax.broadcasted_iota(jnp.int32, (8, LANES), 1) & 7
        usable = key_patch <= query_patch
        for member in range(GROUP):
            parts = qo_ref[member, rows:].astype(F32)
            for local in range(blocks_here):
                lse = (
                    parts[local : local + 1] + parts[blocks_here + local : blocks_here + local + 1]
                ) + parts[2 * blocks_here + local : 2 * blocks_here + local + 1]
                at = member * blocks_here + local
                shifts[at, 0, :, low] = jnp.where(usable, -lse[:, low], -1e30)
                shifts[at, 0, :, high] = jnp.broadcast_to(-lse[:, high], (8, LANES))
                shifts[at, 1, :, low] = jnp.where(usable, -lse[:, high], -1e30)

        @pl.loop(0, window)
        def _(block):
            k_turn[block] = kv_win[block, :, low].T

    unorder = reorder_matrix(True)
    lane = lax.broadcasted_iota(jnp.int32, (HALF, LANES), 1)
    head_a = lane < HALF

    def picks(query_block):
        return [kb_ref[base + query_block, s] - base + SPAN for s in range(slot_count)]

    def lay_out(member, local, buf):
        at = pl.multiple_of(local * BLOCK, BLOCK)
        for part in range(2):
            rows_at = pl.ds(at + part * HALF, HALF)
            for cols, target in ((low, queries), (high, grads)):
                tile = qo_ref[member, rows_at, cols]
                zero = jnp.zeros_like(tile)
                both = jnp.concatenate(
                    [jnp.where(head_a, tile, zero), jnp.where(head_a, zero, tile)], axis=0
                )
                target[buf, part * BLOCK : (part + 1) * BLOCK] = both
                if part == 1:
                    side = 0 if target is queries else 1
                    crossed[
                        buf, side * BLOCK : (side + 1) * BLOCK, side * LANES : (side + 1) * LANES
                    ] = both

    def gather(index, rows_of, cols):
        return jnp.concatenate([kv_win[i, rows_of, cols] for i in index], axis=0)

    early = slice(0, HALF)
    late = slice(HALF, BLOCK)
    both_cols = slice(0, 2 * LANES)
    early_rows = slot_count * HALF
    part_slots = slot_count // PARTS
    part_rows = part_slots * HALF

    def forward_part(index, query_block, buf, part):
        some = index[part * part_slots : (part + 1) * part_slots]
        at = slice(part * part_rows, (part + 1) * part_rows)
        after = slice(early_rows + part * part_rows, early_rows + (part + 1) * part_rows)
        s = dot_nt(gather(some, early, low), queries[buf])
        g = dot_nt(gather(some, early, high), grads[buf])
        x = dot_nt(gather(some, late, both_cols), crossed[buf])
        shift = shifts[query_block, 0][None]
        p = jnp.exp(s.reshape(part_rows // 8, 8, 2 * LANES) + shift).reshape(part_rows, 2 * LANES)
        prob[buf, at] = p
        slope[buf, at] = g
        delta = jnp.sum((p * g).reshape(part_rows // 8, 8, 2 * LANES), axis=0)
        late_shift = shifts[query_block, 1, :, low][None]
        q = jnp.exp(x[:, low].reshape(part_rows // 8, 8, LANES) + late_shift).reshape(
            part_rows, LANES
        )
        prob[buf, after, low] = q
        slope[buf, after, low] = x[:, high]
        more = jnp.sum((q * x[:, high]).reshape(part_rows // 8, 8, LANES), axis=0)
        return delta[:, low], delta[:, high] + more

    def backward_part(index, buf, delta, part):
        at = slice(part * part_rows, (part + 1) * part_rows)
        after = slice(early_rows + part * part_rows, early_rows + (part + 1) * part_rows)
        p = prob[buf, at]
        ds = (p * (slope[buf, at] - delta)).astype(BF16)
        q = prob[buf, after, low]
        ds_late = (q * (slope[buf, after, low] - delta[:, high])).astype(BF16)
        dk = dot(ds, queries[buf])
        dv = dot(p.astype(BF16), grads[buf])
        r = dot(jnp.concatenate([ds_late, q.astype(BF16)], axis=1), crossed[buf])
        nothing = jnp.zeros((HALF, LANES), BF16)
        pieces = []
        for s in range(part_slots):
            at = slice(s * HALF, (s + 1) * HALF)
            where = index[part * part_slots + s]
            acc[where, early, low] = acc[where, early, low] + dk[at]
            acc[where, early, high] = acc[where, early, high] + dv[at]
            acc[where, late] = acc[where, late] + r[at]
            pieces.append(ds[at])
            pieces.append(jnp.concatenate([nothing, ds_late[at]], axis=1))
        keys_turned = jnp.concatenate(
            [k_turn[i] for i in index[part * part_slots : (part + 1) * part_slots]], axis=1
        )
        return dot(keys_turned, jnp.concatenate(pieces, axis=0))

    def write_dq(query_block, dq):
        dq = dq * scale
        halves = []
        for cols in (low, high):
            turned = dq[:, cols].T
            halves.append(jnp.where(head_a, turned[:HALF], turned[HALF:]))
        moved = dot(unorder, jnp.concatenate(halves, axis=0).astype(BF16)).astype(BF16)
        local = pl.multiple_of((query_block % blocks_here) * BLOCK, BLOCK)
        dq_all[query_block // blocks_here, pl.ds(local, BLOCK)] = moved

    def run(ahead, ahead_buf, behind, behind_buf, delta):
        sums, dq = None, None
        if ahead is not None:
            lay_out(ahead // blocks_here, ahead % blocks_here, ahead_buf)
            ahead_index = picks(ahead)
        if behind is not None:
            behind_index = picks(behind)
        for part in range(PARTS):
            if ahead is not None:
                more = forward_part(ahead_index, ahead, ahead_buf, part)
                sums = more if sums is None else (sums[0] + more[0], sums[1] + more[1])
            if behind is not None:
                more = backward_part(behind_index, behind_buf, delta, part)
                dq = more if dq is None else dq + more
        if behind is not None:
            write_dq(behind, dq)
        if ahead is None:
            return None
        return jnp.concatenate([jnp.sum(x, axis=0, keepdims=True) for x in sums], axis=1)

    def block_of(j):
        if last:
            return j + OUTER
        return j + jnp.where(j < OUTER, 0, group_blocks - 2 * OUTER)

    count = group_blocks - 2 * OUTER if last else 2 * OUTER
    delta = run(block_of(0), 0, None, None, None)

    def step(j, delta):
        delta = run(block_of(2 * j + 1), 1, block_of(2 * j), 0, delta)
        return run(block_of(2 * j + 2), 0, block_of(2 * j + 1), 1, delta)

    delta = lax.fori_loop(0, (count - 1) // 2, step, delta)
    if count % 2 == 0:
        delta = run(block_of(count - 1), 1, block_of(count - 2), 0, delta)
    run(None, None, block_of(count - 1), (count - 1) % 2, delta)

    groups = BLOCK // 16

    def in_token_order(part):
        blocks = part.shape[0]
        part = part.reshape(blocks, 2, groups, 8, 2 * LANES)
        return jnp.swapaxes(part, 1, 2).reshape(blocks, BLOCK, 2 * LANES)

    if last:
        acc[OUTER : window - OUTER] = acc[OUTER : window - OUTER] + before[...]
        top = window - SPAN
        for out, side in ((first_out, 1 - odd), (second_out, odd)):
            start = OUTER + side * (top - OUTER)
            out[...] = in_token_order(acc[pl.ds(start, OUTER)]).astype(BF16)
        own_out[...] = in_token_order(acc[SPAN : SPAN + group_blocks])
        send_pieces(dq_outs, dq_all)
    else:
        for out, side in ((first_out, 1 - odd), (second_out, odd)):
            start = side * (window - OUTER)
            out[...] = in_token_order(acc[pl.ds(start, OUTER)]).astype(BF16)
        kept_out[...] = acc[OUTER : window - OUTER]


def owner_start(piece, half):
    heads = lax.axis_size("head")
    return pl.multiple_of(((lax.axis_index("head") + 1 + piece) % heads) * half, half)


def add_arrived(total, starts, refs):
    level = lax.axis_index("var") // GROUP
    levels = lax.axis_size("var") // GROUP
    odd = below_first()
    for side, ref in zip((1 - odd, odd), refs):
        other = level - 1 + 2 * side
        start = jnp.where(side == 1, starts[1], starts[0])

        @pl.when((other >= 0) & (other < levels))
        def _(start=start, ref=ref):
            at = pl.ds(start, OUTER)
            total[at] = total[at] + ref[...].astype(F32)


def combine_outer_kernel(carried, own_ref, first_ref, second_ref, *refs):
    total = refs[carried]
    total[...] = own_ref[...]
    add_arrived(total, (SPAN - OUTER, own_ref.shape[0] - SPAN), (first_ref, second_ref))


def combine_kernel(own_ref, first_ref, second_ref, *rest):
    aways, homes, (total, moved) = rest[:GROUP], rest[GROUP : 2 * GROUP], rest[2 * GROUP :]
    total[...] = own_ref[...]
    add_arrived(total, (0, own_ref.shape[0] - OUTER), (first_ref, second_ref))
    moved[...] = total[...].astype(BF16).reshape(moved.shape)
    half = homes[0].shape[0]
    away = aways[0].shape[0] // half
    me = lax.axis_index("var") % GROUP
    for distance in range(GROUP):
        member = me ^ distance
        for piece in range(away):
            aways[distance][piece * half : (piece + 1) * half] = moved[
                member, pl.ds(owner_start(piece, half), half)
            ]
        homes[distance][...] = moved[member, pl.ds(owner_start(away, half), half)]


def gather_rows(grads, dq, start, dkv, dkv_at):
    half = grads.shape[1]
    width = grads.shape[2] // GROUP
    for member in range(GROUP):
        at = slice(member * width, (member + 1) * width)
        both = dkv[member, dkv_at * half : (dkv_at + 1) * half]
        grads[0, :, at] = dq[member, pl.ds(start, half)][:, :width]
        grads[1, :, at] = both[:, :width]
        grads[2, :, at] = both[:, LANES : LANES + width]


def product(grads, w_ref):
    total = dot_nt(grads[0], w_ref[0])
    for s in (1, 2):
        total = total + dot_nt(grads[s], w_ref[s])
    return total


def away_kernel(*refs):
    dqs, dkvs, (w_ref, *rest) = refs[:4], refs[4:8], refs[8:]
    outs, (grads, dq, dkv) = rest[:-3], rest[-3:]
    half = grads.shape[1]
    stage_pieces(dq, dqs)
    stage_pieces(dkv, dkvs)
    for piece, out in enumerate(outs):
        gather_rows(grads, dq, owner_start(piece, half), dkv, piece)
        out[...] = product(grads, w_ref).astype(BF16)


def home_kernel(*refs):
    dqs, aways, homes, rest = refs[:4], refs[4:8], refs[8:12], refs[12:]
    w_ref, dq_out, dk_out, dv_out, keep_out, grads, dq, away_dkv, home_dkv = rest
    half = grads.shape[1]
    away = away_dkv.shape[1] // half
    stage_pieces(dq, dqs)
    stage_pieces(away_dkv, aways)
    stage_pieces(home_dkv, homes)
    for piece in range(away + 1):
        start = owner_start(piece, half)
        if piece < away:
            gather_rows(grads, dq, start, away_dkv, piece)
        else:
            gather_rows(grads, dq, start, home_dkv, 0)
        at = pl.ds(start, half)
        dq_out[at] = grads[0]
        dk_out[at] = grads[1]
        dv_out[at] = grads[2]
    keep_out[...] = product(grads, w_ref)


def body(queries, keys, values, out_grad, log_sum_exp, key_blocks, w_qkv):
    rows, features = queries.shape
    head_count = log_sum_exp.shape[0]
    head_dim = features // head_count
    slots = head_count // GROUP
    blocks_here = rows // BLOCK
    group_blocks = GROUP * blocks_here
    window = group_blocks + 2 * SPAN
    slot_count = key_blocks.shape[1]
    devices = lax.axis_size("var")
    heads = lax.axis_size("head")
    half = rows // heads
    model = w_qkv.shape[1]
    wide = 2 * LANES
    hbm = pl.BlockSpec(memory_space=pltpu.HBM)

    def trade(x, distance):
        return lax.ppermute(x, "var", [(n, n ^ distance) for n in range(devices)])

    def trade_level(x, turn):
        pairs = []
        for n in range(devices):
            other = n - GROUP if (n // GROUP + n + turn) % 2 else n + GROUP
            for h in range(heads):
                if 0 <= other < devices:
                    target = other * heads + h
                else:
                    target = n * heads + (h ^ 1) % heads
                pairs.append((n * heads + h, target))
        return lax.ppermute(x, ("var", "head"), pairs)

    def trade_first(x):
        return trade_level(x, 0)

    def trade_second(x):
        return trade_level(x, 1)

    def swap(pieces):
        got = [pieces[0]] + [None] * (GROUP - 1)
        for distance in (2, 3, 1):
            got[distance] = trade(pieces[distance], distance)
        return got

    def staged(count, width=LANES):
        return pltpu.VMEM((GROUP, count, width), BF16)

    block = (BLOCK, LANES)
    anywhere = pl.BlockSpec(memory_space=pl.ANY)

    def cost(flops, moved):
        return pl.CostEstimate(flops=flops, bytes_accessed=moved, transcendentals=0)

    size = rows * features * 2

    kvs = pl.pallas_call(
        pack_kv_kernel,
        out_shape=(shaped((rows, wide)),) * GROUP,
        in_specs=[hbm] * 2,
        out_specs=(vmem(),) * GROUP,
        scratch_shapes=[pltpu.VMEM((rows, features), BF16)] * 2
        + [staged(rows, wide), pltpu.SemaphoreType.DMA((2, LOADS))],
        compiler_params=params(PACK_MIB),
        cost_estimate=cost(4 * rows * features * BLOCK, 5 * size),
    )(keys, values)
    kvs = swap(kvs)
    *qos, kvs[0] = pl.pallas_call(
        functools.partial(pack_qo_kernel, slots, head_dim),
        out_shape=(shaped((rows + LSE_ROWS, wide)),) * GROUP + (shaped((rows, wide)),),
        in_specs=[vmem()] * 4 + [anywhere],
        out_specs=(vmem(),) * (GROUP + 1),
        scratch_shapes=[staged(rows + LSE_ROWS, wide)],
        compiler_params=params(8),
        cost_estimate=cost(4 * rows * features * BLOCK, 10 * size),
    )(queries, out_grad, log_sum_exp, kvs[0], kvs[1])
    carried = tuple(qos[1:])
    own, first, second, *carried = pl.pallas_call(
        functools.partial(line_kernel, len(carried)),
        out_shape=(shaped((GROUP * rows + rows + LSE_ROWS, wide)),)
        + (shaped((SPAN * BLOCK, wide)),) * 2
        + tuple(shaped(x.shape) for x in carried),
        in_specs=[vmem()] * (GROUP + 1) + [anywhere] * len(carried),
        out_specs=(vmem(),) * 3 + (anywhere,) * len(carried),
        input_output_aliases={GROUP + 1 + i: 3 + i for i in range(len(carried))},
        compiler_params=params(8),
        cost_estimate=cost(0, 5 * size),
    )(*kvs, qos[0], *carried)
    first = trade_first(first)
    second = trade_second(second)
    qos = swap([None, *carried])[1:]

    pairs = group_blocks * slot_count * BLOCK * BLOCK * slots
    tall = (BLOCK, wide)
    acc_scratch = pltpu.VMEM((window,) + tall, F32)
    work = [
        pltpu.VMEM((2, wide, LANES), BF16),
        pltpu.VMEM((2, wide, LANES), BF16),
        pltpu.VMEM((2, wide, wide), BF16),
        pltpu.VMEM((2, slot_count * BLOCK, wide), F32),
        pltpu.VMEM((2, slot_count * BLOCK, wide), F32),
    ]
    smem = pl.BlockSpec(memory_space=pltpu.SMEM)
    outer = (shaped((OUTER,) + tall),) * 2

    def attend_cost(part):
        return pl.CostEstimate(
            flops=int(40 * pairs * head_dim * part),
            bytes_accessed=2_000_000,
            transcendentals=int(pairs * part),
        )

    state = (
        shaped((window,) + tall),
        shaped((window, LANES, BLOCK)),
        shaped((group_blocks, 2, 8, wide), F32),
        shaped((GROUP, rows + LSE_ROWS, wide)),
        shaped((window - 2 * OUTER,) + tall, F32),
        shaped((GROUP, rows, LANES)),
    )
    first, second, *state = pl.pallas_call(
        functools.partial(attend_kernel, False, blocks_here, head_dim),
        out_shape=outer + state,
        in_specs=[smem] + [vmem()] * (2 + GROUP),
        out_specs=(vmem(),) * 8,
        scratch_shapes=[acc_scratch] + work,
        compiler_params=params(16),
        cost_estimate=attend_cost(0.67),
    )(key_blocks, own, first, second, *qos)
    outer_back = (trade_first(first), trade_second(second))
    own_sum, first, second, *dqs = pl.pallas_call(
        functools.partial(attend_kernel, True, blocks_here, head_dim),
        out_shape=(shaped((group_blocks,) + tall, F32),)
        + outer
        + (shaped((rows, LANES)),) * GROUP,
        in_specs=[smem] + [vmem()] * 6,
        out_specs=(vmem(),) * (3 + GROUP),
        scratch_shapes=[acc_scratch] + work + [staged(rows)],
        compiler_params=params(16),
        cost_estimate=attend_cost(0.33),
    )(key_blocks, *state)
    inner_back = (trade_first(first), trade_second(second))
    carried = tuple(dqs[1:])
    *carried, own_sum = pl.pallas_call(
        functools.partial(combine_outer_kernel, 2 * len(carried)),
        out_shape=tuple(shaped(x.shape) for x in carried) + (shaped((group_blocks,) + tall, F32),),
        in_specs=[vmem()] * 3 + [anywhere] * len(carried),
        out_specs=(anywhere,) * len(carried) + (vmem(),),
        input_output_aliases={3 + i: i for i in range(len(carried))},
        compiler_params=params(8),
        cost_estimate=cost(0, 4 * size),
    )(own_sum, *outer_back, *carried)
    dqs = swap([dqs[0], *carried])
    split = pl.pallas_call(
        combine_kernel,
        out_shape=(shaped((rows - half, wide)),) * GROUP + (shaped((half, wide)),) * GROUP,
        in_specs=[vmem()] * 3,
        out_specs=(vmem(),) * (2 * GROUP),
        scratch_shapes=[pltpu.VMEM((group_blocks,) + tall, F32), staged(rows, wide)],
        compiler_params=params(8),
        cost_estimate=cost(0, 8 * size),
    )(own_sum, *inner_back)
    aways = swap(split[:GROUP])
    homes = swap(split[GROUP:])

    grads = pltpu.VMEM((3, half, features), BF16)
    sends = pl.pallas_call(
        away_kernel,
        out_shape=(shaped((half, model)),) * (heads - 1),
        in_specs=[vmem()] * (2 * GROUP + 1),
        out_specs=(vmem(),) * (heads - 1),
        scratch_shapes=[grads, staged(rows), staged(rows - half, wide)],
        compiler_params=params(8),
        cost_estimate=cost(6 * (rows - half) * features * model, 4_000_000),
    )(*dqs, *aways, w_qkv)
    dq_out, dk_out, dv_out, total = pl.pallas_call(
        home_kernel,
        out_shape=(shaped((rows, features)),) * 3 + (shaped((half, model), F32),),
        in_specs=[vmem()] * (3 * GROUP + 1),
        out_specs=(vmem(),) * 4,
        scratch_shapes=[grads, staged(rows), staged(rows - half, wide), staged(half, wide)],
        compiler_params=params(8),
        cost_estimate=cost(6 * half * features * model, 6_000_000),
    )(*dqs, *aways, *homes, w_qkv)
    for piece, send in enumerate(sends):
        got = lax.ppermute(send, "head", [(n, (n + piece + 1) % heads) for n in range(heads)])
        total = total + got.astype(F32)
    return dq_out, dk_out, dv_out, total.astype(BF16)


def solution(mesh):
    in_specs = (
        P("var", "head"),
        P("var", "head"),
        P("var", "head"),
        P("var", "head"),
        P("head", "var"),
        P(),
        P(None, None, "head"),
    )
    out_specs = (P("var", "head"), P("var", "head"), P("var", "head"), P(("var", "head"), None))
    return jax.shard_map(body, mesh=mesh, in_specs=in_specs, out_specs=out_specs, check_vma=False)
```

```python
import functools

import jax
import jax.numpy as jnp
from jax import lax
from jax.experimental import pallas as pl
from jax.experimental.pallas import tpu as pltpu
from jax.sharding import PartitionSpec as P

PATCHES = 16
BLOCK = 128
HALF = BLOCK // 2
SPAN = 8
OUTER = SPAN // 2
GROUP = 4
LANES = 128
LSE_ROWS = 16
PARTS = 2
LOADS = 3
F32 = jnp.float32
BF16 = jnp.bfloat16
MIB = 1024 * 1024
PACK_MIB = 62


def vmem():
    return pl.BlockSpec(memory_space=pltpu.VMEM)


def params(mib):
    return pltpu.CompilerParams(vmem_limit_bytes=mib * MIB)


def shaped(shape, dtype=BF16):
    return jax.ShapeDtypeStruct(shape, dtype)


def dot(a, b):
    return jnp.dot(a, b, preferred_element_type=F32)


def dot_nt(a, b):
    return lax.dot_general(a, b, (((1,), (1,)), ((), ())), preferred_element_type=F32)


def token_at(place):
    return (((place & (HALF - 1)) >> 3) << 4) + ((place >> 6) << 3) + (place & 7)


def one_where(mask):
    return jnp.where(mask, 1.0, 0.0).astype(BF16)


def reorder_matrix(inverse):
    row = lax.broadcasted_iota(jnp.int32, (BLOCK, BLOCK), 0)
    col = lax.broadcasted_iota(jnp.int32, (BLOCK, BLOCK), 1)
    return one_where(row == token_at(col)) if inverse else one_where(col == token_at(row))


def split_three(x):
    high = x.astype(BF16).astype(F32)
    rest = x - high
    mid = rest.astype(BF16).astype(F32)
    return high, mid, rest - mid


def widen(x):
    if x.shape[1] == LANES:
        return x
    return jnp.concatenate([x, jnp.zeros((x.shape[0], LANES - x.shape[1]), x.dtype)], axis=1)


def send_pieces(outs, stage):
    me = lax.axis_index("var") % GROUP
    for distance, out in enumerate(outs):
        out[...] = stage[me ^ distance]


def stage_pieces(stage, pieces):
    me = lax.axis_index("var") % GROUP
    for distance, piece in enumerate(pieces):
        stage[me ^ distance] = piece[...]


def load_all(pairs, sems):
    copies = []
    for i, (source, target) in enumerate(pairs):
        rows = source.shape[0] // LOADS
        for part in range(LOADS):
            at = pl.ds(part * rows, rows)
            copies.append(pltpu.make_async_copy(source.at[at], target.at[at], sems.at[i, part]))
    for copy in copies:
        copy.start()
    return [copies[i * LOADS : (i + 1) * LOADS] for i in range(len(pairs))]


def reorder_into(staged, half, ref, scale=None):
    rows, features = ref.shape
    width = features // GROUP
    order = reorder_matrix(False)
    for b in range(rows // BLOCK):
        at = slice(b * BLOCK, (b + 1) * BLOCK)
        moved = dot(order, ref[at])
        if scale is not None:
            moved = moved * scale
        moved = moved.astype(BF16)
        for member in range(GROUP):
            staged[member, at, half * LANES : (half + 1) * LANES] = widen(
                moved[:, member * width : (member + 1) * width]
            )


def pack_kv_kernel(k_hbm, v_hbm, *rest):
    outs, (k_ref, v_ref, turned, sems) = rest[: 2 * GROUP], rest[2 * GROUP :]
    arrivals = load_all([(k_hbm, k_ref), (v_hbm, v_ref)], sems)
    for i, ref in enumerate((k_ref, v_ref)):
        for copy in arrivals[i]:
            copy.wait()
        reorder_into(turned.at[i], 0, ref)
        send_pieces(outs[i * GROUP : (i + 1) * GROUP], turned.at[i])


def pack_qo_kernel(slots, head_dim, q_ref, g_ref, lse_ref, key_ref, value_ref, after_ref, *rest):
    outs, (hold_key, hold_value, qo_ref) = rest[:GROUP], rest[GROUP:]
    hold_key[...] = key_ref[...]
    hold_value[...] = value_ref[...]
    rows = q_ref.shape[0]
    blocks = rows // BLOCK
    reorder_into(qo_ref, 0, q_ref, head_dim ** (-0.5))
    reorder_into(qo_ref, 1, g_ref)
    token = lax.broadcasted_iota(jnp.int32, (BLOCK, 2 * LANES), 0)
    lane = lax.broadcasted_iota(jnp.int32, (BLOCK, 2 * LANES), 1)
    place = ((lane >> 7) << 6) + (lane & (HALF - 1))
    hit = token == token_at(place)
    upper = (lane & HALF) != 0
    spread = [one_where(hit & ~upper), one_where(hit & upper)]
    for member in range(GROUP):
        total = None
        for slot in range(slots):
            lse = lse_ref[member * slots + slot : member * slots + slot + 1, :]
            parts = [
                part[:, b * BLOCK : (b + 1) * BLOCK]
                for part in split_three(lse)
                for b in range(blocks)
            ]
            parts.append(jnp.zeros((LSE_ROWS - len(parts), BLOCK), F32))
            moved = dot(jnp.concatenate(parts, axis=0).astype(BF16), spread[slot])
            total = moved if total is None else total + moved
        qo_ref[member, rows:] = total.astype(BF16)
    send_pieces(outs, qo_ref)


def below_first():
    me = lax.axis_index("var")
    return (me // GROUP + me) % 2


def exchange_start(group_blocks):
    odd = below_first()
    reach = group_blocks - SPAN
    return (1 - odd) * reach, odd * reach


def line_kernel(carried, *refs):
    pieces, refs = refs[:GROUP], refs[GROUP:]
    rows = pieces[0].shape[0]
    blocks = rows // BLOCK
    if carried:
        query_piece, refs = refs[0], refs[2 + carried :]
        tail = GROUP * rows
        for cols in (slice(0, LANES), slice(LANES, 2 * LANES)):
            refs[0][tail : tail + rows + LSE_ROWS] = query_piece[:, cols]
            tail += rows + LSE_ROWS
    else:
        refs = refs[2:]
    own, first_out, second_out = refs[:3]
    me = lax.axis_index("var") % GROUP
    for distance in range(GROUP):
        at = pl.ds(pl.multiple_of((me ^ distance) * rows, rows), rows)
        own[at] = pieces[distance][...]
    first, second = exchange_start(GROUP * blocks)
    for start, out in ((first, first_out), (second, second_out)):
        out[...] = own[pl.ds(pl.multiple_of(start * BLOCK, BLOCK), SPAN * BLOCK)]


def gate_kernel(*refs):
    pass


def attend_kernel(last, blocks_here, head_dim, kb_ref, *refs):
    if last:
        kv_win, k_turn, shifts, qo_ref, before, dq_before, *refs = refs
        own_out, first_out, second_out, *refs = refs
        dq_outs, refs = refs[:GROUP], refs[GROUP:]
        acc, queries, grads, crossed, prob, slope, dq_all = refs
    else:
        key_refs, value_refs, refs = refs[:3], refs[3:6], refs[6:]
        qo_pieces, refs = refs[: GROUP - 1], refs[GROUP - 1 :]
        first_out, second_out, kv_win, k_turn, shifts, qo_ref, kept_out, dq_all, *refs = refs
        acc, queries, grads, crossed, prob, slope = refs
    group_blocks = GROUP * blocks_here
    window = group_blocks + 2 * SPAN
    rows = blocks_here * BLOCK
    slot_count = kb_ref.shape[1]
    scale = head_dim ** (-0.5)
    base = (lax.axis_index("var") // GROUP) * group_blocks
    odd = below_first()
    low = slice(0, LANES)
    high = slice(LANES, 2 * LANES)

    acc[...] = jnp.zeros_like(acc)
    crossed[...] = jnp.zeros_like(crossed)
    if last:
        dq_all[...] = dq_before[...]
    else:
        top = window - SPAN
        for cols, kv_refs in ((low, key_refs), (high, value_refs)):
            for ref, start, count in zip(
                kv_refs, (SPAN, (1 - odd) * top, odd * top), (group_blocks, SPAN, SPAN)
            ):
                kv_win[pl.ds(start, count), :, cols] = ref[: count * BLOCK].reshape(
                    count, BLOCK, LANES
                )
        me = lax.axis_index("var") % GROUP
        tail = group_blocks * BLOCK
        for cols in (low, high):
            qo_ref[me, :, cols] = value_refs[0][tail : tail + rows + LSE_ROWS]
            tail += rows + LSE_ROWS
        for distance, piece in enumerate(qo_pieces):
            qo_ref[me ^ (distance + 1)] = piece[...]
        key_patch = lax.broadcasted_iota(jnp.int32, (8, LANES), 0)
        query_patch = lax.broadcasted_iota(jnp.int32, (8, LANES), 1) & 7
        usable = key_patch <= query_patch
        for member in range(GROUP):
            parts = qo_ref[member, rows:].astype(F32)
            for local in range(blocks_here):
                lse = (
                    parts[local : local + 1] + parts[blocks_here + local : blocks_here + local + 1]
                ) + parts[2 * blocks_here + local : 2 * blocks_here + local + 1]
                at = member * blocks_here + local
                shifts[at, 0, :, low] = jnp.where(usable, -lse[:, low], -1e30)
                shifts[at, 0, :, high] = jnp.broadcast_to(-lse[:, high], (8, LANES))
                shifts[at, 1, :, low] = jnp.where(usable, -lse[:, high], -1e30)

        @pl.loop(0, window)
        def _(block):
            k_turn[block] = kv_win[block, :, low].T

    unorder = reorder_matrix(True)
    lane = lax.broadcasted_iota(jnp.int32, (HALF, LANES), 1)
    head_a = lane < HALF

    def picks(query_block):
        return [kb_ref[base + query_block, s] - base + SPAN for s in range(slot_count)]

    def lay_out(member, local, buf):
        at = pl.multiple_of(local * BLOCK, BLOCK)
        for part in range(2):
            rows_at = pl.ds(at + part * HALF, HALF)
            for cols, target in ((low, queries), (high, grads)):
                tile = qo_ref[member, rows_at, cols]
                zero = jnp.zeros_like(tile)
                both = jnp.concatenate(
                    [jnp.where(head_a, tile, zero), jnp.where(head_a, zero, tile)], axis=0
                )
                target[buf, part * BLOCK : (part + 1) * BLOCK] = both
                if part == 1:
                    side = 0 if target is queries else 1
                    crossed[
                        buf, side * BLOCK : (side + 1) * BLOCK, side * LANES : (side + 1) * LANES
                    ] = both

    def gather(index, rows_of, cols):
        return jnp.concatenate([kv_win[i, rows_of, cols] for i in index], axis=0)

    early = slice(0, HALF)
    late = slice(HALF, BLOCK)
    both_cols = slice(0, 2 * LANES)
    early_rows = slot_count * HALF
    part_slots = slot_count // PARTS
    part_rows = part_slots * HALF

    def forward_part(index, query_block, buf, part):
        some = index[part * part_slots : (part + 1) * part_slots]
        at = slice(part * part_rows, (part + 1) * part_rows)
        after = slice(early_rows + part * part_rows, early_rows + (part + 1) * part_rows)
        s = dot_nt(gather(some, early, low), queries[buf])
        g = dot_nt(gather(some, early, high), grads[buf])
        x = dot_nt(gather(some, late, both_cols), crossed[buf])
        shift = shifts[query_block, 0][None]
        p = jnp.exp(s.reshape(part_rows // 8, 8, 2 * LANES) + shift).reshape(part_rows, 2 * LANES)
        prob[buf, at] = p
        slope[buf, at] = g
        delta = jnp.sum((p * g).reshape(part_rows // 8, 8, 2 * LANES), axis=0)
        late_shift = shifts[query_block, 1, :, low][None]
        q = jnp.exp(x[:, low].reshape(part_rows // 8, 8, LANES) + late_shift).reshape(
            part_rows, LANES
        )
        prob[buf, after, low] = q
        slope[buf, after, low] = x[:, high]
        more = jnp.sum((q * x[:, high]).reshape(part_rows // 8, 8, LANES), axis=0)
        return delta[:, low], delta[:, high] + more

    def backward_part(index, buf, delta, part):
        at = slice(part * part_rows, (part + 1) * part_rows)
        after = slice(early_rows + part * part_rows, early_rows + (part + 1) * part_rows)
        p = prob[buf, at]
        ds = (p * (slope[buf, at] - delta)).astype(BF16)
        q = prob[buf, after, low]
        ds_late = (q * (slope[buf, after, low] - delta[:, high])).astype(BF16)
        dk = dot(ds, queries[buf])
        dv = dot(p.astype(BF16), grads[buf])
        r = dot(jnp.concatenate([ds_late, q.astype(BF16)], axis=1), crossed[buf])
        nothing = jnp.zeros((HALF, LANES), BF16)
        pieces = []
        for s in range(part_slots):
            at = slice(s * HALF, (s + 1) * HALF)
            where = index[part * part_slots + s]
            acc[where, early, low] = acc[where, early, low] + dk[at]
            acc[where, early, high] = acc[where, early, high] + dv[at]
            acc[where, late] = acc[where, late] + r[at]
            pieces.append(ds[at])
            pieces.append(jnp.concatenate([nothing, ds_late[at]], axis=1))
        keys_turned = jnp.concatenate(
            [k_turn[i] for i in index[part * part_slots : (part + 1) * part_slots]], axis=1
        )
        return dot(keys_turned, jnp.concatenate(pieces, axis=0))

    def write_dq(query_block, dq):
        dq = dq * scale
        halves = []
        for cols in (low, high):
            turned = dq[:, cols].T
            halves.append(jnp.where(head_a, turned[:HALF], turned[HALF:]))
        moved = dot(unorder, jnp.concatenate(halves, axis=0).astype(BF16)).astype(BF16)
        local = pl.multiple_of((query_block % blocks_here) * BLOCK, BLOCK)
        dq_all[query_block // blocks_here, pl.ds(local, BLOCK)] = moved

    def run(ahead, ahead_buf, behind, behind_buf, delta):
        sums, dq = None, None
        if ahead is not None:
            lay_out(ahead // blocks_here, ahead % blocks_here, ahead_buf)
            ahead_index = picks(ahead)
        if behind is not None:
            behind_index = picks(behind)
        for part in range(PARTS):
            if ahead is not None:
                more = forward_part(ahead_index, ahead, ahead_buf, part)
                sums = more if sums is None else (sums[0] + more[0], sums[1] + more[1])
            if behind is not None:
                more = backward_part(behind_index, behind_buf, delta, part)
                dq = more if dq is None else dq + more
        if behind is not None:
            write_dq(behind, dq)
        if ahead is None:
            return None
        return jnp.concatenate([jnp.sum(x, axis=0, keepdims=True) for x in sums], axis=1)

    def block_of(j):
        if last:
            return j + OUTER
        return j + jnp.where(j < OUTER, 0, group_blocks - 2 * OUTER)

    count = group_blocks - 2 * OUTER if last else 2 * OUTER
    delta = run(block_of(0), 0, None, None, None)

    def step(j, delta):
        delta = run(block_of(2 * j + 1), 1, block_of(2 * j), 0, delta)
        return run(block_of(2 * j + 2), 0, block_of(2 * j + 1), 1, delta)

    delta = lax.fori_loop(0, (count - 1) // 2, step, delta)
    if count % 2 == 0:
        delta = run(block_of(count - 1), 1, block_of(count - 2), 0, delta)
    run(None, None, block_of(count - 1), (count - 1) % 2, delta)

    groups = BLOCK // 16

    def in_token_order(part):
        blocks = part.shape[0]
        part = part.reshape(blocks, 2, groups, 8, 2 * LANES)
        return jnp.swapaxes(part, 1, 2).reshape(blocks, BLOCK, 2 * LANES)

    if last:
        acc[OUTER : window - OUTER] = acc[OUTER : window - OUTER] + before[...]
        top = window - SPAN
        for out, side in ((first_out, 1 - odd), (second_out, odd)):
            start = OUTER + side * (top - OUTER)
            out[...] = in_token_order(acc[pl.ds(start, OUTER)]).astype(BF16)
        own_out[...] = in_token_order(acc[SPAN : SPAN + group_blocks])
        send_pieces(dq_outs, dq_all)
    else:
        for out, side in ((first_out, 1 - odd), (second_out, odd)):
            start = side * (window - OUTER)
            out[...] = in_token_order(acc[pl.ds(start, OUTER)]).astype(BF16)
        kept_out[...] = acc[OUTER : window - OUTER]


def owner_start(piece, half):
    heads = lax.axis_size("head")
    return pl.multiple_of(((lax.axis_index("head") + 1 + piece) % heads) * half, half)


def add_arrived(total, starts, refs):
    level = lax.axis_index("var") // GROUP
    levels = lax.axis_size("var") // GROUP
    odd = below_first()
    for side, ref in zip((1 - odd, odd), refs):
        other = level - 1 + 2 * side
        start = jnp.where(side == 1, starts[1], starts[0])

        @pl.when((other >= 0) & (other < levels))
        def _(start=start, ref=ref):
            at = pl.ds(start, OUTER)
            total[at] = total[at] + ref[...].astype(F32)


def combine_outer_kernel(carried, own_ref, first_ref, second_ref, *refs):
    total = refs[carried]
    total[...] = own_ref[...]
    add_arrived(total, (SPAN - OUTER, own_ref.shape[0] - SPAN), (first_ref, second_ref))


def combine_kernel(own_ref, first_ref, second_ref, *rest):
    aways, homes, (total, moved) = rest[:GROUP], rest[GROUP : 2 * GROUP], rest[2 * GROUP :]
    total[...] = own_ref[...]
    add_arrived(total, (0, own_ref.shape[0] - OUTER), (first_ref, second_ref))
    moved[...] = total[...].astype(BF16).reshape(moved.shape)
    half = homes[0].shape[0]
    away = aways[0].shape[0] // half
    me = lax.axis_index("var") % GROUP
    for distance in range(GROUP):
        member = me ^ distance
        for piece in range(away):
            aways[distance][piece * half : (piece + 1) * half] = moved[
                member, pl.ds(owner_start(piece, half), half)
            ]
        homes[distance][...] = moved[member, pl.ds(owner_start(away, half), half)]


def gather_rows(grads, dq, start, dkv, dkv_at):
    half = grads.shape[1]
    width = grads.shape[2] // GROUP
    for member in range(GROUP):
        at = slice(member * width, (member + 1) * width)
        both = dkv[member, dkv_at * half : (dkv_at + 1) * half]
        grads[0, :, at] = dq[member, pl.ds(start, half)][:, :width]
        grads[1, :, at] = both[:, :width]
        grads[2, :, at] = both[:, LANES : LANES + width]


def product(grads, w_ref):
    total = dot_nt(grads[0], w_ref[0])
    for s in (1, 2):
        total = total + dot_nt(grads[s], w_ref[s])
    return total


def away_kernel(*refs):
    dqs, dkvs, (w_ref, *rest) = refs[:4], refs[4:8], refs[8:]
    outs, (grads, dq, dkv) = rest[:-3], rest[-3:]
    half = grads.shape[1]
    stage_pieces(dq, dqs)
    stage_pieces(dkv, dkvs)
    for piece, out in enumerate(outs):
        gather_rows(grads, dq, owner_start(piece, half), dkv, piece)
        out[...] = product(grads, w_ref).astype(BF16)


def home_kernel(*refs):
    dqs, aways, homes, rest = refs[:4], refs[4:8], refs[8:12], refs[12:]
    w_ref, dq_out, dk_out, dv_out, keep_out, grads, dq, away_dkv, home_dkv = rest
    half = grads.shape[1]
    away = away_dkv.shape[1] // half
    stage_pieces(dq, dqs)
    stage_pieces(away_dkv, aways)
    stage_pieces(home_dkv, homes)
    for piece in range(away + 1):
        start = owner_start(piece, half)
        if piece < away:
            gather_rows(grads, dq, start, away_dkv, piece)
        else:
            gather_rows(grads, dq, start, home_dkv, 0)
        at = pl.ds(start, half)
        dq_out[at] = grads[0]
        dk_out[at] = grads[1]
        dv_out[at] = grads[2]
    keep_out[...] = product(grads, w_ref)


def body(queries, keys, values, out_grad, log_sum_exp, key_blocks, w_qkv):
    rows, features = queries.shape
    head_count = log_sum_exp.shape[0]
    head_dim = features // head_count
    slots = head_count // GROUP
    blocks_here = rows // BLOCK
    group_blocks = GROUP * blocks_here
    window = group_blocks + 2 * SPAN
    slot_count = key_blocks.shape[1]
    devices = lax.axis_size("var")
    heads = lax.axis_size("head")
    half = rows // heads
    model = w_qkv.shape[1]
    wide = 2 * LANES
    hbm = pl.BlockSpec(memory_space=pltpu.HBM)

    def trade(x, distance):
        return lax.ppermute(x, "var", [(n, n ^ distance) for n in range(devices)])

    def trade_level(x, turn):
        pairs = []
        for n in range(devices):
            other = n - GROUP if (n // GROUP + n + turn) % 2 else n + GROUP
            for h in range(heads):
                if 0 <= other < devices:
                    target = other * heads + h
                else:
                    target = n * heads + (h ^ 1) % heads
                pairs.append((n * heads + h, target))
        return lax.ppermute(x, ("var", "head"), pairs)

    def trade_first(x):
        return trade_level(x, 0)

    def trade_second(x):
        return trade_level(x, 1)

    def swap(pieces):
        got = [pieces[0]] + [None] * (GROUP - 1)
        for distance in (2, 3, 1):
            got[distance] = trade(pieces[distance], distance)
        return got

    def staged(count, width=LANES):
        return pltpu.VMEM((GROUP, count, width), BF16)

    block = (BLOCK, LANES)
    anywhere = pl.BlockSpec(memory_space=pl.ANY)

    def cost(flops, moved):
        return pl.CostEstimate(flops=flops, bytes_accessed=moved, transcendentals=0)

    size = rows * features * 2

    packed = pl.pallas_call(
        pack_kv_kernel,
        out_shape=(shaped((rows, LANES)),) * (2 * GROUP),
        in_specs=[hbm] * 2,
        out_specs=(vmem(),) * (2 * GROUP),
        scratch_shapes=[pltpu.VMEM((rows, features), BF16)] * 2
        + [pltpu.VMEM((2, GROUP, rows, LANES), BF16), pltpu.SemaphoreType.DMA((2, LOADS))],
        compiler_params=params(PACK_MIB),
        cost_estimate=cost(4 * rows * features * BLOCK, 5 * size),
    )(keys, values)
    key_pieces = swap(packed[:GROUP])
    value_pieces = swap(packed[GROUP:])
    *qos, key_pieces[0], value_pieces[0] = pl.pallas_call(
        functools.partial(pack_qo_kernel, slots, head_dim),
        out_shape=(shaped((rows + LSE_ROWS, wide)),) * GROUP + (shaped((rows, LANES)),) * 2,
        in_specs=[vmem()] * 5 + [anywhere],
        out_specs=(vmem(),) * (GROUP + 2),
        scratch_shapes=[staged(rows + LSE_ROWS, wide)],
        compiler_params=params(8),
        cost_estimate=cost(4 * rows * features * BLOCK, 10 * size),
    )(queries, out_grad, log_sum_exp, packed[0], packed[GROUP], key_pieces[1])
    sends_shape = (shaped((SPAN * BLOCK, LANES)),) * 2
    own_keys, first_keys, second_keys = pl.pallas_call(
        functools.partial(line_kernel, 0),
        out_shape=(shaped((GROUP * rows, LANES)),) + sends_shape,
        in_specs=[vmem()] * GROUP + [anywhere] * 2,
        out_specs=(vmem(),) * 3,
        compiler_params=params(8),
        cost_estimate=cost(0, 3 * size),
    )(*key_pieces, value_pieces[1], value_pieces[2])
    first_keys = trade_first(first_keys)
    second_keys = trade_second(second_keys)
    carried = tuple(qos[1:])
    count = len(carried)
    own_values, first_values, second_values, *carried = pl.pallas_call(
        functools.partial(line_kernel, count),
        out_shape=(shaped((GROUP * rows + 2 * (rows + LSE_ROWS), LANES)),)
        + sends_shape
        + tuple(shaped(x.shape) for x in carried),
        in_specs=[vmem()] * (GROUP + 1) + [anywhere] * (count + 1),
        out_specs=(vmem(),) * 3 + (anywhere,) * count,
        input_output_aliases={GROUP + 2 + i: 3 + i for i in range(count)},
        compiler_params=params(8),
        cost_estimate=cost(0, 5 * size),
    )(*value_pieces, qos[0], own_keys, *carried)
    first_values = trade_first(first_values)
    second_values = trade_second(second_values)
    carried[-1] = pl.pallas_call(
        gate_kernel,
        out_shape=shaped(carried[-1].shape),
        in_specs=[anywhere] * 3,
        out_specs=anywhere,
        input_output_aliases={0: 0},
        compiler_params=params(4),
        cost_estimate=cost(0, 1024),
    )(carried[-1], first_keys, second_keys)
    qos = swap([None, *carried])[1:]

    pairs = group_blocks * slot_count * BLOCK * BLOCK * slots
    tall = (BLOCK, wide)
    acc_scratch = pltpu.VMEM((window,) + tall, F32)
    work = [
        pltpu.VMEM((2, wide, LANES), BF16),
        pltpu.VMEM((2, wide, LANES), BF16),
        pltpu.VMEM((2, wide, wide), BF16),
        pltpu.VMEM((2, slot_count * BLOCK, wide), F32),
        pltpu.VMEM((2, slot_count * BLOCK, wide), F32),
    ]
    smem = pl.BlockSpec(memory_space=pltpu.SMEM)
    outer = (shaped((OUTER,) + tall),) * 2

    def attend_cost(part):
        return pl.CostEstimate(
            flops=int(40 * pairs * head_dim * part),
            bytes_accessed=2_000_000,
            transcendentals=int(pairs * part),
        )

    state = (
        shaped((window,) + tall),
        shaped((window, LANES, BLOCK)),
        shaped((group_blocks, 2, 8, wide), F32),
        shaped((GROUP, rows + LSE_ROWS, wide)),
        shaped((window - 2 * OUTER,) + tall, F32),
        shaped((GROUP, rows, LANES)),
    )
    first, second, *state = pl.pallas_call(
        functools.partial(attend_kernel, False, blocks_here, head_dim),
        out_shape=outer + state,
        in_specs=[smem] + [vmem()] * (5 + GROUP),
        out_specs=(vmem(),) * 8,
        scratch_shapes=[acc_scratch] + work,
        compiler_params=params(16),
        cost_estimate=attend_cost(0.67),
    )(
        key_blocks,
        own_keys,
        first_keys,
        second_keys,
        own_values,
        first_values,
        second_values,
        *qos,
    )
    outer_back = (trade_first(first), trade_second(second))
    own_sum, first, second, *dqs = pl.pallas_call(
        functools.partial(attend_kernel, True, blocks_here, head_dim),
        out_shape=(shaped((group_blocks,) + tall, F32),)
        + outer
        + (shaped((rows, LANES)),) * GROUP,
        in_specs=[smem] + [vmem()] * 6,
        out_specs=(vmem(),) * (3 + GROUP),
        scratch_shapes=[acc_scratch] + work + [staged(rows)],
        compiler_params=params(16),
        cost_estimate=attend_cost(0.33),
    )(key_blocks, *state)
    inner_back = (trade_first(first), trade_second(second))
    carried = tuple(dqs[1:])
    *carried, own_sum = pl.pallas_call(
        functools.partial(combine_outer_kernel, 2 * len(carried)),
        out_shape=tuple(shaped(x.shape) for x in carried) + (shaped((group_blocks,) + tall, F32),),
        in_specs=[vmem()] * 3 + [anywhere] * len(carried),
        out_specs=(anywhere,) * len(carried) + (vmem(),),
        input_output_aliases={3 + i: i for i in range(len(carried))},
        compiler_params=params(8),
        cost_estimate=cost(0, 4 * size),
    )(own_sum, *outer_back, *carried)
    dqs = swap([dqs[0], *carried])
    split = pl.pallas_call(
        combine_kernel,
        out_shape=(shaped((rows - half, wide)),) * GROUP + (shaped((half, wide)),) * GROUP,
        in_specs=[vmem()] * 3,
        out_specs=(vmem(),) * (2 * GROUP),
        scratch_shapes=[pltpu.VMEM((group_blocks,) + tall, F32), staged(rows, wide)],
        compiler_params=params(8),
        cost_estimate=cost(0, 8 * size),
    )(own_sum, *inner_back)
    aways = swap(split[:GROUP])
    homes = swap(split[GROUP:])

    grads = pltpu.VMEM((3, half, features), BF16)
    sends = pl.pallas_call(
        away_kernel,
        out_shape=(shaped((half, model)),) * (heads - 1),
        in_specs=[vmem()] * (2 * GROUP + 1),
        out_specs=(vmem(),) * (heads - 1),
        scratch_shapes=[grads, staged(rows), staged(rows - half, wide)],
        compiler_params=params(8),
        cost_estimate=cost(6 * (rows - half) * features * model, 4_000_000),
    )(*dqs, *aways, w_qkv)
    dq_out, dk_out, dv_out, total = pl.pallas_call(
        home_kernel,
        out_shape=(shaped((rows, features)),) * 3 + (shaped((half, model), F32),),
        in_specs=[vmem()] * (3 * GROUP + 1),
        out_specs=(vmem(),) * 4,
        scratch_shapes=[grads, staged(rows), staged(rows - half, wide), staged(half, wide)],
        compiler_params=params(8),
        cost_estimate=cost(6 * half * features * model, 6_000_000),
    )(*dqs, *aways, *homes, w_qkv)
    for piece, send in enumerate(sends):
        got = lax.ppermute(send, "head", [(n, (n + piece + 1) % heads) for n in range(heads)])
        total = total + got.astype(F32)
    return dq_out, dk_out, dv_out, total.astype(BF16)


def solution(mesh):
    in_specs = (
        P("var", "head"),
        P("var", "head"),
        P("var", "head"),
        P("var", "head"),
        P("head", "var"),
        P(),
        P(None, None, "head"),
    )
    out_specs = (P("var", "head"), P("var", "head"), P("var", "head"), P(("var", "head"), None))
    return jax.shard_map(body, mesh=mesh, in_specs=in_specs, out_specs=out_specs, check_vma=False)
```

```python
import functools

import jax
import jax.numpy as jnp
from jax import lax
from jax.experimental import pallas as pl
from jax.experimental.pallas import tpu as pltpu
from jax.sharding import PartitionSpec as P

PATCHES = 16
BLOCK = 128
HALF = BLOCK // 2
SPAN = 8
OUTER = SPAN // 2
GROUP = 4
LANES = 128
LSE_ROWS = 16
PARTS = 2
CHUNKS = 2
LOADS = 3
F32 = jnp.float32
BF16 = jnp.bfloat16
MIB = 1024 * 1024
PACK_MIB = 62


def vmem():
    return pl.BlockSpec(memory_space=pltpu.VMEM)


def params(mib):
    return pltpu.CompilerParams(vmem_limit_bytes=mib * MIB)


def shaped(shape, dtype=BF16):
    return jax.ShapeDtypeStruct(shape, dtype)


def dot(a, b):
    return jnp.dot(a, b, preferred_element_type=F32)


def dot_nt(a, b):
    return lax.dot_general(a, b, (((1,), (1,)), ((), ())), preferred_element_type=F32)


def token_at(place):
    return (((place & (HALF - 1)) >> 3) << 4) + ((place >> 6) << 3) + (place & 7)


def one_where(mask):
    return jnp.where(mask, 1.0, 0.0).astype(BF16)


def reorder_matrix(inverse):
    row = lax.broadcasted_iota(jnp.int32, (BLOCK, BLOCK), 0)
    col = lax.broadcasted_iota(jnp.int32, (BLOCK, BLOCK), 1)
    return one_where(row == token_at(col)) if inverse else one_where(col == token_at(row))


def split_three(x):
    high = x.astype(BF16).astype(F32)
    rest = x - high
    mid = rest.astype(BF16).astype(F32)
    return high, mid, rest - mid


def widen(x):
    if x.shape[1] == LANES:
        return x
    return jnp.concatenate([x, jnp.zeros((x.shape[0], LANES - x.shape[1]), x.dtype)], axis=1)


def send_pieces(outs, stage):
    me = lax.axis_index("var") % GROUP
    for distance, out in enumerate(outs):
        out[...] = stage[me ^ distance]


def stage_pieces(stage, pieces):
    me = lax.axis_index("var") % GROUP
    for distance, piece in enumerate(pieces):
        stage[me ^ distance] = piece[...]


def load_all(pairs, sems):
    copies = []
    for i, (source, target) in enumerate(pairs):
        rows = source.shape[0] // LOADS
        for part in range(LOADS):
            at = pl.ds(part * rows, rows)
            copies.append(pltpu.make_async_copy(source.at[at], target.at[at], sems.at[i, part]))
    for copy in copies:
        copy.start()
    return [copies[i * LOADS : (i + 1) * LOADS] for i in range(len(pairs))]


def reorder_into(staged, half, ref, scale=None):
    rows, features = ref.shape
    width = features // GROUP
    order = reorder_matrix(False)
    for b in range(rows // BLOCK):
        at = slice(b * BLOCK, (b + 1) * BLOCK)
        moved = dot(order, ref[at])
        if scale is not None:
            moved = moved * scale
        moved = moved.astype(BF16)
        for member in range(GROUP):
            staged[member, at, half * LANES : (half + 1) * LANES] = widen(
                moved[:, member * width : (member + 1) * width]
            )


def pack_kv_kernel(k_hbm, v_hbm, *rest):
    outs, (k_ref, v_ref, turned, sems) = rest[:GROUP], rest[GROUP:]
    arrivals = load_all([(k_hbm, k_ref), (v_hbm, v_ref)], sems)
    for half, ref in enumerate((k_ref, v_ref)):
        for copy in arrivals[half]:
            copy.wait()
        reorder_into(turned, half, ref)
    send_pieces(outs, turned)


def pack_qo_kernel(slots, head_dim, q_ref, g_ref, lse_ref, mine_ref, after_ref, *rest):
    outs, (hold, qo_ref) = rest[:GROUP], rest[GROUP:]
    hold[...] = mine_ref[...]
    rows = q_ref.shape[0]
    blocks = rows // BLOCK
    reorder_into(qo_ref, 0, q_ref, head_dim ** (-0.5))
    reorder_into(qo_ref, 1, g_ref)
    token = lax.broadcasted_iota(jnp.int32, (BLOCK, 2 * LANES), 0)
    lane = lax.broadcasted_iota(jnp.int32, (BLOCK, 2 * LANES), 1)
    place = ((lane >> 7) << 6) + (lane & (HALF - 1))
    hit = token == token_at(place)
    upper = (lane & HALF) != 0
    spread = [one_where(hit & ~upper), one_where(hit & upper)]
    for member in range(GROUP):
        total = None
        for slot in range(slots):
            lse = lse_ref[member * slots + slot : member * slots + slot + 1, :]
            parts = [
                part[:, b * BLOCK : (b + 1) * BLOCK]
                for part in split_three(lse)
                for b in range(blocks)
            ]
            parts.append(jnp.zeros((LSE_ROWS - len(parts), BLOCK), F32))
            moved = dot(jnp.concatenate(parts, axis=0).astype(BF16), spread[slot])
            total = moved if total is None else total + moved
        qo_ref[member, rows:] = total.astype(BF16)
    send_pieces(outs, qo_ref)


def below_first():
    me = lax.axis_index("var")
    return (me // GROUP + me) % 2


def exchange_start(group_blocks):
    odd = below_first()
    reach = group_blocks - SPAN
    return (1 - odd) * reach, odd * reach


def line_kernel(carried, *refs):
    pieces, query_piece, refs = refs[:GROUP], refs[GROUP], refs[GROUP + 1 + carried :]
    own, first_out, second_out = refs[:3]
    rows = pieces[0].shape[0]
    own[GROUP * rows :] = query_piece[...]
    blocks = rows // BLOCK
    me = lax.axis_index("var") % GROUP
    for distance in range(GROUP):
        at = pl.ds(pl.multiple_of((me ^ distance) * rows, rows), rows)
        own[at] = pieces[distance][...]
    first, second = exchange_start(GROUP * blocks)
    for start, out in ((first, first_out), (second, second_out)):
        out[...] = own[pl.ds(pl.multiple_of(start * BLOCK, BLOCK), SPAN * BLOCK)]


def attend_kernel(last, blocks_here, head_dim, kb_ref, *refs):
    if last:
        kv_win, k_turn, shifts, qo_ref, before, dq_before, *refs = refs
        own_out, first_out, second_out, *refs = refs
        dq_outs, refs = refs[:GROUP], refs[GROUP:]
        acc, queries, grads, crossed, prob, slope, dq_all = refs
    else:
        kv_refs, refs = refs[:3], refs[3:]
        qo_pieces, refs = refs[: GROUP - 1], refs[GROUP - 1 :]
        first_out, second_out, kv_win, k_turn, shifts, qo_ref, kept_out, dq_all, *refs = refs
        acc, queries, grads, crossed, prob, slope = refs
    group_blocks = GROUP * blocks_here
    window = group_blocks + 2 * SPAN
    rows = blocks_here * BLOCK
    slot_count = kb_ref.shape[1]
    scale = head_dim ** (-0.5)
    base = (lax.axis_index("var") // GROUP) * group_blocks
    odd = below_first()
    low = slice(0, LANES)
    high = slice(LANES, 2 * LANES)

    acc[...] = jnp.zeros_like(acc)
    crossed[...] = jnp.zeros_like(crossed)
    if last:
        dq_all[...] = dq_before[...]
    else:
        top = window - SPAN
        for ref, start, count in zip(
            kv_refs, (SPAN, (1 - odd) * top, odd * top), (group_blocks, SPAN, SPAN)
        ):
            kv_win[pl.ds(start, count)] = ref[: count * BLOCK].reshape(count, BLOCK, 2 * LANES)
        own_queries = kv_refs[0].at[pl.ds(group_blocks * BLOCK, rows + LSE_ROWS)]
        stage_pieces(qo_ref, (own_queries, *qo_pieces))
        key_patch = lax.broadcasted_iota(jnp.int32, (8, LANES), 0)
        query_patch = lax.broadcasted_iota(jnp.int32, (8, LANES), 1) & 7
        usable = key_patch <= query_patch
        for member in range(GROUP):
            parts = qo_ref[member, rows:].astype(F32)
            for local in range(blocks_here):
                lse = (
                    parts[local : local + 1] + parts[blocks_here + local : blocks_here + local + 1]
                ) + parts[2 * blocks_here + local : 2 * blocks_here + local + 1]
                at = member * blocks_here + local
                shifts[at, 0, :, low] = jnp.where(usable, -lse[:, low], -1e30)
                shifts[at, 0, :, high] = jnp.broadcast_to(-lse[:, high], (8, LANES))
                shifts[at, 1, :, low] = jnp.where(usable, -lse[:, high], -1e30)

        @pl.loop(0, window)
        def _(block):
            k_turn[block] = kv_win[block, :, low].T

    unorder = reorder_matrix(True)
    lane = lax.broadcasted_iota(jnp.int32, (HALF, LANES), 1)
    head_a = lane < HALF

    def picks(query_block):
        return [kb_ref[base + query_block, s] - base + SPAN for s in range(slot_count)]

    def lay_out(member, local, buf):
        at = pl.multiple_of(local * BLOCK, BLOCK)
        for part in range(2):
            rows_at = pl.ds(at + part * HALF, HALF)
            for cols, target in ((low, queries), (high, grads)):
                tile = qo_ref[member, rows_at, cols]
                zero = jnp.zeros_like(tile)
                both = jnp.concatenate(
                    [jnp.where(head_a, tile, zero), jnp.where(head_a, zero, tile)], axis=0
                )
                target[buf, part * BLOCK : (part + 1) * BLOCK] = both
                if part == 1:
                    side = 0 if target is queries else 1
                    crossed[
                        buf, side * BLOCK : (side + 1) * BLOCK, side * LANES : (side + 1) * LANES
                    ] = both

    def gather(index, rows_of, cols):
        return jnp.concatenate([kv_win[i, rows_of, cols] for i in index], axis=0)

    early = slice(0, HALF)
    late = slice(HALF, BLOCK)
    both_cols = slice(0, 2 * LANES)
    early_rows = slot_count * HALF
    part_slots = slot_count // PARTS
    part_rows = part_slots * HALF

    def forward_part(index, query_block, buf, part):
        some = index[part * part_slots : (part + 1) * part_slots]
        at = slice(part * part_rows, (part + 1) * part_rows)
        after = slice(early_rows + part * part_rows, early_rows + (part + 1) * part_rows)
        s = dot_nt(gather(some, early, low), queries[buf])
        g = dot_nt(gather(some, early, high), grads[buf])
        x = dot_nt(gather(some, late, both_cols), crossed[buf])
        shift = shifts[query_block, 0][None]
        p = jnp.exp(s.reshape(part_rows // 8, 8, 2 * LANES) + shift).reshape(part_rows, 2 * LANES)
        prob[buf, at] = p
        slope[buf, at] = g
        delta = jnp.sum((p * g).reshape(part_rows // 8, 8, 2 * LANES), axis=0)
        late_shift = shifts[query_block, 1, :, low][None]
        q = jnp.exp(x[:, low].reshape(part_rows // 8, 8, LANES) + late_shift).reshape(
            part_rows, LANES
        )
        prob[buf, after, low] = q
        slope[buf, after, low] = x[:, high]
        more = jnp.sum((q * x[:, high]).reshape(part_rows // 8, 8, LANES), axis=0)
        return delta[:, low], delta[:, high] + more

    def backward_part(index, buf, delta, part):
        at = slice(part * part_rows, (part + 1) * part_rows)
        after = slice(early_rows + part * part_rows, early_rows + (part + 1) * part_rows)
        p = prob[buf, at]
        ds = (p * (slope[buf, at] - delta)).astype(BF16)
        q = prob[buf, after, low]
        ds_late = (q * (slope[buf, after, low] - delta[:, high])).astype(BF16)
        dk = dot(ds, queries[buf])
        dv = dot(p.astype(BF16), grads[buf])
        r = dot(jnp.concatenate([ds_late, q.astype(BF16)], axis=1), crossed[buf])
        nothing = jnp.zeros((HALF, LANES), BF16)
        pieces = []
        for s in range(part_slots):
            at = slice(s * HALF, (s + 1) * HALF)
            where = index[part * part_slots + s]
            acc[where, early, low] = acc[where, early, low] + dk[at]
            acc[where, early, high] = acc[where, early, high] + dv[at]
            acc[where, late] = acc[where, late] + r[at]
            pieces.append(ds[at])
            pieces.append(jnp.concatenate([nothing, ds_late[at]], axis=1))
        keys_turned = jnp.concatenate(
            [k_turn[i] for i in index[part * part_slots : (part + 1) * part_slots]], axis=1
        )
        return dot(keys_turned, jnp.concatenate(pieces, axis=0))

    def write_dq(query_block, dq):
        dq = dq * scale
        halves = []
        for cols in (low, high):
            turned = dq[:, cols].T
            halves.append(jnp.where(head_a, turned[:HALF], turned[HALF:]))
        moved = dot(unorder, jnp.concatenate(halves, axis=0).astype(BF16)).astype(BF16)
        local = pl.multiple_of((query_block % blocks_here) * BLOCK, BLOCK)
        dq_all[query_block // blocks_here, pl.ds(local, BLOCK)] = moved

    def run(ahead, ahead_buf, behind, behind_buf, delta):
        sums, dq = None, None
        if ahead is not None:
            lay_out(ahead // blocks_here, ahead % blocks_here, ahead_buf)
            ahead_index = picks(ahead)
        if behind is not None:
            behind_index = picks(behind)
        for part in range(PARTS):
            if ahead is not None:
                more = forward_part(ahead_index, ahead, ahead_buf, part)
                sums = more if sums is None else (sums[0] + more[0], sums[1] + more[1])
            if behind is not None:
                more = backward_part(behind_index, behind_buf, delta, part)
                dq = more if dq is None else dq + more
        if behind is not None:
            write_dq(behind, dq)
        if ahead is None:
            return None
        return jnp.concatenate([jnp.sum(x, axis=0, keepdims=True) for x in sums], axis=1)

    def block_of(j):
        if last:
            return j + OUTER
        return j + jnp.where(j < OUTER, 0, group_blocks - 2 * OUTER)

    count = group_blocks - 2 * OUTER if last else 2 * OUTER
    delta = run(block_of(0), 0, None, None, None)

    def step(j, delta):
        delta = run(block_of(2 * j + 1), 1, block_of(2 * j), 0, delta)
        return run(block_of(2 * j + 2), 0, block_of(2 * j + 1), 1, delta)

    delta = lax.fori_loop(0, (count - 1) // 2, step, delta)
    if count % 2 == 0:
        delta = run(block_of(count - 1), 1, block_of(count - 2), 0, delta)
    run(None, None, block_of(count - 1), (count - 1) % 2, delta)

    groups = BLOCK // 16

    def in_token_order(part):
        blocks = part.shape[0]
        part = part.reshape(blocks, 2, groups, 8, 2 * LANES)
        return jnp.swapaxes(part, 1, 2).reshape(blocks, BLOCK, 2 * LANES)

    if last:
        acc[OUTER : window - OUTER] = acc[OUTER : window - OUTER] + before[...]
        top = window - SPAN
        for out, side in ((first_out, 1 - odd), (second_out, odd)):
            start = OUTER + side * (top - OUTER)
            out[...] = in_token_order(acc[pl.ds(start, OUTER)]).astype(BF16)
        own_out[...] = in_token_order(acc[SPAN : SPAN + group_blocks])
        send_pieces(dq_outs, dq_all)
    else:
        for out, side in ((first_out, 1 - odd), (second_out, odd)):
            start = side * (window - OUTER)
            out[...] = in_token_order(acc[pl.ds(start, OUTER)]).astype(BF16)
        kept_out[...] = acc[OUTER : window - OUTER]


def owner_start(piece, half):
    heads = lax.axis_size("head")
    return pl.multiple_of(((lax.axis_index("head") + 1 + piece) % heads) * half, half)


def add_arrived(total, starts, refs):
    level = lax.axis_index("var") // GROUP
    levels = lax.axis_size("var") // GROUP
    odd = below_first()
    for side, ref in zip((1 - odd, odd), refs):
        other = level - 1 + 2 * side
        start = jnp.where(side == 1, starts[1], starts[0])

        @pl.when((other >= 0) & (other < levels))
        def _(start=start, ref=ref):
            at = pl.ds(start, OUTER)
            total[at] = total[at] + ref[...].astype(F32)


def combine_outer_kernel(carried, own_ref, first_ref, second_ref, *refs):
    total = refs[carried]
    total[...] = own_ref[...]
    add_arrived(total, (SPAN - OUTER, own_ref.shape[0] - SPAN), (first_ref, second_ref))


def combine_kernel(own_ref, first_ref, second_ref, *rest):
    rest = rest[GROUP - 1 :]
    chunks, rest = rest[: CHUNKS * GROUP], rest[CHUNKS * GROUP :]
    homes, (total, moved) = rest[:GROUP], rest[GROUP:]
    total[...] = own_ref[...]
    add_arrived(total, (0, own_ref.shape[0] - OUTER), (first_ref, second_ref))
    moved[...] = total[...].astype(BF16).reshape(moved.shape)
    half = homes[0].shape[0]
    small = half // CHUNKS
    away = chunks[0].shape[0] // small
    me = lax.axis_index("var") % GROUP
    for distance in range(GROUP):
        member = me ^ distance
        for chunk in range(CHUNKS):
            for piece in range(away):
                chunks[chunk * GROUP + distance][piece * small : (piece + 1) * small] = moved[
                    member, pl.ds(chunk_start(piece, half, chunk), small)
                ]
        homes[distance][...] = moved[member, pl.ds(owner_start(away, half), half)]


def chunk_start(piece, half, chunk):
    small = half // CHUNKS
    return pl.multiple_of(owner_start(piece, half) + chunk * small, small)


def gather_rows(grads, dq, start, dkv, dkv_at):
    half = grads.shape[1]
    width = grads.shape[2] // GROUP
    for member in range(GROUP):
        at = slice(member * width, (member + 1) * width)
        both = dkv[member, dkv_at * half : (dkv_at + 1) * half]
        grads[0, :, at] = dq[member, pl.ds(start, half)][:, :width]
        grads[1, :, at] = both[:, :width]
        grads[2, :, at] = both[:, LANES : LANES + width]


def product(grads, w_ref):
    total = dot_nt(grads[0], w_ref[0])
    for s in (1, 2):
        total = total + dot_nt(grads[s], w_ref[s])
    return total


def away_kernel(chunk, *refs):
    dqs, dkvs, w_ref, rest = refs[:4], refs[4:8], refs[8], refs[9 + (chunk > 0) :]
    outs, (grads, dq, dkv) = rest[:-3], rest[-3:]
    half = grads.shape[1] * CHUNKS
    stage_pieces(dq, dqs)
    stage_pieces(dkv, dkvs)
    for piece, out in enumerate(outs):
        gather_rows(grads, dq, chunk_start(piece, half, chunk), dkv, piece)
        out[...] = product(grads, w_ref).astype(BF16)


def home_kernel(*refs):
    dqs, aways, refs = refs[:4], refs[4 : 4 + 4 * CHUNKS], refs[4 + 4 * CHUNKS :]
    homes, w_ref, gots, refs = refs[:4], refs[4], refs[5:-9], refs[-9:]
    dq_out, dk_out, dv_out, keep_out, grads, small_grads, dq, away_dkv, home_dkv = refs
    half = grads.shape[1]
    small = half // CHUNKS
    away = away_dkv.shape[1] // small
    stage_pieces(dq, dqs)
    stage_pieces(home_dkv, homes)

    def write(rows_at, some):
        dq_out[rows_at] = some[0]
        dk_out[rows_at] = some[1]
        dv_out[rows_at] = some[2]

    for chunk in range(CHUNKS):
        stage_pieces(away_dkv, aways[chunk * GROUP : (chunk + 1) * GROUP])
        for piece in range(away):
            start = chunk_start(piece, half, chunk)
            gather_rows(small_grads, dq, start, away_dkv, piece)
            write(pl.ds(start, small), small_grads)
    start = owner_start(away, half)
    gather_rows(grads, dq, start, home_dkv, 0)
    write(pl.ds(start, half), grads)
    keep_out[...] = product(grads, w_ref)
    for i, got in enumerate(gots):
        chunk = i // away
        at = slice(chunk * small, (chunk + 1) * small)
        keep_out[at] = keep_out[at] + got[...].astype(F32)


def add_kernel(keep_ref, *refs):
    gots, out = refs[:-1], refs[-1]
    begin = keep_ref.shape[0] - gots[0].shape[0]
    out[:begin] = keep_ref[:begin].astype(BF16)
    total = keep_ref[begin:]
    for got in gots:
        total = total + got[...].astype(F32)
    out[begin:] = total.astype(BF16)


def body(queries, keys, values, out_grad, log_sum_exp, key_blocks, w_qkv):
    rows, features = queries.shape
    head_count = log_sum_exp.shape[0]
    head_dim = features // head_count
    slots = head_count // GROUP
    blocks_here = rows // BLOCK
    group_blocks = GROUP * blocks_here
    window = group_blocks + 2 * SPAN
    slot_count = key_blocks.shape[1]
    devices = lax.axis_size("var")
    heads = lax.axis_size("head")
    half = rows // heads
    model = w_qkv.shape[1]
    wide = 2 * LANES
    hbm = pl.BlockSpec(memory_space=pltpu.HBM)

    def trade(x, distance):
        return lax.ppermute(x, "var", [(n, n ^ distance) for n in range(devices)])

    def trade_level(x, turn):
        pairs = []
        for n in range(devices):
            other = n - GROUP if (n // GROUP + n + turn) % 2 else n + GROUP
            for h in range(heads):
                if 0 <= other < devices:
                    target = other * heads + h
                else:
                    target = n * heads + (h ^ 1) % heads
                pairs.append((n * heads + h, target))
        return lax.ppermute(x, ("var", "head"), pairs)

    def trade_first(x):
        return trade_level(x, 0)

    def trade_second(x):
        return trade_level(x, 1)

    def swap(pieces):
        got = [pieces[0]] + [None] * (GROUP - 1)
        for distance in (2, 3, 1):
            got[distance] = trade(pieces[distance], distance)
        return got

    def staged(count, width=LANES):
        return pltpu.VMEM((GROUP, count, width), BF16)

    block = (BLOCK, LANES)
    anywhere = pl.BlockSpec(memory_space=pl.ANY)

    def cost(flops, moved):
        return pl.CostEstimate(flops=flops, bytes_accessed=moved, transcendentals=0)

    size = rows * features * 2

    kvs = pl.pallas_call(
        pack_kv_kernel,
        out_shape=(shaped((rows, wide)),) * GROUP,
        in_specs=[hbm] * 2,
        out_specs=(vmem(),) * GROUP,
        scratch_shapes=[pltpu.VMEM((rows, features), BF16)] * 2
        + [staged(rows, wide), pltpu.SemaphoreType.DMA((2, LOADS))],
        compiler_params=params(PACK_MIB),
        cost_estimate=cost(4 * rows * features * BLOCK, 5 * size),
    )(keys, values)
    kvs = swap(kvs)
    *qos, kvs[0] = pl.pallas_call(
        functools.partial(pack_qo_kernel, slots, head_dim),
        out_shape=(shaped((rows + LSE_ROWS, wide)),) * GROUP + (shaped((rows, wide)),),
        in_specs=[vmem()] * 4 + [anywhere],
        out_specs=(vmem(),) * (GROUP + 1),
        scratch_shapes=[staged(rows + LSE_ROWS, wide)],
        compiler_params=params(8),
        cost_estimate=cost(4 * rows * features * BLOCK, 10 * size),
    )(queries, out_grad, log_sum_exp, kvs[0], kvs[1])
    carried = tuple(qos[1:])
    own, first, second, *carried = pl.pallas_call(
        functools.partial(line_kernel, len(carried)),
        out_shape=(shaped((GROUP * rows + rows + LSE_ROWS, wide)),)
        + (shaped((SPAN * BLOCK, wide)),) * 2
        + tuple(shaped(x.shape) for x in carried),
        in_specs=[vmem()] * (GROUP + 1) + [anywhere] * len(carried),
        out_specs=(vmem(),) * 3 + (anywhere,) * len(carried),
        input_output_aliases={GROUP + 1 + i: 3 + i for i in range(len(carried))},
        compiler_params=params(8),
        cost_estimate=cost(0, 5 * size),
    )(*kvs, qos[0], *carried)
    first = trade_first(first)
    second = trade_second(second)
    qos = swap([None, *carried])[1:]

    pairs = group_blocks * slot_count * BLOCK * BLOCK * slots
    tall = (BLOCK, wide)
    acc_scratch = pltpu.VMEM((window,) + tall, F32)
    work = [
        pltpu.VMEM((2, wide, LANES), BF16),
        pltpu.VMEM((2, wide, LANES), BF16),
        pltpu.VMEM((2, wide, wide), BF16),
        pltpu.VMEM((2, slot_count * BLOCK, wide), F32),
        pltpu.VMEM((2, slot_count * BLOCK, wide), F32),
    ]
    smem = pl.BlockSpec(memory_space=pltpu.SMEM)
    outer = (shaped((OUTER,) + tall),) * 2

    def attend_cost(part):
        return pl.CostEstimate(
            flops=int(40 * pairs * head_dim * part),
            bytes_accessed=2_000_000,
            transcendentals=int(pairs * part),
        )

    state = (
        shaped((window,) + tall),
        shaped((window, LANES, BLOCK)),
        shaped((group_blocks, 2, 8, wide), F32),
        shaped((GROUP, rows + LSE_ROWS, wide)),
        shaped((window - 2 * OUTER,) + tall, F32),
        shaped((GROUP, rows, LANES)),
    )
    first, second, *state = pl.pallas_call(
        functools.partial(attend_kernel, False, blocks_here, head_dim),
        out_shape=outer + state,
        in_specs=[smem] + [vmem()] * (2 + GROUP),
        out_specs=(vmem(),) * 8,
        scratch_shapes=[acc_scratch] + work,
        compiler_params=params(16),
        cost_estimate=attend_cost(0.67),
    )(key_blocks, own, first, second, *qos)
    outer_back = (trade_first(first), trade_second(second))
    own_sum, first, second, *dqs = pl.pallas_call(
        functools.partial(attend_kernel, True, blocks_here, head_dim),
        out_shape=(shaped((group_blocks,) + tall, F32),)
        + outer
        + (shaped((rows, LANES)),) * GROUP,
        in_specs=[smem] + [vmem()] * 6,
        out_specs=(vmem(),) * (3 + GROUP),
        scratch_shapes=[acc_scratch] + work + [staged(rows)],
        compiler_params=params(16),
        cost_estimate=attend_cost(0.33),
    )(key_blocks, *state)
    inner_back = (trade_first(first), trade_second(second))
    carried = tuple(dqs[1:])
    *carried, own_sum = pl.pallas_call(
        functools.partial(combine_outer_kernel, 2 * len(carried)),
        out_shape=tuple(shaped(x.shape) for x in carried) + (shaped((group_blocks,) + tall, F32),),
        in_specs=[vmem()] * 3 + [anywhere] * len(carried),
        out_specs=(anywhere,) * len(carried) + (vmem(),),
        input_output_aliases={3 + i: i for i in range(len(carried))},
        compiler_params=params(8),
        cost_estimate=cost(0, 4 * size),
    )(own_sum, *outer_back, *carried)
    dqs = swap([dqs[0], *carried])
    split = pl.pallas_call(
        combine_kernel,
        out_shape=(shaped(((rows - half) // CHUNKS, wide)),) * (CHUNKS * GROUP)
        + (shaped((half, wide)),) * GROUP,
        in_specs=[vmem()] * 3 + [anywhere] * (GROUP - 1),
        out_specs=(vmem(),) * ((CHUNKS + 1) * GROUP),
        scratch_shapes=[pltpu.VMEM((group_blocks,) + tall, F32), staged(rows, wide)],
        compiler_params=params(8),
        cost_estimate=cost(0, 8 * size),
    )(own_sum, *inner_back, *dqs[1:])
    aways = [swap(split[c * GROUP : (c + 1) * GROUP]) for c in range(CHUNKS)]
    homes = swap(split[CHUNKS * GROUP :])

    small = half // CHUNKS
    grads = pltpu.VMEM((3, half, features), BF16)
    small_grads = pltpu.VMEM((3, small, features), BF16)
    away_stage = staged((rows - half) // CHUNKS, wide)
    sends, after = [], ()
    for chunk in range(CHUNKS):
        sent = pl.pallas_call(
            functools.partial(away_kernel, chunk),
            out_shape=(shaped((small, model)),) * (heads - 1),
            in_specs=[vmem()] * (2 * GROUP + 1) + [anywhere] * len(after),
            out_specs=(vmem(),) * (heads - 1),
            scratch_shapes=[small_grads, staged(rows), away_stage],
            compiler_params=params(8),
            cost_estimate=cost(6 * (rows - half) * features * model // CHUNKS, 4_000_000),
        )(*dqs, *aways[chunk], w_qkv, *after)
        after = (sent[0],)
        got = []
        for piece, send in enumerate(sent):
            turn = [(n, (n + piece + 1) % heads) for n in range(heads)]
            got.append(lax.ppermute(send, "head", turn))
        sends.append(got)
    early = [x for got in sends[:-1] for x in got]
    dq_out, dk_out, dv_out, keep = pl.pallas_call(
        home_kernel,
        out_shape=(shaped((rows, features)),) * 3 + (shaped((half, model), F32),),
        in_specs=[vmem()] * ((2 + CHUNKS) * GROUP + 1 + len(early)),
        out_specs=(vmem(),) * 4,
        scratch_shapes=[grads, small_grads, staged(rows), away_stage, staged(half, wide)],
        compiler_params=params(8),
        cost_estimate=cost(6 * half * features * model, 6_000_000),
    )(*dqs, *[x for pieces in aways for x in pieces], *homes, w_qkv, *early)
    total = pl.pallas_call(
        add_kernel,
        out_shape=shaped((half, model)),
        in_specs=[vmem()] * heads,
        out_specs=vmem(),
        compiler_params=params(8),
    )(keep, *sends[-1])
    return dq_out, dk_out, dv_out, total


def solution(mesh):
    in_specs = (
        P("var", "head"),
        P("var", "head"),
        P("var", "head"),
        P("var", "head"),
        P("head", "var"),
        P(),
        P(None, None, "head"),
    )
    out_specs = (P("var", "head"), P("var", "head"), P("var", "head"), P(("var", "head"), None))
    return jax.shard_map(body, mesh=mesh, in_specs=in_specs, out_specs=out_specs, check_vma=False)
```

```python
import functools

import jax
import jax.numpy as jnp
from jax import lax
from jax.experimental import pallas as pl
from jax.experimental.pallas import tpu as pltpu
from jax.sharding import PartitionSpec as P

PATCHES = 16
BLOCK = 128
HALF = BLOCK // 2
SPAN = 8
OUTER = SPAN // 2
GROUP = 4
LANES = 128
LSE_ROWS = 16
PARTS = 4
LOADS = 3
F32 = jnp.float32
BF16 = jnp.bfloat16
MIB = 1024 * 1024
PACK_MIB = 62


def vmem():
    return pl.BlockSpec(memory_space=pltpu.VMEM)


def params(mib):
    return pltpu.CompilerParams(vmem_limit_bytes=mib * MIB)


def shaped(shape, dtype=BF16):
    return jax.ShapeDtypeStruct(shape, dtype)


def dot(a, b):
    return jnp.dot(a, b, preferred_element_type=F32)


def dot_nt(a, b):
    return lax.dot_general(a, b, (((1,), (1,)), ((), ())), preferred_element_type=F32)


def token_at(place):
    return (((place & (HALF - 1)) >> 3) << 4) + ((place >> 6) << 3) + (place & 7)


def one_where(mask):
    return jnp.where(mask, 1.0, 0.0).astype(BF16)


def reorder_matrix(inverse):
    row = lax.broadcasted_iota(jnp.int32, (BLOCK, BLOCK), 0)
    col = lax.broadcasted_iota(jnp.int32, (BLOCK, BLOCK), 1)
    return one_where(row == token_at(col)) if inverse else one_where(col == token_at(row))


def split_three(x):
    high = x.astype(BF16).astype(F32)
    rest = x - high
    mid = rest.astype(BF16).astype(F32)
    return high, mid, rest - mid


def widen(x):
    if x.shape[1] == LANES:
        return x
    return jnp.concatenate([x, jnp.zeros((x.shape[0], LANES - x.shape[1]), x.dtype)], axis=1)


def send_pieces(outs, stage):
    me = lax.axis_index("var") % GROUP
    for distance, out in enumerate(outs):
        out[...] = stage[me ^ distance]


def stage_pieces(stage, pieces):
    me = lax.axis_index("var") % GROUP
    for distance, piece in enumerate(pieces):
        stage[me ^ distance] = piece[...]


def load_all(pairs, sems):
    copies = []
    for i, (source, target) in enumerate(pairs):
        rows = source.shape[0] // LOADS
        for part in range(LOADS):
            at = pl.ds(part * rows, rows)
            copies.append(pltpu.make_async_copy(source.at[at], target.at[at], sems.at[i, part]))
    for copy in copies:
        copy.start()
    return [copies[i * LOADS : (i + 1) * LOADS] for i in range(len(pairs))]


def reorder_into(staged, half, ref, scale=None):
    rows, features = ref.shape
    width = features // GROUP
    order = reorder_matrix(False)
    for b in range(rows // BLOCK):
        at = slice(b * BLOCK, (b + 1) * BLOCK)
        moved = dot(order, ref[at])
        if scale is not None:
            moved = moved * scale
        moved = moved.astype(BF16)
        for member in range(GROUP):
            staged[member, at, half * LANES : (half + 1) * LANES] = widen(
                moved[:, member * width : (member + 1) * width]
            )


def pack_kv_kernel(k_hbm, v_hbm, *rest):
    outs, (k_ref, v_ref, turned, sems) = rest[:GROUP], rest[GROUP:]
    arrivals = load_all([(k_hbm, k_ref), (v_hbm, v_ref)], sems)
    for half, ref in enumerate((k_ref, v_ref)):
        for copy in arrivals[half]:
            copy.wait()
        reorder_into(turned, half, ref)
    send_pieces(outs, turned)


def pack_qo_kernel(slots, head_dim, q_ref, g_ref, lse_ref, mine_ref, after_ref, *rest):
    outs, (hold, qo_ref) = rest[:GROUP], rest[GROUP:]
    hold[...] = mine_ref[...]
    rows = q_ref.shape[0]
    blocks = rows // BLOCK
    reorder_into(qo_ref, 0, q_ref, head_dim ** (-0.5))
    reorder_into(qo_ref, 1, g_ref)
    token = lax.broadcasted_iota(jnp.int32, (BLOCK, 2 * LANES), 0)
    lane = lax.broadcasted_iota(jnp.int32, (BLOCK, 2 * LANES), 1)
    place = ((lane >> 7) << 6) + (lane & (HALF - 1))
    hit = token == token_at(place)
    upper = (lane & HALF) != 0
    spread = [one_where(hit & ~upper), one_where(hit & upper)]
    for member in range(GROUP):
        total = None
        for slot in range(slots):
            lse = lse_ref[member * slots + slot : member * slots + slot + 1, :]
            parts = [
                part[:, b * BLOCK : (b + 1) * BLOCK]
                for part in split_three(lse)
                for b in range(blocks)
            ]
            parts.append(jnp.zeros((LSE_ROWS - len(parts), BLOCK), F32))
            moved = dot(jnp.concatenate(parts, axis=0).astype(BF16), spread[slot])
            total = moved if total is None else total + moved
        qo_ref[member, rows:] = total.astype(BF16)
    send_pieces(outs, qo_ref)


def below_first():
    me = lax.axis_index("var")
    return (me // GROUP + me) % 2


def exchange_start(group_blocks):
    odd = below_first()
    reach = group_blocks - SPAN
    return (1 - odd) * reach, odd * reach


def line_kernel(carried, *refs):
    pieces, query_piece, refs = refs[:GROUP], refs[GROUP], refs[GROUP + 1 + carried :]
    own, first_out, second_out = refs[:3]
    rows = pieces[0].shape[0]
    own[GROUP * rows :] = query_piece[...]
    blocks = rows // BLOCK
    me = lax.axis_index("var") % GROUP
    for distance in range(GROUP):
        at = pl.ds(pl.multiple_of((me ^ distance) * rows, rows), rows)
        own[at] = pieces[distance][...]
    first, second = exchange_start(GROUP * blocks)
    for start, out in ((first, first_out), (second, second_out)):
        out[...] = own[pl.ds(pl.multiple_of(start * BLOCK, BLOCK), SPAN * BLOCK)]


def attend_kernel(last, blocks_here, head_dim, kb_ref, *refs):
    if last:
        kv_win, k_turn, shifts, qo_ref, before, dq_before, *refs = refs
        own_out, first_out, second_out, *refs = refs
        dq_outs, refs = refs[:GROUP], refs[GROUP:]
        acc, queries, grads, crossed, prob, slope, dq_all = refs
    else:
        kv_refs, refs = refs[:3], refs[3:]
        qo_pieces, refs = refs[: GROUP - 1], refs[GROUP - 1 :]
        first_out, second_out, kv_win, k_turn, shifts, qo_ref, kept_out, dq_all, *refs = refs
        acc, queries, grads, crossed, prob, slope = refs
    group_blocks = GROUP * blocks_here
    window = group_blocks + 2 * SPAN
    rows = blocks_here * BLOCK
    slot_count = kb_ref.shape[1]
    scale = head_dim ** (-0.5)
    base = (lax.axis_index("var") // GROUP) * group_blocks
    odd = below_first()
    low = slice(0, LANES)
    high = slice(LANES, 2 * LANES)

    acc[...] = jnp.zeros_like(acc)
    crossed[...] = jnp.zeros_like(crossed)
    if last:
        dq_all[...] = dq_before[...]
    else:
        top = window - SPAN
        for ref, start, count in zip(
            kv_refs, (SPAN, (1 - odd) * top, odd * top), (group_blocks, SPAN, SPAN)
        ):
            kv_win[pl.ds(start, count)] = ref[: count * BLOCK].reshape(count, BLOCK, 2 * LANES)
        own_queries = kv_refs[0].at[pl.ds(group_blocks * BLOCK, rows + LSE_ROWS)]
        stage_pieces(qo_ref, (own_queries, *qo_pieces))
        key_patch = lax.broadcasted_iota(jnp.int32, (8, LANES), 0)
        query_patch = lax.broadcasted_iota(jnp.int32, (8, LANES), 1) & 7
        usable = key_patch <= query_patch
        for member in range(GROUP):
            parts = qo_ref[member, rows:].astype(F32)
            for local in range(blocks_here):
                lse = (
                    parts[local : local + 1] + parts[blocks_here + local : blocks_here + local + 1]
                ) + parts[2 * blocks_here + local : 2 * blocks_here + local + 1]
                at = member * blocks_here + local
                shifts[at, 0, :, low] = jnp.where(usable, -lse[:, low], -1e30)
                shifts[at, 0, :, high] = jnp.broadcast_to(-lse[:, high], (8, LANES))
                shifts[at, 1, :, low] = jnp.where(usable, -lse[:, high], -1e30)

        @pl.loop(0, window)
        def _(block):
            k_turn[block] = kv_win[block, :, low].T

    unorder = reorder_matrix(True)
    lane = lax.broadcasted_iota(jnp.int32, (HALF, LANES), 1)
    head_a = lane < HALF

    def picks(query_block):
        return [kb_ref[base + query_block, s] - base + SPAN for s in range(slot_count)]

    def lay_out(member, local, buf):
        at = pl.multiple_of(local * BLOCK, BLOCK)
        for part in range(2):
            rows_at = pl.ds(at + part * HALF, HALF)
            for cols, target in ((low, queries), (high, grads)):
                tile = qo_ref[member, rows_at, cols]
                zero = jnp.zeros_like(tile)
                both = jnp.concatenate(
                    [jnp.where(head_a, tile, zero), jnp.where(head_a, zero, tile)], axis=0
                )
                target[buf, part * BLOCK : (part + 1) * BLOCK] = both
                if part == 1:
                    side = 0 if target is queries else 1
                    crossed[
                        buf, side * BLOCK : (side + 1) * BLOCK, side * LANES : (side + 1) * LANES
                    ] = both

    def gather(index, rows_of, cols):
        return jnp.concatenate([kv_win[i, rows_of, cols] for i in index], axis=0)

    early = slice(0, HALF)
    late = slice(HALF, BLOCK)
    both_cols = slice(0, 2 * LANES)
    early_rows = slot_count * HALF
    part_slots = slot_count // PARTS
    part_rows = part_slots * HALF

    def forward_part(index, query_block, buf, part):
        some = index[part * part_slots : (part + 1) * part_slots]
        at = slice(part * part_rows, (part + 1) * part_rows)
        after = slice(early_rows + part * part_rows, early_rows + (part + 1) * part_rows)
        s = dot_nt(gather(some, early, low), queries[buf])
        g = dot_nt(gather(some, early, high), grads[buf])
        x = dot_nt(gather(some, late, both_cols), crossed[buf])
        shift = shifts[query_block, 0][None]
        p = jnp.exp(s.reshape(part_rows // 8, 8, 2 * LANES) + shift).reshape(part_rows, 2 * LANES)
        prob[buf, at] = p
        slope[buf, at] = g
        delta = jnp.sum((p * g).reshape(part_rows // 8, 8, 2 * LANES), axis=0)
        late_shift = shifts[query_block, 1, :, low][None]
        q = jnp.exp(x[:, low].reshape(part_rows // 8, 8, LANES) + late_shift).reshape(
            part_rows, LANES
        )
        prob[buf, after, low] = q
        slope[buf, after, low] = x[:, high]
        more = jnp.sum((q * x[:, high]).reshape(part_rows // 8, 8, LANES), axis=0)
        return delta[:, low], delta[:, high] + more

    def backward_part(index, buf, delta, part):
        at = slice(part * part_rows, (part + 1) * part_rows)
        after = slice(early_rows + part * part_rows, early_rows + (part + 1) * part_rows)
        p = prob[buf, at]
        ds = (p * (slope[buf, at] - delta)).astype(BF16)
        q = prob[buf, after, low]
        ds_late = (q * (slope[buf, after, low] - delta[:, high])).astype(BF16)
        dk = dot(ds, queries[buf])
        dv = dot(p.astype(BF16), grads[buf])
        r = dot(jnp.concatenate([ds_late, q.astype(BF16)], axis=1), crossed[buf])
        nothing = jnp.zeros((HALF, LANES), BF16)
        pieces = []
        for s in range(part_slots):
            at = slice(s * HALF, (s + 1) * HALF)
            where = index[part * part_slots + s]
            acc[where, early, low] = acc[where, early, low] + dk[at]
            acc[where, early, high] = acc[where, early, high] + dv[at]
            acc[where, late] = acc[where, late] + r[at]
            pieces.append(ds[at])
            pieces.append(jnp.concatenate([nothing, ds_late[at]], axis=1))
        keys_turned = jnp.concatenate(
            [k_turn[i] for i in index[part * part_slots : (part + 1) * part_slots]], axis=1
        )
        return dot(keys_turned, jnp.concatenate(pieces, axis=0))

    def write_dq(query_block, dq):
        dq = dq * scale
        halves = []
        for cols in (low, high):
            turned = dq[:, cols].T
            halves.append(jnp.where(head_a, turned[:HALF], turned[HALF:]))
        moved = dot(unorder, jnp.concatenate(halves, axis=0).astype(BF16)).astype(BF16)
        local = pl.multiple_of((query_block % blocks_here) * BLOCK, BLOCK)
        dq_all[query_block // blocks_here, pl.ds(local, BLOCK)] = moved

    def run(ahead, ahead_buf, behind, behind_buf, delta):
        sums, dq = None, None
        if ahead is not None:
            lay_out(ahead // blocks_here, ahead % blocks_here, ahead_buf)
            ahead_index = picks(ahead)
        if behind is not None:
            behind_index = picks(behind)
        for part in range(PARTS):
            if ahead is not None:
                more = forward_part(ahead_index, ahead, ahead_buf, part)
                sums = more if sums is None else (sums[0] + more[0], sums[1] + more[1])
            if behind is not None:
                more = backward_part(behind_index, behind_buf, delta, part)
                dq = more if dq is None else dq + more
        if behind is not None:
            write_dq(behind, dq)
        if ahead is None:
            return None
        return jnp.concatenate([jnp.sum(x, axis=0, keepdims=True) for x in sums], axis=1)

    def block_of(j):
        if last:
            return j + OUTER
        return j + jnp.where(j < OUTER, 0, group_blocks - 2 * OUTER)

    count = group_blocks - 2 * OUTER if last else 2 * OUTER
    delta = run(block_of(0), 0, None, None, None)

    def step(j, delta):
        delta = run(block_of(2 * j + 1), 1, block_of(2 * j), 0, delta)
        return run(block_of(2 * j + 2), 0, block_of(2 * j + 1), 1, delta)

    delta = lax.fori_loop(0, (count - 1) // 2, step, delta)
    if count % 2 == 0:
        delta = run(block_of(count - 1), 1, block_of(count - 2), 0, delta)
    run(None, None, block_of(count - 1), (count - 1) % 2, delta)

    groups = BLOCK // 16

    def in_token_order(part):
        blocks = part.shape[0]
        part = part.reshape(blocks, 2, groups, 8, 2 * LANES)
        return jnp.swapaxes(part, 1, 2).reshape(blocks, BLOCK, 2 * LANES)

    if last:
        acc[OUTER : window - OUTER] = acc[OUTER : window - OUTER] + before[...]
        top = window - SPAN
        for out, side in ((first_out, 1 - odd), (second_out, odd)):
            start = OUTER + side * (top - OUTER)
            out[...] = in_token_order(acc[pl.ds(start, OUTER)]).astype(BF16)
        own_out[...] = in_token_order(acc[SPAN : SPAN + group_blocks])
        send_pieces(dq_outs, dq_all)
    else:
        for out, side in ((first_out, 1 - odd), (second_out, odd)):
            start = side * (window - OUTER)
            out[...] = in_token_order(acc[pl.ds(start, OUTER)]).astype(BF16)
        kept_out[...] = acc[OUTER : window - OUTER]


def owner_start(piece, half):
    heads = lax.axis_size("head")
    return pl.multiple_of(((lax.axis_index("head") + 1 + piece) % heads) * half, half)


def add_arrived(total, starts, refs):
    level = lax.axis_index("var") // GROUP
    levels = lax.axis_size("var") // GROUP
    odd = below_first()
    for side, ref in zip((1 - odd, odd), refs):
        other = level - 1 + 2 * side
        start = jnp.where(side == 1, starts[1], starts[0])

        @pl.when((other >= 0) & (other < levels))
        def _(start=start, ref=ref):
            at = pl.ds(start, OUTER)
            total[at] = total[at] + ref[...].astype(F32)


def combine_outer_kernel(carried, own_ref, first_ref, second_ref, *refs):
    total = refs[carried]
    total[...] = own_ref[...]
    add_arrived(total, (SPAN - OUTER, own_ref.shape[0] - SPAN), (first_ref, second_ref))


def combine_kernel(own_ref, first_ref, second_ref, *rest):
    aways, homes, (total, moved) = rest[:GROUP], rest[GROUP : 2 * GROUP], rest[2 * GROUP :]
    total[...] = own_ref[...]
    add_arrived(total, (0, own_ref.shape[0] - OUTER), (first_ref, second_ref))
    moved[...] = total[...].astype(BF16).reshape(moved.shape)
    half = homes[0].shape[0]
    away = aways[0].shape[0] // half
    me = lax.axis_index("var") % GROUP
    for distance in range(GROUP):
        member = me ^ distance
        for piece in range(away):
            aways[distance][piece * half : (piece + 1) * half] = moved[
                member, pl.ds(owner_start(piece, half), half)
            ]
        homes[distance][...] = moved[member, pl.ds(owner_start(away, half), half)]


def gather_rows(grads, dq, start, dkv, dkv_at):
    half = grads.shape[1]
    width = grads.shape[2] // GROUP
    for member in range(GROUP):
        at = slice(member * width, (member + 1) * width)
        both = dkv[member, dkv_at * half : (dkv_at + 1) * half]
        grads[0, :, at] = dq[member, pl.ds(start, half)][:, :width]
        grads[1, :, at] = both[:, :width]
        grads[2, :, at] = both[:, LANES : LANES + width]


def product(grads, w_ref):
    total = dot_nt(grads[0], w_ref[0])
    for s in (1, 2):
        total = total + dot_nt(grads[s], w_ref[s])
    return total


def away_kernel(*refs):
    dqs, dkvs, (w_ref, *rest) = refs[:4], refs[4:8], refs[8:]
    outs, (grads, dq, dkv) = rest[:-3], rest[-3:]
    half = grads.shape[1]
    stage_pieces(dq, dqs)
    stage_pieces(dkv, dkvs)
    for piece, out in enumerate(outs):
        gather_rows(grads, dq, owner_start(piece, half), dkv, piece)
        out[...] = product(grads, w_ref).astype(BF16)


def home_kernel(*refs):
    dqs, aways, homes, rest = refs[:4], refs[4:8], refs[8:12], refs[12:]
    w_ref, dq_out, dk_out, dv_out, keep_out, grads, dq, away_dkv, home_dkv = rest
    half = grads.shape[1]
    away = away_dkv.shape[1] // half
    stage_pieces(dq, dqs)
    stage_pieces(away_dkv, aways)
    stage_pieces(home_dkv, homes)
    for piece in range(away + 1):
        start = owner_start(piece, half)
        if piece < away:
            gather_rows(grads, dq, start, away_dkv, piece)
        else:
            gather_rows(grads, dq, start, home_dkv, 0)
        at = pl.ds(start, half)
        dq_out[at] = grads[0]
        dk_out[at] = grads[1]
        dv_out[at] = grads[2]
    keep_out[...] = product(grads, w_ref)


def body(queries, keys, values, out_grad, log_sum_exp, key_blocks, w_qkv):
    rows, features = queries.shape
    head_count = log_sum_exp.shape[0]
    head_dim = features // head_count
    slots = head_count // GROUP
    blocks_here = rows // BLOCK
    group_blocks = GROUP * blocks_here
    window = group_blocks + 2 * SPAN
    slot_count = key_blocks.shape[1]
    devices = lax.axis_size("var")
    heads = lax.axis_size("head")
    half = rows // heads
    model = w_qkv.shape[1]
    wide = 2 * LANES
    hbm = pl.BlockSpec(memory_space=pltpu.HBM)

    def trade(x, distance):
        return lax.ppermute(x, "var", [(n, n ^ distance) for n in range(devices)])

    def trade_level(x, turn):
        pairs = []
        for n in range(devices):
            other = n - GROUP if (n // GROUP + n + turn) % 2 else n + GROUP
            for h in range(heads):
                if 0 <= other < devices:
                    target = other * heads + h
                else:
                    target = n * heads + (h ^ 1) % heads
                pairs.append((n * heads + h, target))
        return lax.ppermute(x, ("var", "head"), pairs)

    def trade_first(x):
        return trade_level(x, 0)

    def trade_second(x):
        return trade_level(x, 1)

    def swap(pieces):
        got = [pieces[0]] + [None] * (GROUP - 1)
        for distance in (2, 3, 1):
            got[distance] = trade(pieces[distance], distance)
        return got

    def staged(count, width=LANES):
        return pltpu.VMEM((GROUP, count, width), BF16)

    block = (BLOCK, LANES)
    anywhere = pl.BlockSpec(memory_space=pl.ANY)

    def cost(flops, moved):
        return pl.CostEstimate(flops=flops, bytes_accessed=moved, transcendentals=0)

    size = rows * features * 2

    kvs = pl.pallas_call(
        pack_kv_kernel,
        out_shape=(shaped((rows, wide)),) * GROUP,
        in_specs=[hbm] * 2,
        out_specs=(vmem(),) * GROUP,
        scratch_shapes=[pltpu.VMEM((rows, features), BF16)] * 2
        + [staged(rows, wide), pltpu.SemaphoreType.DMA((2, LOADS))],
        compiler_params=params(PACK_MIB),
        cost_estimate=cost(4 * rows * features * BLOCK, 5 * size),
    )(keys, values)
    kvs = swap(kvs)
    *qos, kvs[0] = pl.pallas_call(
        functools.partial(pack_qo_kernel, slots, head_dim),
        out_shape=(shaped((rows + LSE_ROWS, wide)),) * GROUP + (shaped((rows, wide)),),
        in_specs=[vmem()] * 4 + [anywhere],
        out_specs=(vmem(),) * (GROUP + 1),
        scratch_shapes=[staged(rows + LSE_ROWS, wide)],
        compiler_params=params(8),
        cost_estimate=cost(4 * rows * features * BLOCK, 10 * size),
    )(queries, out_grad, log_sum_exp, kvs[0], kvs[1])
    carried = tuple(qos[1:])
    own, first, second, *carried = pl.pallas_call(
        functools.partial(line_kernel, len(carried)),
        out_shape=(shaped((GROUP * rows + rows + LSE_ROWS, wide)),)
        + (shaped((SPAN * BLOCK, wide)),) * 2
        + tuple(shaped(x.shape) for x in carried),
        in_specs=[vmem()] * (GROUP + 1) + [anywhere] * len(carried),
        out_specs=(vmem(),) * 3 + (anywhere,) * len(carried),
        input_output_aliases={GROUP + 1 + i: 3 + i for i in range(len(carried))},
        compiler_params=params(8),
        cost_estimate=cost(0, 5 * size),
    )(*kvs, qos[0], *carried)
    first = trade_first(first)
    second = trade_second(second)
    qos = swap([None, *carried])[1:]

    pairs = group_blocks * slot_count * BLOCK * BLOCK * slots
    tall = (BLOCK, wide)
    acc_scratch = pltpu.VMEM((window,) + tall, F32)
    work = [
        pltpu.VMEM((2, wide, LANES), BF16),
        pltpu.VMEM((2, wide, LANES), BF16),
        pltpu.VMEM((2, wide, wide), BF16),
        pltpu.VMEM((2, slot_count * BLOCK, wide), F32),
        pltpu.VMEM((2, slot_count * BLOCK, wide), F32),
    ]
    smem = pl.BlockSpec(memory_space=pltpu.SMEM)
    outer = (shaped((OUTER,) + tall),) * 2

    def attend_cost(part):
        return pl.CostEstimate(
            flops=int(40 * pairs * head_dim * part),
            bytes_accessed=2_000_000,
            transcendentals=int(pairs * part),
        )

    state = (
        shaped((window,) + tall),
        shaped((window, LANES, BLOCK)),
        shaped((group_blocks, 2, 8, wide), F32),
        shaped((GROUP, rows + LSE_ROWS, wide)),
        shaped((window - 2 * OUTER,) + tall, F32),
        shaped((GROUP, rows, LANES)),
    )
    first, second, *state = pl.pallas_call(
        functools.partial(attend_kernel, False, blocks_here, head_dim),
        out_shape=outer + state,
        in_specs=[smem] + [vmem()] * (2 + GROUP),
        out_specs=(vmem(),) * 8,
        scratch_shapes=[acc_scratch] + work,
        compiler_params=params(16),
        cost_estimate=attend_cost(0.67),
    )(key_blocks, own, first, second, *qos)
    outer_back = (trade_first(first), trade_second(second))
    own_sum, first, second, *dqs = pl.pallas_call(
        functools.partial(attend_kernel, True, blocks_here, head_dim),
        out_shape=(shaped((group_blocks,) + tall, F32),)
        + outer
        + (shaped((rows, LANES)),) * GROUP,
        in_specs=[smem] + [vmem()] * 6,
        out_specs=(vmem(),) * (3 + GROUP),
        scratch_shapes=[acc_scratch] + work + [staged(rows)],
        compiler_params=params(16),
        cost_estimate=attend_cost(0.33),
    )(key_blocks, *state)
    inner_back = (trade_first(first), trade_second(second))
    carried = tuple(dqs[1:])
    *carried, own_sum = pl.pallas_call(
        functools.partial(combine_outer_kernel, 2 * len(carried)),
        out_shape=tuple(shaped(x.shape) for x in carried) + (shaped((group_blocks,) + tall, F32),),
        in_specs=[vmem()] * 3 + [anywhere] * len(carried),
        out_specs=(anywhere,) * len(carried) + (vmem(),),
        input_output_aliases={3 + i: i for i in range(len(carried))},
        compiler_params=params(8),
        cost_estimate=cost(0, 4 * size),
    )(own_sum, *outer_back, *carried)
    dqs = swap([dqs[0], *carried])
    split = pl.pallas_call(
        combine_kernel,
        out_shape=(shaped((rows - half, wide)),) * GROUP + (shaped((half, wide)),) * GROUP,
        in_specs=[vmem()] * 3,
        out_specs=(vmem(),) * (2 * GROUP),
        scratch_shapes=[pltpu.VMEM((group_blocks,) + tall, F32), staged(rows, wide)],
        compiler_params=params(8),
        cost_estimate=cost(0, 8 * size),
    )(own_sum, *inner_back)
    aways = swap(split[:GROUP])
    homes = swap(split[GROUP:])

    grads = pltpu.VMEM((3, half, features), BF16)
    sends = pl.pallas_call(
        away_kernel,
        out_shape=(shaped((half, model)),) * (heads - 1),
        in_specs=[vmem()] * (2 * GROUP + 1),
        out_specs=(vmem(),) * (heads - 1),
        scratch_shapes=[grads, staged(rows), staged(rows - half, wide)],
        compiler_params=params(8),
        cost_estimate=cost(6 * (rows - half) * features * model, 4_000_000),
    )(*dqs, *aways, w_qkv)
    dq_out, dk_out, dv_out, total = pl.pallas_call(
        home_kernel,
        out_shape=(shaped((rows, features)),) * 3 + (shaped((half, model), F32),),
        in_specs=[vmem()] * (3 * GROUP + 1),
        out_specs=(vmem(),) * 4,
        scratch_shapes=[grads, staged(rows), staged(rows - half, wide), staged(half, wide)],
        compiler_params=params(8),
        cost_estimate=cost(6 * half * features * model, 6_000_000),
    )(*dqs, *aways, *homes, w_qkv)
    for piece, send in enumerate(sends):
        got = lax.ppermute(send, "head", [(n, (n + piece + 1) % heads) for n in range(heads)])
        total = total + got.astype(F32)
    return dq_out, dk_out, dv_out, total.astype(BF16)


def solution(mesh):
    in_specs = (
        P("var", "head"),
        P("var", "head"),
        P("var", "head"),
        P("var", "head"),
        P("head", "var"),
        P(),
        P(None, None, "head"),
    )
    out_specs = (P("var", "head"), P("var", "head"), P("var", "head"), P(("var", "head"), None))
    return jax.shard_map(body, mesh=mesh, in_specs=in_specs, out_specs=out_specs, check_vma=False)
```

```python
import functools

import jax
import jax.numpy as jnp
from jax import lax
from jax.experimental import pallas as pl
from jax.experimental.pallas import tpu as pltpu
from jax.sharding import PartitionSpec as P

PATCHES = 16
BLOCK = 128
HALF = BLOCK // 2
SPAN = 8
OUTER = SPAN // 2
GROUP = 4
LANES = 128
LSE_ROWS = 16
PARTS = 2
LOADS = 3
F32 = jnp.float32
BF16 = jnp.bfloat16
MIB = 1024 * 1024
PACK_MIB = 62


def vmem():
    return pl.BlockSpec(memory_space=pltpu.VMEM)


def params(mib):
    return pltpu.CompilerParams(vmem_limit_bytes=mib * MIB)


def shaped(shape, dtype=BF16):
    return jax.ShapeDtypeStruct(shape, dtype)


def dot(a, b):
    return jnp.dot(a, b, preferred_element_type=F32)


def dot_nt(a, b):
    return lax.dot_general(a, b, (((1,), (1,)), ((), ())), preferred_element_type=F32)


def token_at(place):
    return (((place & (HALF - 1)) >> 3) << 4) + ((place >> 6) << 3) + (place & 7)


def one_where(mask):
    return jnp.where(mask, 1.0, 0.0).astype(BF16)


def reorder_matrix(inverse):
    row = lax.broadcasted_iota(jnp.int32, (BLOCK, BLOCK), 0)
    col = lax.broadcasted_iota(jnp.int32, (BLOCK, BLOCK), 1)
    return one_where(row == token_at(col)) if inverse else one_where(col == token_at(row))


def split_three(x):
    high = x.astype(BF16).astype(F32)
    rest = x - high
    mid = rest.astype(BF16).astype(F32)
    return high, mid, rest - mid


def widen(x):
    if x.shape[1] == LANES:
        return x
    return jnp.concatenate([x, jnp.zeros((x.shape[0], LANES - x.shape[1]), x.dtype)], axis=1)


def send_pieces(outs, stage):
    me = lax.axis_index("var") % GROUP
    for distance, out in enumerate(outs):
        out[...] = stage[me ^ distance]


def stage_pieces(stage, pieces):
    me = lax.axis_index("var") % GROUP
    for distance, piece in enumerate(pieces):
        stage[me ^ distance] = piece[...]


def load_all(pairs, sems):
    copies = []
    for i, (source, target) in enumerate(pairs):
        rows = source.shape[0] // LOADS
        for part in range(LOADS):
            at = pl.ds(part * rows, rows)
            copies.append(pltpu.make_async_copy(source.at[at], target.at[at], sems.at[i, part]))
    for copy in copies:
        copy.start()
    return [copies[i * LOADS : (i + 1) * LOADS] for i in range(len(pairs))]


def reorder_into(staged, half, ref, scale=None):
    rows, features = ref.shape
    width = features // GROUP
    order = reorder_matrix(False)
    for b in range(rows // BLOCK):
        at = slice(b * BLOCK, (b + 1) * BLOCK)
        moved = dot(order, ref[at])
        if scale is not None:
            moved = moved * scale
        moved = moved.astype(BF16)
        for member in range(GROUP):
            staged[member, at, half * LANES : (half + 1) * LANES] = widen(
                moved[:, member * width : (member + 1) * width]
            )


def pack_kv_kernel(k_hbm, v_hbm, *rest):
    outs, (k_ref, v_ref, turned, sems) = rest[:GROUP], rest[GROUP:]
    arrivals = load_all([(k_hbm, k_ref), (v_hbm, v_ref)], sems)
    for half, ref in enumerate((k_ref, v_ref)):
        for copy in arrivals[half]:
            copy.wait()
        reorder_into(turned, half, ref)
    send_pieces(outs, turned)


def pack_qo_kernel(slots, head_dim, q_ref, g_ref, lse_ref, mine_ref, after_ref, *rest):
    outs, (hold, qo_ref) = rest[:GROUP], rest[GROUP:]
    hold[...] = mine_ref[...]
    rows = q_ref.shape[0]
    blocks = rows // BLOCK
    reorder_into(qo_ref, 0, q_ref, head_dim ** (-0.5))
    reorder_into(qo_ref, 1, g_ref)
    token = lax.broadcasted_iota(jnp.int32, (BLOCK, 2 * LANES), 0)
    lane = lax.broadcasted_iota(jnp.int32, (BLOCK, 2 * LANES), 1)
    place = ((lane >> 7) << 6) + (lane & (HALF - 1))
    hit = token == token_at(place)
    upper = (lane & HALF) != 0
    spread = [one_where(hit & ~upper), one_where(hit & upper)]
    for member in range(GROUP):
        total = None
        for slot in range(slots):
            lse = lse_ref[member * slots + slot : member * slots + slot + 1, :]
            parts = [
                part[:, b * BLOCK : (b + 1) * BLOCK]
                for part in split_three(lse)
                for b in range(blocks)
            ]
            parts.append(jnp.zeros((LSE_ROWS - len(parts), BLOCK), F32))
            moved = dot(jnp.concatenate(parts, axis=0).astype(BF16), spread[slot])
            total = moved if total is None else total + moved
        qo_ref[member, rows:] = total.astype(BF16)
    send_pieces(outs, qo_ref)


def below_first():
    me = lax.axis_index("var")
    return (me // GROUP + me) % 2


def exchange_start(group_blocks):
    odd = below_first()
    reach = group_blocks - SPAN
    return (1 - odd) * reach, odd * reach


def line_kernel(carried, *refs):
    pieces, query_piece, refs = refs[:GROUP], refs[GROUP], refs[GROUP + 1 + carried :]
    own, first_out, second_out = refs[:3]
    rows = pieces[0].shape[0]
    own[GROUP * rows :] = query_piece[...]
    blocks = rows // BLOCK
    me = lax.axis_index("var") % GROUP
    for distance in range(GROUP):
        at = pl.ds(pl.multiple_of((me ^ distance) * rows, rows), rows)
        own[at] = pieces[distance][...]
    first, second = exchange_start(GROUP * blocks)
    for start, out in ((first, first_out), (second, second_out)):
        out[...] = own[pl.ds(pl.multiple_of(start * BLOCK, BLOCK), SPAN * BLOCK)]


def attend_kernel(last, blocks_here, head_dim, kb_ref, *refs):
    if last:
        kv_win, k_turn, shifts, qo_ref, before, dq_before, *refs = refs
        own_out, first_out, second_out, *refs = refs
        dq_outs, refs = refs[:GROUP], refs[GROUP:]
        acc, queries, grads, crossed, prob, slope, dq_all = refs
    else:
        kv_refs, refs = refs[:3], refs[3:]
        qo_pieces, refs = refs[: GROUP - 1], refs[GROUP - 1 :]
        first_out, second_out, kv_win, k_turn, shifts, qo_ref, kept_out, dq_all, *refs = refs
        acc, queries, grads, crossed, prob, slope = refs
    group_blocks = GROUP * blocks_here
    window = group_blocks + 2 * SPAN
    rows = blocks_here * BLOCK
    slot_count = kb_ref.shape[1]
    scale = head_dim ** (-0.5)
    base = (lax.axis_index("var") // GROUP) * group_blocks
    odd = below_first()
    low = slice(0, LANES)
    high = slice(LANES, 2 * LANES)

    acc[...] = jnp.zeros_like(acc)
    crossed[...] = jnp.zeros_like(crossed)
    if last:
        dq_all[...] = dq_before[...]
    else:
        top = window - SPAN
        for ref, start, count in zip(
            kv_refs, (SPAN, (1 - odd) * top, odd * top), (group_blocks, SPAN, SPAN)
        ):
            kv_win[pl.ds(start, count)] = ref[: count * BLOCK].reshape(count, BLOCK, 2 * LANES)
        own_queries = kv_refs[0].at[pl.ds(group_blocks * BLOCK, rows + LSE_ROWS)]
        stage_pieces(qo_ref, (own_queries, *qo_pieces))
        key_patch = lax.broadcasted_iota(jnp.int32, (8, LANES), 0)
        query_patch = lax.broadcasted_iota(jnp.int32, (8, LANES), 1) & 7
        usable = key_patch <= query_patch
        for member in range(GROUP):
            parts = qo_ref[member, rows:].astype(F32)
            for local in range(blocks_here):
                lse = (
                    parts[local : local + 1] + parts[blocks_here + local : blocks_here + local + 1]
                ) + parts[2 * blocks_here + local : 2 * blocks_here + local + 1]
                at = member * blocks_here + local
                shifts[at, 0, :, low] = jnp.where(usable, -lse[:, low], -1e30)
                shifts[at, 0, :, high] = jnp.broadcast_to(-lse[:, high], (8, LANES))
                shifts[at, 1, :, low] = jnp.where(usable, -lse[:, high], -1e30)

        @pl.loop(0, window, unroll=4)
        def _(block):
            k_turn[block] = kv_win[block, :, low].T

    unorder = reorder_matrix(True)
    lane = lax.broadcasted_iota(jnp.int32, (HALF, LANES), 1)
    head_a = lane < HALF

    def picks(query_block):
        return [kb_ref[base + query_block, s] - base + SPAN for s in range(slot_count)]

    def lay_out(member, local, buf):
        at = pl.multiple_of(local * BLOCK, BLOCK)
        for part in range(2):
            rows_at = pl.ds(at + part * HALF, HALF)
            for cols, target in ((low, queries), (high, grads)):
                tile = qo_ref[member, rows_at, cols]
                zero = jnp.zeros_like(tile)
                both = jnp.concatenate(
                    [jnp.where(head_a, tile, zero), jnp.where(head_a, zero, tile)], axis=0
                )
                target[buf, part * BLOCK : (part + 1) * BLOCK] = both
                if part == 1:
                    side = 0 if target is queries else 1
                    crossed[
                        buf, side * BLOCK : (side + 1) * BLOCK, side * LANES : (side + 1) * LANES
                    ] = both

    def gather(index, rows_of, cols):
        return jnp.concatenate([kv_win[i, rows_of, cols] for i in index], axis=0)

    early = slice(0, HALF)
    late = slice(HALF, BLOCK)
    both_cols = slice(0, 2 * LANES)
    early_rows = slot_count * HALF
    part_slots = slot_count // PARTS
    part_rows = part_slots * HALF

    def forward_part(index, query_block, buf, part):
        some = index[part * part_slots : (part + 1) * part_slots]
        at = slice(part * part_rows, (part + 1) * part_rows)
        after = slice(early_rows + part * part_rows, early_rows + (part + 1) * part_rows)
        s = dot_nt(gather(some, early, low), queries[buf])
        g = dot_nt(gather(some, early, high), grads[buf])
        x = dot_nt(gather(some, late, both_cols), crossed[buf])
        shift = shifts[query_block, 0][None]
        p = jnp.exp(s.reshape(part_rows // 8, 8, 2 * LANES) + shift).reshape(part_rows, 2 * LANES)
        prob[buf, at] = p
        slope[buf, at] = g
        delta = jnp.sum((p * g).reshape(part_rows // 8, 8, 2 * LANES), axis=0)
        late_shift = shifts[query_block, 1, :, low][None]
        q = jnp.exp(x[:, low].reshape(part_rows // 8, 8, LANES) + late_shift).reshape(
            part_rows, LANES
        )
        prob[buf, after, low] = q
        slope[buf, after, low] = x[:, high]
        more = jnp.sum((q * x[:, high]).reshape(part_rows // 8, 8, LANES), axis=0)
        return delta[:, low], delta[:, high] + more

    def backward_part(index, buf, delta, part):
        at = slice(part * part_rows, (part + 1) * part_rows)
        after = slice(early_rows + part * part_rows, early_rows + (part + 1) * part_rows)
        p = prob[buf, at]
        ds = (p * (slope[buf, at] - delta)).astype(BF16)
        q = prob[buf, after, low]
        ds_late = (q * (slope[buf, after, low] - delta[:, high])).astype(BF16)
        dk = dot(ds, queries[buf])
        dv = dot(p.astype(BF16), grads[buf])
        r = dot(jnp.concatenate([ds_late, q.astype(BF16)], axis=1), crossed[buf])
        nothing = jnp.zeros((HALF, LANES), BF16)
        pieces = []
        for s in range(part_slots):
            at = slice(s * HALF, (s + 1) * HALF)
            where = index[part * part_slots + s]
            acc[where, early, low] = acc[where, early, low] + dk[at]
            acc[where, early, high] = acc[where, early, high] + dv[at]
            acc[where, late] = acc[where, late] + r[at]
            pieces.append(ds[at])
            pieces.append(jnp.concatenate([nothing, ds_late[at]], axis=1))
        keys_turned = jnp.concatenate(
            [k_turn[i] for i in index[part * part_slots : (part + 1) * part_slots]], axis=1
        )
        return dot(keys_turned, jnp.concatenate(pieces, axis=0))

    def write_dq(query_block, dq):
        dq = dq * scale
        halves = []
        for cols in (low, high):
            turned = dq[:, cols].T
            halves.append(jnp.where(head_a, turned[:HALF], turned[HALF:]))
        moved = dot(unorder, jnp.concatenate(halves, axis=0).astype(BF16)).astype(BF16)
        local = pl.multiple_of((query_block % blocks_here) * BLOCK, BLOCK)
        dq_all[query_block // blocks_here, pl.ds(local, BLOCK)] = moved

    def run(ahead, ahead_buf, behind, behind_buf, delta):
        sums, dq = None, None
        if ahead is not None:
            lay_out(ahead // blocks_here, ahead % blocks_here, ahead_buf)
            ahead_index = picks(ahead)
        if behind is not None:
            behind_index = picks(behind)
        for part in range(PARTS):
            if ahead is not None:
                more = forward_part(ahead_index, ahead, ahead_buf, part)
                sums = more if sums is None else (sums[0] + more[0], sums[1] + more[1])
            if behind is not None:
                more = backward_part(behind_index, behind_buf, delta, part)
                dq = more if dq is None else dq + more
        if behind is not None:
            write_dq(behind, dq)
        if ahead is None:
            return None
        return jnp.concatenate([jnp.sum(x, axis=0, keepdims=True) for x in sums], axis=1)

    def block_of(j):
        if last:
            return j + OUTER
        return j + jnp.where(j < OUTER, 0, group_blocks - 2 * OUTER)

    count = group_blocks - 2 * OUTER if last else 2 * OUTER
    delta = run(block_of(0), 0, None, None, None)

    def step(j, delta):
        delta = run(block_of(2 * j + 1), 1, block_of(2 * j), 0, delta)
        return run(block_of(2 * j + 2), 0, block_of(2 * j + 1), 1, delta)

    delta = lax.fori_loop(0, (count - 1) // 2, step, delta)
    if count % 2 == 0:
        delta = run(block_of(count - 1), 1, block_of(count - 2), 0, delta)
    run(None, None, block_of(count - 1), (count - 1) % 2, delta)

    groups = BLOCK // 16

    def in_token_order(part):
        blocks = part.shape[0]
        part = part.reshape(blocks, 2, groups, 8, 2 * LANES)
        return jnp.swapaxes(part, 1, 2).reshape(blocks, BLOCK, 2 * LANES)

    if last:
        acc[OUTER : window - OUTER] = acc[OUTER : window - OUTER] + before[...]
        top = window - SPAN
        for out, side in ((first_out, 1 - odd), (second_out, odd)):
            start = OUTER + side * (top - OUTER)
            out[...] = in_token_order(acc[pl.ds(start, OUTER)]).astype(BF16)
        own_out[...] = in_token_order(acc[SPAN : SPAN + group_blocks])
        send_pieces(dq_outs, dq_all)
    else:
        for out, side in ((first_out, 1 - odd), (second_out, odd)):
            start = side * (window - OUTER)
            out[...] = in_token_order(acc[pl.ds(start, OUTER)]).astype(BF16)
        kept_out[...] = acc[OUTER : window - OUTER]


def owner_start(piece, half):
    heads = lax.axis_size("head")
    return pl.multiple_of(((lax.axis_index("head") + 1 + piece) % heads) * half, half)


def add_arrived(total, starts, refs):
    level = lax.axis_index("var") // GROUP
    levels = lax.axis_size("var") // GROUP
    odd = below_first()
    for side, ref in zip((1 - odd, odd), refs):
        other = level - 1 + 2 * side
        start = jnp.where(side == 1, starts[1], starts[0])

        @pl.when((other >= 0) & (other < levels))
        def _(start=start, ref=ref):
            at = pl.ds(start, OUTER)
            total[at] = total[at] + ref[...].astype(F32)


def combine_outer_kernel(carried, own_ref, first_ref, second_ref, *refs):
    total = refs[carried]
    total[...] = own_ref[...]
    add_arrived(total, (SPAN - OUTER, own_ref.shape[0] - SPAN), (first_ref, second_ref))


def combine_kernel(own_ref, first_ref, second_ref, *rest):
    aways, homes, (total, moved) = rest[:GROUP], rest[GROUP : 2 * GROUP], rest[2 * GROUP :]
    total[...] = own_ref[...]
    add_arrived(total, (0, own_ref.shape[0] - OUTER), (first_ref, second_ref))
    moved[...] = total[...].astype(BF16).reshape(moved.shape)
    half = homes[0].shape[0]
    away = aways[0].shape[0] // half
    me = lax.axis_index("var") % GROUP
    for distance in range(GROUP):
        member = me ^ distance
        for piece in range(away):
            aways[distance][piece * half : (piece + 1) * half] = moved[
                member, pl.ds(owner_start(piece, half), half)
            ]
        homes[distance][...] = moved[member, pl.ds(owner_start(away, half), half)]


def gather_rows(grads, dq, start, dkv, dkv_at):
    half = grads.shape[1]
    width = grads.shape[2] // GROUP
    for member in range(GROUP):
        at = slice(member * width, (member + 1) * width)
        both = dkv[member, dkv_at * half : (dkv_at + 1) * half]
        grads[0, :, at] = dq[member, pl.ds(start, half)][:, :width]
        grads[1, :, at] = both[:, :width]
        grads[2, :, at] = both[:, LANES : LANES + width]


def product(grads, w_ref):
    total = dot_nt(grads[0], w_ref[0])
    for s in (1, 2):
        total = total + dot_nt(grads[s], w_ref[s])
    return total


def away_kernel(*refs):
    dqs, dkvs, (w_ref, *rest) = refs[:4], refs[4:8], refs[8:]
    outs, (grads, dq, dkv) = rest[:-3], rest[-3:]
    half = grads.shape[1]
    stage_pieces(dq, dqs)
    stage_pieces(dkv, dkvs)
    for piece, out in enumerate(outs):
        gather_rows(grads, dq, owner_start(piece, half), dkv, piece)
        out[...] = product(grads, w_ref).astype(BF16)


def home_kernel(*refs):
    dqs, aways, homes, rest = refs[:4], refs[4:8], refs[8:12], refs[12:]
    w_ref, dq_out, dk_out, dv_out, keep_out, grads, dq, away_dkv, home_dkv = rest
    half = grads.shape[1]
    away = away_dkv.shape[1] // half
    stage_pieces(dq, dqs)
    stage_pieces(away_dkv, aways)
    stage_pieces(home_dkv, homes)
    for piece in range(away + 1):
        start = owner_start(piece, half)
        if piece < away:
            gather_rows(grads, dq, start, away_dkv, piece)
        else:
            gather_rows(grads, dq, start, home_dkv, 0)
        at = pl.ds(start, half)
        dq_out[at] = grads[0]
        dk_out[at] = grads[1]
        dv_out[at] = grads[2]
    keep_out[...] = product(grads, w_ref)


def body(queries, keys, values, out_grad, log_sum_exp, key_blocks, w_qkv):
    rows, features = queries.shape
    head_count = log_sum_exp.shape[0]
    head_dim = features // head_count
    slots = head_count // GROUP
    blocks_here = rows // BLOCK
    group_blocks = GROUP * blocks_here
    window = group_blocks + 2 * SPAN
    slot_count = key_blocks.shape[1]
    devices = lax.axis_size("var")
    heads = lax.axis_size("head")
    half = rows // heads
    model = w_qkv.shape[1]
    wide = 2 * LANES
    hbm = pl.BlockSpec(memory_space=pltpu.HBM)

    def trade(x, distance):
        return lax.ppermute(x, "var", [(n, n ^ distance) for n in range(devices)])

    def trade_level(x, turn):
        pairs = []
        for n in range(devices):
            other = n - GROUP if (n // GROUP + n + turn) % 2 else n + GROUP
            for h in range(heads):
                if 0 <= other < devices:
                    target = other * heads + h
                else:
                    target = n * heads + (h ^ 1) % heads
                pairs.append((n * heads + h, target))
        return lax.ppermute(x, ("var", "head"), pairs)

    def trade_first(x):
        return trade_level(x, 0)

    def trade_second(x):
        return trade_level(x, 1)

    def swap(pieces):
        got = [pieces[0]] + [None] * (GROUP - 1)
        for distance in (2, 3, 1):
            got[distance] = trade(pieces[distance], distance)
        return got

    def staged(count, width=LANES):
        return pltpu.VMEM((GROUP, count, width), BF16)

    block = (BLOCK, LANES)
    anywhere = pl.BlockSpec(memory_space=pl.ANY)

    def cost(flops, moved):
        return pl.CostEstimate(flops=flops, bytes_accessed=moved, transcendentals=0)

    size = rows * features * 2

    kvs = pl.pallas_call(
        pack_kv_kernel,
        out_shape=(shaped((rows, wide)),) * GROUP,
        in_specs=[hbm] * 2,
        out_specs=(vmem(),) * GROUP,
        scratch_shapes=[pltpu.VMEM((rows, features), BF16)] * 2
        + [staged(rows, wide), pltpu.SemaphoreType.DMA((2, LOADS))],
        compiler_params=params(PACK_MIB),
        cost_estimate=cost(4 * rows * features * BLOCK, 5 * size),
    )(keys, values)
    kvs = swap(kvs)
    *qos, kvs[0] = pl.pallas_call(
        functools.partial(pack_qo_kernel, slots, head_dim),
        out_shape=(shaped((rows + LSE_ROWS, wide)),) * GROUP + (shaped((rows, wide)),),
        in_specs=[vmem()] * 4 + [anywhere],
        out_specs=(vmem(),) * (GROUP + 1),
        scratch_shapes=[staged(rows + LSE_ROWS, wide)],
        compiler_params=params(8),
        cost_estimate=cost(4 * rows * features * BLOCK, 10 * size),
    )(queries, out_grad, log_sum_exp, kvs[0], kvs[1])
    carried = tuple(qos[1:])
    own, first, second, *carried = pl.pallas_call(
        functools.partial(line_kernel, len(carried)),
        out_shape=(shaped((GROUP * rows + rows + LSE_ROWS, wide)),)
        + (shaped((SPAN * BLOCK, wide)),) * 2
        + tuple(shaped(x.shape) for x in carried),
        in_specs=[vmem()] * (GROUP + 1) + [anywhere] * len(carried),
        out_specs=(vmem(),) * 3 + (anywhere,) * len(carried),
        input_output_aliases={GROUP + 1 + i: 3 + i for i in range(len(carried))},
        compiler_params=params(8),
        cost_estimate=cost(0, 5 * size),
    )(*kvs, qos[0], *carried)
    first = trade_first(first)
    second = trade_second(second)
    qos = swap([None, *carried])[1:]

    pairs = group_blocks * slot_count * BLOCK * BLOCK * slots
    tall = (BLOCK, wide)
    acc_scratch = pltpu.VMEM((window,) + tall, F32)
    work = [
        pltpu.VMEM((2, wide, LANES), BF16),
        pltpu.VMEM((2, wide, LANES), BF16),
        pltpu.VMEM((2, wide, wide), BF16),
        pltpu.VMEM((2, slot_count * BLOCK, wide), F32),
        pltpu.VMEM((2, slot_count * BLOCK, wide), F32),
    ]
    smem = pl.BlockSpec(memory_space=pltpu.SMEM)
    outer = (shaped((OUTER,) + tall),) * 2

    def attend_cost(part):
        return pl.CostEstimate(
            flops=int(40 * pairs * head_dim * part),
            bytes_accessed=2_000_000,
            transcendentals=int(pairs * part),
        )

    state = (
        shaped((window,) + tall),
        shaped((window, LANES, BLOCK)),
        shaped((group_blocks, 2, 8, wide), F32),
        shaped((GROUP, rows + LSE_ROWS, wide)),
        shaped((window - 2 * OUTER,) + tall, F32),
        shaped((GROUP, rows, LANES)),
    )
    first, second, *state = pl.pallas_call(
        functools.partial(attend_kernel, False, blocks_here, head_dim),
        out_shape=outer + state,
        in_specs=[smem] + [vmem()] * (2 + GROUP),
        out_specs=(vmem(),) * 8,
        scratch_shapes=[acc_scratch] + work,
        compiler_params=params(16),
        cost_estimate=attend_cost(0.67),
    )(key_blocks, own, first, second, *qos)
    outer_back = (trade_first(first), trade_second(second))
    own_sum, first, second, *dqs = pl.pallas_call(
        functools.partial(attend_kernel, True, blocks_here, head_dim),
        out_shape=(shaped((group_blocks,) + tall, F32),)
        + outer
        + (shaped((rows, LANES)),) * GROUP,
        in_specs=[smem] + [vmem()] * 6,
        out_specs=(vmem(),) * (3 + GROUP),
        scratch_shapes=[acc_scratch] + work + [staged(rows)],
        compiler_params=params(16),
        cost_estimate=attend_cost(0.33),
    )(key_blocks, *state)
    inner_back = (trade_first(first), trade_second(second))
    carried = tuple(dqs[1:])
    *carried, own_sum = pl.pallas_call(
        functools.partial(combine_outer_kernel, 2 * len(carried)),
        out_shape=tuple(shaped(x.shape) for x in carried) + (shaped((group_blocks,) + tall, F32),),
        in_specs=[vmem()] * 3 + [anywhere] * len(carried),
        out_specs=(anywhere,) * len(carried) + (vmem(),),
        input_output_aliases={3 + i: i for i in range(len(carried))},
        compiler_params=params(8),
        cost_estimate=cost(0, 4 * size),
    )(own_sum, *outer_back, *carried)
    dqs = swap([dqs[0], *carried])
    split = pl.pallas_call(
        combine_kernel,
        out_shape=(shaped((rows - half, wide)),) * GROUP + (shaped((half, wide)),) * GROUP,
        in_specs=[vmem()] * 3,
        out_specs=(vmem(),) * (2 * GROUP),
        scratch_shapes=[pltpu.VMEM((group_blocks,) + tall, F32), staged(rows, wide)],
        compiler_params=params(8),
        cost_estimate=cost(0, 8 * size),
    )(own_sum, *inner_back)
    aways = swap(split[:GROUP])
    homes = swap(split[GROUP:])

    grads = pltpu.VMEM((3, half, features), BF16)
    sends = pl.pallas_call(
        away_kernel,
        out_shape=(shaped((half, model)),) * (heads - 1),
        in_specs=[vmem()] * (2 * GROUP + 1),
        out_specs=(vmem(),) * (heads - 1),
        scratch_shapes=[grads, staged(rows), staged(rows - half, wide)],
        compiler_params=params(8),
        cost_estimate=cost(6 * (rows - half) * features * model, 4_000_000),
    )(*dqs, *aways, w_qkv)
    dq_out, dk_out, dv_out, total = pl.pallas_call(
        home_kernel,
        out_shape=(shaped((rows, features)),) * 3 + (shaped((half, model), F32),),
        in_specs=[vmem()] * (3 * GROUP + 1),
        out_specs=(vmem(),) * 4,
        scratch_shapes=[grads, staged(rows), staged(rows - half, wide), staged(half, wide)],
        compiler_params=params(8),
        cost_estimate=cost(6 * half * features * model, 6_000_000),
    )(*dqs, *aways, *homes, w_qkv)
    for piece, send in enumerate(sends):
        got = lax.ppermute(send, "head", [(n, (n + piece + 1) % heads) for n in range(heads)])
        total = total + got.astype(F32)
    return dq_out, dk_out, dv_out, total.astype(BF16)


def solution(mesh):
    in_specs = (
        P("var", "head"),
        P("var", "head"),
        P("var", "head"),
        P("var", "head"),
        P("head", "var"),
        P(),
        P(None, None, "head"),
    )
    out_specs = (P("var", "head"), P("var", "head"), P("var", "head"), P(("var", "head"), None))
    return jax.shard_map(body, mesh=mesh, in_specs=in_specs, out_specs=out_specs, check_vma=False)
```
